32 devices in a mesh: dom: 8 (over z, core), sub: 4 (over y, x).
Axes of the slice: x: 2, y: 2, z: 4, core: 2. Of those that a mesh axis runs over, the one named last changes fastest.
Arguments:
- modal_state: float32 [56, 9, 4096], P(None, None, ('dom', 'sub')), may hold values from -6 to 6
- stiffness: float32 [3, 56, 56], replicated, may hold values from -0.75 to 0.75
- jacobians: float32 [3, 9, 9, 4096], P(None, None, None, ('dom', 'sub')), may hold values from -1.25 to 1.25
- flux_solvers: float32 [2, 4, 9, 9, 4096], P(None, None, None, None, ('dom', 'sub')), may hold values from -0.75 to 0.75
- projector: float32 [4, 21, 56], replicated, may hold values from -0.75 to 0.75
- rotations: float32 [3, 21, 21], replicated, may hold values from -1.25 to 1.25
- yield_stress: float32 [4096], P(('dom', 'sub')), may hold values from 0.5 to 8
- cluster: int32 [4096], P(('dom', 'sub')), may hold values from 0 to 1
- orient: int32 [4, 4096], P(None, ('dom', 'sub')), may hold values from 0 to 2
- neighbour_slot: int32 [4, 4096], P(None, ('dom', 'sub')), may hold values from 0 to 703, as said below
- send_map: int32 [6144], P(('dom', 'sub')), may hold values from 0 to 511, as said below
Outputs:
- updated: float32 [56, 9, 4096], P(None, None, ('dom', 'sub'))
The draws below stay inside these ranges and needn't reach their ends.
Inputs may be any that keep to these rules, and one draw needn't show every extreme that they name: `neighbour_slot`: within one partition every received slot 512 + r is named by exactly one face; the other faces name local faces. `send_map`: the 192 entries of one partition are distinct local face numbers.
All inputs are finite; a program needn't handle non-finite values.
Results may differ from the reference program's by a relative error of at most 0.0003.
Values sent between devices are 32-bit elements; how exact they have to be, the bound alone decides.
No kernel may reach another device: no remote copies, remote signals or barrier semaphores. Data moves between devices by JAX's collectives and lax.ppermute only.
A program may use at most 64 MiB of HBM per device.

```python
import math
import jax
import jax.numpy as jnp
from jax import lax

BASIS = 56
QUANT = 9
MODES = 21
ORDER = 6
ELEM_DEV = 128
SLOTS_DOM = 64
SLOTS_SUB = 32
ELEMS = 4096
N_DOM = 8
N_SUB = 4


def draw_neighbour_slot(key, part):
    parts_count = ELEMS // ELEM_DEV
    faces_count = 4 * ELEM_DEV
    slot_count = 2 * SLOTS_DOM + 2 * SLOTS_SUB
    keys = jax.random.split(jax.random.fold_in(key, 11), parts_count)

    def one_part(part_key):
        order_key, local_key = jax.random.split(part_key)
        order = jax.random.permutation(order_key, faces_count).astype(jnp.int32)
        local = jax.random.randint(local_key, (faces_count,), 0, faces_count, dtype=jnp.int32)
        ranks = jnp.zeros((faces_count,), jnp.int32).at[order].set(jnp.arange(faces_count, dtype=jnp.int32))
        return jnp.where(ranks < slot_count, faces_count + ranks, local).reshape(4, ELEM_DEV)
    blocks = jax.vmap(one_part)(keys)
    return jnp.transpose(blocks, (1, 0, 2)).reshape(4, ELEMS)


def draw_send_map(key, part):
    parts_count = ELEMS // ELEM_DEV
    faces_count = 4 * ELEM_DEV
    slot_count = 2 * SLOTS_DOM + 2 * SLOTS_SUB
    keys = jax.random.split(jax.random.fold_in(key, 23), parts_count)

    def one_part(part_key):
        first_key, second_key = jax.random.split(part_key)
        chosen = jax.random.permutation(first_key, faces_count - 1)[:slot_count - 1].astype(jnp.int32)
        values = jnp.concatenate([chosen, jnp.full((1,), faces_count - 1, jnp.int32)])
        return jax.random.permutation(second_key, values).astype(jnp.int32)
    return jax.vmap(one_part)(keys).reshape(-1)


def place_ends(values, key, low, largest):
    longest = values.shape.index(max(values.shape))
    spots = []
    for shift in (0, 1):
        where = [jax.random.randint(jax.random.fold_in(key, axis), (), 0, length) for axis, length in enumerate(values.shape)]
        where[longest] = (where[longest] + shift) % values.shape[longest]
        spots.append(tuple(where))
    return values.at[spots[0]].set(low).at[spots[1]].set(largest)


def block_scale(key, extent, shards, low, largest):
    level = 1.0
    for dim, blocks in shards:
        steps = jax.random.uniform(jax.random.fold_in(jax.random.fold_in(key, 6), dim), (blocks,), jnp.float32, low / len(shards), largest / len(shards))
        level = level * jnp.repeat(jnp.exp(steps), extent[dim] // blocks).reshape((-1,) + (1,) * (len(extent) - 1 - dim))
    return level


def noise(key, dims, width, most, cuts=(), kind=jnp.bfloat16):
    factor_of = block_scale(key, dims, cuts, -0.22, 0.18) if cuts else 1.0
    values = jax.random.normal(key, dims, jnp.float32) * width * factor_of
    return jnp.minimum(jnp.maximum(values, -most), most).astype(kind)


def setup_inputs(seed: int = 0) -> dict:
    seeds = jax.random.split(jax.random.key(seed), 12)
    modal_state = noise(seeds[0], (BASIS, QUANT, ELEMS), 1.0, 6.0, ((2, 32),), jnp.float32)
    stiffness = noise(seeds[1], (3, BASIS, BASIS), BASIS ** -0.5, 0.75, (), jnp.float32)
    jacobians = noise(seeds[2], (3, QUANT, QUANT, ELEMS), (3 * QUANT) ** -0.5, 1.25, ((3, 32),), jnp.float32)
    flux_solvers = noise(seeds[3], (2, 4, QUANT, QUANT, ELEMS), (8 * QUANT) ** -0.5, 0.75, ((4, 32),), jnp.float32)
    projector = noise(seeds[4], (4, MODES, BASIS), BASIS ** -0.5, 0.75, (), jnp.float32)
    rotations = noise(seeds[5], (3, MODES, MODES), MODES ** -0.5, 1.25, (), jnp.float32)
    yield_stress = jnp.clip(jnp.exp(math.log(8.0) - 2.7725887 * jax.random.uniform(seeds[6], (ELEMS,), jnp.float32) ** block_scale(seeds[6], (ELEMS,), ((0, 32),), -0.2, 0.2)), 0.5, 8.0)
    cluster = place_ends(jax.random.randint(seeds[7], (ELEMS,), 0, 2), jax.random.fold_in(seeds[7], 1), 0, 1).astype(jnp.int32)
    orient = place_ends(jax.random.randint(seeds[8], (4, ELEMS), 0, 3), jax.random.fold_in(seeds[8], 1), 0, 2).astype(jnp.int32)
    neighbour_slot = draw_neighbour_slot(jax.random.fold_in(seeds[11], 71), 0)
    send_map = draw_send_map(jax.random.fold_in(seeds[11], 71), 0)
    return {"modal_state": modal_state, "stiffness": stiffness, "jacobians": jacobians, "flux_solvers": flux_solvers, "projector": projector, "rotations": rotations, "yield_stress": yield_stress, "cluster": cluster, "orient": orient, "neighbour_slot": neighbour_slot, "send_map": send_map}


exact_dots = lax.Precision.HIGHEST

def derive(current, stiffness, jacobians):
    basis_size = current.shape[0]
    starred = jnp.einsum('bqe,dqpe->dbpe', current, jacobians, precision=exact_dots)
    stacked = jnp.transpose(stiffness, (1, 0, 2)).reshape(basis_size, 3 * basis_size)
    return jnp.dot(stacked, starred.reshape(3 * basis_size, -1), precision=exact_dots).reshape(current.shape)

def predict(state, stiffness, jacobians, both):
    half_one = jnp.zeros_like(state)
    half_two = jnp.zeros_like(state)
    current = state
    for power in range(ORDER):
        factor = float(math.factorial(power + 1))
        half_one = half_one + 1.0 / factor * current
        if both:
            half_two = half_two + (2.0 ** (power + 1) - 1.0) / factor * current
        if power + 1 < ORDER:
            current = derive(current, stiffness, jacobians)
    return (half_one, half_two)

def project(field, projector):
    basis_size, quantities, elem_count = field.shape
    mode_count = projector.shape[1]
    flat = jnp.dot(projector.reshape(4 * mode_count, basis_size), field.reshape(basis_size, quantities * elem_count), precision=exact_dots)
    return flat.reshape(4, mode_count, quantities, elem_count)

def face_table(projected):
    return jnp.transpose(projected, (1, 2, 0, 3)).reshape(projected.shape[1], projected.shape[2], -1)

def neighbours(table, received, neighbour_slot, orient, rotations):
    mode_count, quantities = (table.shape[0], table.shape[1])
    elem_count = neighbour_slot.shape[1]
    extended = jnp.concatenate([table, received], axis=2)
    picked = jnp.take(extended, neighbour_slot.reshape(-1), axis=2)
    turned = jnp.dot(rotations.reshape(3 * mode_count, mode_count), picked.reshape(mode_count, -1), precision=exact_dots)
    turned = turned.reshape(3, mode_count, quantities, 4, elem_count)
    select_mask = (orient[None] == jnp.arange(3, dtype=jnp.int32)[:, None, None]).astype(jnp.float32)
    chosen = lax.optimization_barrier(jnp.sum(turned * select_mask[:, None, None], axis=0))
    return jnp.transpose(chosen, (2, 0, 1, 3))

def update(base, integral, own, near, stiffness, jacobians, flux_solvers, projector):
    basis_size = base.shape[0]
    mode_count = projector.shape[1]
    starred = jnp.einsum('bqe,dqpe->dbpe', integral, jacobians, precision=exact_dots)
    stacked = jnp.transpose(stiffness, (2, 0, 1)).reshape(basis_size, 3 * basis_size)
    volume = jnp.dot(stacked, starred.reshape(3 * basis_size, -1), precision=exact_dots).reshape(base.shape)
    solved = jnp.einsum('fmqe,fqpe->fmpe', own, flux_solvers[0], precision=exact_dots)
    solved = solved + jnp.einsum('fmqe,fqpe->fmpe', near, flux_solvers[1], precision=exact_dots)
    lifted = jnp.dot(projector.reshape(4 * mode_count, basis_size).T, solved.reshape(4 * mode_count, -1), precision=exact_dots)
    return base + volume - lifted.reshape(base.shape)

def yield_back(state, yield_stress):
    normal = state[:, 0:3]
    mean_part = lax.optimization_barrier(jnp.sum(normal, axis=1, keepdims=True)) / 3.0
    spread = normal - mean_part
    shear = state[:, 3:6]
    second_inv = 0.5 * lax.optimization_barrier(jnp.sum(spread[0] ** 2, axis=0)) + lax.optimization_barrier(jnp.sum(shear[0] ** 2, axis=0))
    scaling = yield_stress / jnp.maximum(jnp.sqrt(second_inv), yield_stress)
    return jnp.concatenate([mean_part + scaling * spread, scaling * shear, state[:, 6:]], axis=1)

def split_parts(array, parts):
    shaped = array.reshape(array.shape[:-1] + (parts, array.shape[-1] // parts))
    return jnp.moveaxis(shaped, -2, 0)

def grouped(function, *arrays):
    parts = arrays[0].shape[0]
    group = math.gcd(16, parts)
    shaped = tuple((item.reshape((parts // group, group) + item.shape[1:]) for item in arrays))
    result = lax.map(lambda pieces: jax.vmap(function)(*pieces), shaped)
    return jax.tree.map(lambda item: item.reshape((parts,) + item.shape[2:]), result)

def from_lower(grid, axis):
    if axis == 0:
        return jnp.concatenate([jnp.zeros_like(grid[:1]), grid[:-1]], axis=0)
    return jnp.concatenate([jnp.zeros_like(grid[:, :1]), grid[:, :-1]], axis=1)

def from_upper(grid, axis):
    if axis == 0:
        return jnp.concatenate([grid[1:], jnp.zeros_like(grid[:1])], axis=0)
    return jnp.concatenate([grid[:, 1:], jnp.zeros_like(grid[:, :1])], axis=1)

def deliver(sent):
    grid = sent.reshape((N_DOM, N_SUB) + sent.shape[1:])
    dom_end = 2 * SLOTS_DOM
    sub_mid = dom_end + SLOTS_SUB
    pieces = [from_lower(grid[..., SLOTS_DOM:dom_end], 0), from_upper(grid[..., :SLOTS_DOM], 0), from_lower(grid[..., sub_mid:], 1), from_upper(grid[..., dom_end:sub_mid], 1)]
    return jnp.concatenate(pieces, axis=-1).reshape(sent.shape)

def reference(modal_state, stiffness, jacobians, flux_solvers, projector, rotations, yield_stress, cluster, orient, neighbour_slot, send_map):
    parts = N_DOM * N_SUB
    states = split_parts(modal_state, parts)
    jac_parts = split_parts(jacobians, parts)
    flux_parts = split_parts(flux_solvers, parts)
    yield_parts = split_parts(yield_stress, parts)
    cluster_parts = split_parts(cluster, parts)
    orient_parts = split_parts(orient, parts)
    slot_parts = split_parts(neighbour_slot, parts)
    send_parts = split_parts(send_map, parts)

    def section_one(state, jac, sends):
        half_one, half_two = predict(state, stiffness, jac, True)
        table = face_table(project(half_one, projector))
        return (half_one, half_two, jnp.take(table, sends, axis=2))
    half_one, half_two, sent_one = grouped(section_one, states, jac_parts, send_parts)
    got_one = deliver(sent_one)

    def middle_state(state, first_half, jac, flux, orients, slots, arrived, clusters):
        own = project(first_half, projector)
        near = neighbours(face_table(own), arrived, slots, orients, rotations)
        stepped = update(state, first_half, own, near, stiffness, jac, flux, projector)
        return (jnp.where(clusters[None, None] == 0, stepped, state), near)

    def section_two(state, first_half, second_half, jac, flux, orients, slots, arrived, clusters, sends):
        middle, unused = middle_state(state, first_half, jac, flux, orients, slots, arrived, clusters)
        fine_one, unused_two = predict(middle, stiffness, jac, False)
        late = jnp.where(clusters[None, None] == 0, fine_one, second_half)
        return (fine_one, jnp.take(face_table(project(late, projector)), sends, axis=2))
    fine_one, sent_two = grouped(section_two, states, half_one, half_two, jac_parts, flux_parts, orient_parts, slot_parts, got_one, cluster_parts, send_parts)
    got_two = deliver(sent_two)

    def section_three(state, first_half, second_half, fine_half, jac, flux, yields, clusters, orients, slots, arrived_one, arrived_two):
        middle, near_one = middle_state(state, first_half, jac, flux, orients, slots, arrived_one, clusters)
        fine = clusters[None, None] == 0
        late = jnp.where(fine, fine_half, second_half)
        near_two = neighbours(face_table(project(late, projector)), arrived_two, slots, orients, rotations)
        integral = jnp.where(fine, fine_half, first_half + second_half)
        base = jnp.where(fine, middle, state)
        near = jnp.where(clusters[None, None, None] == 0, near_two, near_one + near_two)
        stepped = update(base, integral, project(integral, projector), near, stiffness, jac, flux, projector)
        return yield_back(stepped, yields)
    result = grouped(section_three, states, half_one, half_two, fine_one, jac_parts, flux_parts, yield_parts, cluster_parts, orient_parts, slot_parts, got_one, got_two)
    return jnp.moveaxis(result, 0, 2).reshape(modal_state.shape)
```

```python
import jax
import jax.numpy as jnp
from jax import lax
from jax.experimental import pallas as pl
from jax.experimental.pallas import tpu as pltpu
from jax.sharding import PartitionSpec as P

ORDER = 6
SLOTS_DOM = 64
SLOTS_SUB = 32
ROWS = 24
GROUP = 3

F32 = jnp.float32
BF16 = jnp.bfloat16
EXACT = lax.Precision.HIGHEST

DOM_GROUPS = ((0, 5), (5, 4))
SUB_GROUPS = ((0, 3), (3, 2), (5, 2), (7, 2))


def iota(shape, dim):
    return lax.broadcasted_iota(jnp.int32, shape, dim)


def dot(a, b):
    return jnp.dot(a, b, preferred_element_type=F32)


def exact_dot(a, b):
    return jnp.dot(a, b, precision=EXACT, preferred_element_type=F32)


def halves(value):
    high = value.astype(BF16)
    return high, (value - high.astype(F32)).astype(BF16)


def one_hot(index_row, first, count, modulus=None):
    number = iota((count, index_row.shape[1]), 0)
    if modulus is not None:
        number = lax.rem(number, modulus)
    return jnp.where(number + first == index_row, 1.0, 0.0).astype(BF16)


def fold_depth(basis):
    return -(-3 * basis // 64) * 64


def fold_rows(value):
    basis, lanes = value.shape
    high = value.astype(BF16).astype(F32)
    rest = jnp.zeros((fold_depth(basis) - 3 * basis, lanes), F32)
    return jnp.concatenate([high, high, value - high, rest], axis=0).astype(BF16)


def fold_columns(matrix):
    basis = matrix.shape[1]
    depth = fold_depth(basis)
    high, low = halves(matrix)
    row, column = iota((basis, depth), 0), iota((basis, depth), 1)
    outer = jnp.where((column == row) | (column == row + 2 * basis), 1.0, 0.0).astype(BF16)
    inner = jnp.where(column == row + basis, 1.0, 0.0).astype(BF16)
    return (dot(high, outer) + dot(low, inner)).astype(BF16)


def mix_jacobians(stiffened, jac, basis, quants, lanes, write):
    for start in range(0, quants, GROUP):
        totals = [None] * GROUP
        for q in range(quants):
            for d in range(3):
                block = stiffened[d * basis:(d + 1) * basis, q * lanes:(q + 1) * lanes]
                for i in range(GROUP):
                    term = block * jac[q, start + i, d:d + 1, :]
                    totals[i] = term if totals[i] is None else totals[i] + term
        for i in range(GROUP):
            write(start + i, totals[i])


def mix_faces(table, flux, side, quants, lanes, write):
    for f in range(4):
        blocks = [
            table[q * ROWS:(q + 1) * ROWS, f * lanes:(f + 1) * lanes] for q in range(quants)
        ]
        for p in range(quants):
            total = blocks[0] * flux[side, 0, p, f:f + 1, :]
            for q in range(1, quants):
                total = total + blocks[q] * flux[side, q, p, f:f + 1, :]
            write(f, p, total)


def fill_projector(projector, padded):
    modes, faces, basis = projector.shape
    padded[...] = jnp.zeros(padded.shape, F32)
    for f in range(faces):
        for m in range(modes):
            padded[f * ROWS + m:f * ROWS + m + 1, 0:basis] = projector[m, f:f + 1, :]


def predict(stiff_fold, jac, folded, stiffened, first, second, basis, quants, lanes):
    def step(_, scales):
        factor, power, number = scales
        stiffened[...] = dot(stiff_fold, folded[...])

        def write(p, total):
            folded[:, p * lanes:(p + 1) * lanes] = fold_rows(total)
            first[p] = first[p] + factor * total
            if second is not None:
                second[p] = second[p] + (factor * (power - 1.0)) * total

        mix_jacobians(stiffened, jac, basis, quants, lanes, write)
        return factor / (number + 1.0), power * 2.0, number + 1.0

    lax.fori_loop(0, ORDER - 1, step, (jnp.float32(0.5), jnp.float32(4.0), jnp.float32(2.0)))


def project_table(padded, folded, table, basis, quants, lanes):
    flat = dot(fold_columns(padded[:, 0:basis]), folded[...])
    for q in range(quants):
        for f in range(4):
            table[q * ROWS:(q + 1) * ROWS, f * lanes:(f + 1) * lanes] = flat[
                f * ROWS:(f + 1) * ROWS, q * lanes:(q + 1) * lanes
            ]


def pick_sends(table, send_row, outs, lanes):
    faces = table.shape[1]
    low = jnp.broadcast_to(send_row[:, 0:lanes], (8, lanes))
    lane = iota((8, lanes), 1)
    turned = pltpu.roll(low, SLOTS_DOM, 1)
    high = jnp.broadcast_to(send_row[:, lanes:2 * lanes], (8, lanes))
    pieces = [
        jnp.where(lane < SLOTS_DOM, low, turned),
        jnp.where(lane < SLOTS_DOM, turned, low),
    ]
    spread = jnp.where(lane < 2 * SLOTS_SUB, high, pltpu.roll(high, 2 * SLOTS_SUB, 1))
    moved = pltpu.roll(spread, SLOTS_SUB, 1)
    even = lax.rem(lane, 2 * SLOTS_SUB) < SLOTS_SUB
    pieces += [jnp.where(even, spread, moved), jnp.where(even, moved, spread)]
    index = jnp.concatenate([piece[0:1] for piece in pieces], axis=1)
    chosen = one_hot(index, 0, faces)
    upper, lower = halves(table[...])
    sent = dot(upper, chosen) + dot(lower, chosen)
    for k, (out, groups) in enumerate(
        zip(outs, (DOM_GROUPS, DOM_GROUPS, SUB_GROUPS, SUB_GROUPS))
    ):
        width = lanes // len(groups)
        values = sent[:, k * lanes:(k + 1) * lanes]
        start, count = groups[0]
        packed = values[0:count * ROWS]
        least = min(count for _, count in groups) * ROWS
        place = iota((least, lanes), 1)
        head = packed[0:least]
        for g, (start, _) in enumerate(groups):
            if g:
                head = jnp.where(
                    place >= g * width, values[start * ROWS:start * ROWS + least], head
                )
        out[0:least] = head
        out[least:count * ROWS] = packed[least:]


def spread_received(arrived, groups, lanes):
    width = lanes // len(groups)
    parts = []
    for g, (_, count) in enumerate(groups):
        place = iota((count * ROWS, lanes), 1)
        mine = (place >= g * width) & (place < (g + 1) * width)
        parts.append(jnp.where(mine, arrived[0:count * ROWS], 0.0))
    return jnp.concatenate(parts, axis=0)


def pick_local(table, slot, faces):
    chosen = jnp.concatenate([one_hot(slot[f:f + 1], 0, faces) for f in range(4)], axis=1)
    upper, lower = halves(table)
    return dot(upper, chosen) + dot(lower, chosen)


def pick_received(arrived, slot, faces, lanes):
    spread = jnp.concatenate(
        [
            spread_received(item[...], groups, lanes)
            for item, groups in zip(arrived, (DOM_GROUPS, DOM_GROUPS, SUB_GROUPS, SUB_GROUPS))
        ],
        axis=1,
    )
    starts = (faces, faces + SLOTS_DOM, faces + 2 * SLOTS_DOM, faces + 2 * SLOTS_DOM + SLOTS_SUB)
    widths = (SLOTS_DOM, SLOTS_DOM, SLOTS_SUB, SLOTS_SUB)
    chosen = jnp.concatenate(
        [
            jnp.concatenate(
                [one_hot(slot[f:f + 1], first, lanes, width) for f in range(4)], axis=1
            )
            for first, width in zip(starts, widths)
        ],
        axis=0,
    )
    upper, lower = halves(spread)
    return dot(upper, chosen) + dot(lower, chosen)


def lift(weights, high, low):
    upper, lower = halves(weights)
    return dot(upper, high) + dot(lower, high) + dot(upper, low)


def local_update(
    base, integral, table, jac, stiffness, flux, lifting, folded, stiffened, solved, write,
    basis, quants, lanes,
):
    for q in range(quants):
        folded[:, q * lanes:(q + 1) * lanes] = fold_rows(integral(q))
    turned = jnp.concatenate([stiffness[d].T for d in range(3)], axis=0)
    stiffened[...] = dot(fold_columns(turned), folded[...])

    def keep(f, p, total):
        solved[f * ROWS:(f + 1) * ROWS, p * lanes:(p + 1) * lanes] = total

    mix_faces(table, flux, 0, quants, lanes, keep)
    high, low = halves(solved[...])
    own = lift(lifting, high, low)
    mix_jacobians(
        stiffened, jac, basis, quants, lanes,
        lambda p, total: write(p, base(p) + total - own[:, p * lanes:(p + 1) * lanes]),
    )


def near_lift(picked, flux, orient, lifting, solved, quants, lanes):
    block = 4 * ROWS

    def keep(f, p, total):
        upper = total.astype(BF16).astype(F32)
        lower = total - upper
        for o in range(3):
            mine = orient[f:f + 1] == o
            row = o * block + f * ROWS
            solved[row:row + ROWS, p * lanes:(p + 1) * lanes] = jnp.where(mine, upper, 0.0)
            row += 3 * block
            solved[row:row + ROWS, p * lanes:(p + 1) * lanes] = jnp.where(mine, lower, 0.0)

    mix_faces(picked, flux, 1, quants, lanes, keep)
    depth = 3 * block
    return lift(lifting, solved[0:depth].astype(BF16), solved[depth:2 * depth].astype(BF16))


def near_lifting(own_lifting, rotations):
    count, modes, _ = rotations.shape
    block = 4 * ROWS
    row, column = iota((modes, count * block), 0), iota((modes, count * block), 1)
    turned = jnp.zeros((modes, count * block), F32)
    for o in range(count):
        spot = (lax.rem(column, ROWS) == row) & (lax.div(column, block) == o)
        turned = turned + exact_dot(rotations[o], jnp.where(spot, 1.0, 0.0))
    row, column = iota((block, modes), 0), iota((block, modes), 1)
    tall = exact_dot(jnp.where(lax.rem(row, ROWS) == column, 1.0, 0.0), turned)
    row, column = iota(tall.shape, 0), iota(tall.shape, 1)
    same = lax.div(row, ROWS) == lax.div(lax.rem(column, block), ROWS)
    return exact_dot(own_lifting, jnp.where(same, tall, 0.0))


def first_kernel(
    state, jac, stiffness, projector, send_row,
    first, second, table, to_lower, to_upper, to_left, to_right,
    folded, stiffened, padded,
):
    quants, basis, lanes = state.shape
    for q in range(quants):
        value = state[q]
        first[q] = value
        second[q] = value
        folded[:, q * lanes:(q + 1) * lanes] = fold_rows(value)
    fill_projector(projector, padded)
    stacked = jnp.concatenate([stiffness[d] for d in range(3)], axis=0)
    predict(
        fold_columns(stacked), jac, folded, stiffened, first, second, basis, quants, lanes
    )
    for q in range(quants):
        folded[:, q * lanes:(q + 1) * lanes] = fold_rows(first[q])
    project_table(padded, folded, table, basis, quants, lanes)
    pick_sends(table, send_row, (to_lower, to_upper, to_left, to_right), lanes)


def second_kernel(
    state, first, table, jac, stiffness, projector, rotations, flux, slot,
    part, picked, lifting,
    folded, stiffened, solved, padded,
):
    quants, basis, lanes = state.shape
    fill_projector(projector, padded)
    own_lifting = padded[...].T[0:basis]
    lifting[...] = near_lifting(own_lifting, rotations)
    picked[...] = pick_local(table[...], slot, 4 * lanes)

    def write(p, value):
        part[p] = value

    local_update(
        lambda p: state[p], lambda q: first[q], table, jac, stiffness, flux, own_lifting,
        folded, stiffened, solved, write, basis, quants, lanes,
    )


def third_kernel(
    state, first, second, part, picked_local, from_lower, from_upper, from_left, from_right,
    jac, stiffness, projector, flux, slot, orient, cluster, lifting, send_row,
    middle, integral, picked, table, to_lower, to_upper, to_left, to_right,
    folded, stiffened, solved, padded,
):
    quants, basis, lanes = state.shape
    fill_projector(projector, padded)
    picked[...] = picked_local[...] + pick_received(
        (from_lower, from_upper, from_left, from_right), slot, 4 * lanes, lanes
    )
    near = near_lift(picked, flux, orient, lifting[...], solved, quants, lanes)
    fine = cluster[...] == 0
    for q in range(quants):
        value = jnp.where(fine, part[q] - near[:, q * lanes:(q + 1) * lanes], state[q])
        middle[q] = value
        integral[q] = value
        folded[:, q * lanes:(q + 1) * lanes] = fold_rows(value)
    stacked = jnp.concatenate([stiffness[d] for d in range(3)], axis=0)
    predict(
        fold_columns(stacked), jac, folded, stiffened, integral, None, basis, quants, lanes
    )
    for q in range(quants):
        fine_first = integral[q]
        late = jnp.where(fine, fine_first, second[q])
        folded[:, q * lanes:(q + 1) * lanes] = fold_rows(late)
        integral[q] = jnp.where(fine, fine_first, first[q] + second[q])
    project_table(padded, folded, table, basis, quants, lanes)
    pick_sends(table, send_row, (to_lower, to_upper, to_left, to_right), lanes)


def fourth_kernel(
    middle, integral, table_one, table_two, picked_one, jac, stiffness, projector, flux, slot,
    cluster,
    part, picked,
    folded, stiffened, solved, padded, total_table,
):
    quants, basis, lanes = middle.shape
    fill_projector(projector, padded)
    own_lifting = padded[...].T[0:basis]
    coarse = jnp.concatenate([cluster[...] != 0] * 4, axis=1)
    total_table[...] = table_two[...] + jnp.where(coarse, table_one[...], 0.0)
    picked[...] = pick_local(table_two[...], slot, 4 * lanes) + jnp.where(
        coarse, picked_one[...], 0.0
    )

    def write(p, value):
        part[p] = value

    local_update(
        lambda p: middle[p], lambda q: integral[q], total_table, jac, stiffness, flux,
        own_lifting, folded, stiffened, solved, write, basis, quants, lanes,
    )


def fifth_kernel(
    part, picked_local, from_lower, from_upper, from_left, from_right, flux, slot, orient,
    lifting, yield_stress,
    updated,
    solved, picked,
):
    quants, basis, lanes = part.shape
    picked[...] = picked_local[...] + pick_received(
        (from_lower, from_upper, from_left, from_right), slot, 4 * lanes, lanes
    )
    near = near_lift(picked, flux, orient, lifting[...], solved, quants, lanes)
    stepped = [part[q] - near[:, q * lanes:(q + 1) * lanes] for q in range(quants)]
    mean_part = (stepped[0] + stepped[1] + stepped[2]) / 3.0
    spread = [stepped[q] - mean_part for q in range(3)]
    normal = [item[0:1] for item in spread]
    shear = [stepped[q][0:1] for q in range(3, 6)]
    second_inv = 0.5 * (normal[0] ** 2 + normal[1] ** 2 + normal[2] ** 2) + (
        shear[0] ** 2 + shear[1] ** 2 + shear[2] ** 2
    )
    limit = yield_stress[...]
    scaling = limit / jnp.maximum(jnp.sqrt(second_inv), limit)
    for q in range(3):
        updated[q] = mean_part + scaling * spread[q]
    for q in range(3, 6):
        updated[q] = scaling * stepped[q]
    for q in range(6, quants):
        updated[q] = stepped[q]


def run(body, outs, scratch, *operands):
    vmem = pl.BlockSpec(memory_space=pltpu.VMEM)
    return pl.pallas_call(
        body,
        out_shape=[jax.ShapeDtypeStruct(shape, F32) for shape in outs],
        in_specs=[vmem] * len(operands),
        out_specs=[vmem] * len(outs),
        scratch_shapes=[pltpu.VMEM(shape, kind) for shape, kind in scratch],
        compiler_params=pltpu.CompilerParams(vmem_limit_bytes=32 * 1024 * 1024),
        name=body.__name__,
    )(*operands)


def exchange(sends):
    to_lower, to_upper, to_left, to_right = sends

    def shift(value, axis, step):
        size = lax.axis_size(axis)
        pairs = [(i, i + step) for i in range(size) if 0 <= i + step < size]
        return lax.ppermute(value, axis, pairs)

    return (
        shift(to_upper, "dom", 1),
        shift(to_lower, "dom", -1),
        shift(to_right, "sub", 1),
        shift(to_left, "sub", -1),
    )


def on_device(
    modal_state,
    stiffness,
    jacobians,
    flux_solvers,
    projector,
    rotations,
    yield_stress,
    cluster,
    orient,
    neighbour_slot,
    send_map,
):
    basis, quants, lanes = modal_state.shape
    state = jnp.transpose(modal_state, (1, 0, 2))
    jac = jnp.transpose(jacobians, (1, 2, 0, 3))
    flux = jnp.transpose(flux_solvers, (0, 2, 3, 1, 4))
    proj = jnp.transpose(projector, (1, 0, 2))
    cluster = cluster.reshape(1, lanes)
    limit = yield_stress.reshape(1, lanes)
    send_row = jnp.pad(send_map, (0, 2 * lanes - send_map.shape[0])).reshape(1, 2 * lanes)

    field = (quants, basis, lanes)
    table = (quants * ROWS, 4 * lanes)
    messages = [(groups[0][1] * ROWS, lanes) for groups in (DOM_GROUPS, DOM_GROUPS, SUB_GROUPS, SUB_GROUPS)]
    depth = fold_depth(basis)
    flat = quants * lanes
    folded = ((depth, flat), BF16)
    stiffened = ((3 * basis, flat), F32)
    padded = ((4 * ROWS, 128), F32)
    own_solved = ((4 * ROWS, flat), F32)
    near_solved = ((2 * 3 * 4 * ROWS, flat), F32)

    first, second, table_one, *sends = run(
        first_kernel, [field, field, table] + messages, [folded, stiffened, padded],
        state, jac, stiffness, proj, send_row,
    )
    arrived = exchange(sends)
    part_one, local_one, lifting = run(
        second_kernel, [field, table, (basis, 3 * 4 * ROWS)],
        [folded, stiffened, own_solved, padded],
        state, first, table_one, jac, stiffness, proj, rotations, flux, neighbour_slot,
    )
    middle, integral, picked_one, table_two, *sends = run(
        third_kernel, [field, field, table, table] + messages,
        [folded, stiffened, near_solved, padded],
        state, first, second, part_one, local_one, *arrived,
        jac, stiffness, proj, flux, neighbour_slot, orient, cluster, lifting, send_row,
    )
    arrived = exchange(sends)
    part_two, local_two = run(
        fourth_kernel, [field, table],
        [folded, stiffened, own_solved, padded, (table, F32)],
        middle, integral, table_one, table_two, picked_one, jac, stiffness, proj, flux,
        neighbour_slot, cluster,
    )
    updated, = run(
        fifth_kernel, [field], [near_solved, (table, F32)],
        part_two, local_two, *arrived, flux, neighbour_slot, orient, lifting, limit,
    )
    return jnp.transpose(updated, (1, 0, 2))


def solution(mesh):
    placed = (
        P(None, None, ("dom", "sub")),
        P(),
        P(None, None, None, ("dom", "sub")),
        P(None, None, None, None, ("dom", "sub")),
        P(),
        P(),
        P(("dom", "sub")),
        P(("dom", "sub")),
        P(None, ("dom", "sub")),
        P(None, ("dom", "sub")),
        P(("dom", "sub")),
    )
    return jax.shard_map(
        on_device,
        mesh=mesh,
        in_specs=placed,
        out_specs=P(None, None, ("dom", "sub")),
        check_vma=False,
    )
```

```python
import jax
import jax.numpy as jnp
from jax import lax
from jax.experimental import pallas as pl
from jax.experimental.pallas import tpu as pltpu
from jax.sharding import PartitionSpec as P

ORDER = 6
SLOTS_DOM = 64
SLOTS_SUB = 32
ROWS = 24
GROUP = 3

F32 = jnp.float32
BF16 = jnp.bfloat16
EXACT = lax.Precision.HIGHEST

DOM_GROUPS = ((0, 5), (5, 4))
SUB_GROUPS = ((0, 3), (3, 2), (5, 2), (7, 2))

GRANT = 32
INPUTS = 11
FIRST_USED = 5


def iota(shape, dim):
    return lax.broadcasted_iota(jnp.int32, shape, dim)


def dot(a, b):
    return jnp.dot(a, b, preferred_element_type=F32)


def exact_dot(a, b):
    return jnp.dot(a, b, precision=EXACT, preferred_element_type=F32)


def halves(value):
    high = value.astype(BF16)
    return high, (value - high.astype(F32)).astype(BF16)


def one_hot(index_row, first, count, modulus=None):
    number = iota((count, index_row.shape[1]), 0)
    if modulus is not None:
        number = lax.rem(number, modulus)
    return jnp.where(number + first == index_row, 1.0, 0.0).astype(BF16)


def fold_depth(basis):
    return -(-3 * basis // 64) * 64


def fold_rows(value):
    basis, lanes = value.shape
    high = value.astype(BF16).astype(F32)
    rest = jnp.zeros((fold_depth(basis) - 3 * basis, lanes), F32)
    return jnp.concatenate([high, high, value - high, rest], axis=0).astype(BF16)


def fold_columns(matrix):
    basis = matrix.shape[1]
    depth = fold_depth(basis)
    high, low = halves(matrix)
    row, column = iota((basis, depth), 0), iota((basis, depth), 1)
    outer = jnp.where((column == row) | (column == row + 2 * basis), 1.0, 0.0).astype(BF16)
    inner = jnp.where(column == row + basis, 1.0, 0.0).astype(BF16)
    return (dot(high, outer) + dot(low, inner)).astype(BF16)


def mix_jacobians(stiffened, jac, basis, quants, lanes, write):
    for start in range(0, quants, GROUP):
        totals = [None] * GROUP
        for q in range(quants):
            for d in range(3):
                block = stiffened[d * basis:(d + 1) * basis, q * lanes:(q + 1) * lanes]
                for i in range(GROUP):
                    term = block * jac[q, start + i, d:d + 1, :]
                    totals[i] = term if totals[i] is None else totals[i] + term
        for i in range(GROUP):
            write(start + i, totals[i])


def mix_faces(table, flux, side, quants, lanes, write):
    for f in range(4):
        blocks = [
            table[q * ROWS:(q + 1) * ROWS, f * lanes:(f + 1) * lanes] for q in range(quants)
        ]
        for p in range(quants):
            total = blocks[0] * flux[side, 0, p, f:f + 1, :]
            for q in range(1, quants):
                total = total + blocks[q] * flux[side, q, p, f:f + 1, :]
            write(f, p, total)


def fill_projector(projector, padded):
    modes, faces, basis = projector.shape
    padded[...] = jnp.zeros(padded.shape, F32)
    for f in range(faces):
        for m in range(modes):
            padded[f * ROWS + m:f * ROWS + m + 1, 0:basis] = projector[m, f:f + 1, :]


def predict(stiff_fold, jac, folded, stiffened, first, second, basis, quants, lanes):
    def step(_, scales):
        factor, power, number = scales
        stiffened[...] = dot(stiff_fold, folded[...])

        def write(p, total):
            folded[:, p * lanes:(p + 1) * lanes] = fold_rows(total)
            first[p] = first[p] + factor * total
            if second is not None:
                second[p] = second[p] + (factor * (power - 1.0)) * total

        mix_jacobians(stiffened, jac, basis, quants, lanes, write)
        return factor / (number + 1.0), power * 2.0, number + 1.0

    lax.fori_loop(0, ORDER - 1, step, (jnp.float32(0.5), jnp.float32(4.0), jnp.float32(2.0)))


def project_table(padded, folded, table, basis, quants, lanes):
    flat = dot(fold_columns(padded[:, 0:basis]), folded[...])
    for q in range(quants):
        for f in range(4):
            table[q * ROWS:(q + 1) * ROWS, f * lanes:(f + 1) * lanes] = flat[
                f * ROWS:(f + 1) * ROWS, q * lanes:(q + 1) * lanes
            ]


def grid_spot():
    i, j = lax.axis_index("dom"), lax.axis_index("sub")
    return (
        lax.rem(i, 2), lax.rem(j, 2),
        i > 0, i < lax.axis_size("dom") - 1, j > 0, j < lax.axis_size("sub") - 1,
    )


def partners(parity_dom, parity_sub, tiling):
    u = parity_dom if tiling == 0 else 1 - parity_dom
    v = parity_sub if tiling == 0 else 1 - parity_sub
    return (1 - u) * 2 + v, u * 2 + (1 - v)


def pick_sends(table, send_row, outs, lanes):
    faces = table.shape[1]
    parity_dom, parity_sub, *_ = grid_spot()
    low = jnp.broadcast_to(send_row[:, 0:lanes], (8, lanes))
    lane = iota((8, lanes), 1)
    turned = pltpu.roll(low, SLOTS_DOM, 1)
    to_lower = jnp.where(lane < SLOTS_DOM, low, turned)
    to_upper = jnp.where(lane < SLOTS_DOM, turned, low)
    high = send_row[:, 2 * SLOTS_DOM:2 * SLOTS_DOM + 2 * SLOTS_SUB]
    spread = jnp.broadcast_to(jnp.concatenate([high, high], axis=1), (8, lanes))
    moved = pltpu.roll(spread, SLOTS_SUB, 1)
    left = lax.rem(lane, 2 * SLOTS_SUB) < SLOTS_SUB
    to_left = jnp.where(left, spread, moved)
    to_right = jnp.where(left, moved, spread)
    even_dom, even_sub = parity_dom == 0, parity_sub == 0
    pieces = [
        jnp.where(even_dom, to_upper, to_lower),
        jnp.where(even_dom, to_lower, to_upper),
        jnp.where(even_sub, to_right, to_left),
        jnp.where(even_sub, to_left, to_right),
    ]
    index = jnp.concatenate([piece[0:1] for piece in pieces], axis=1)
    chosen = one_hot(index, 0, faces)
    upper, lower = halves(table[...])
    sent = dot(upper, chosen) + dot(lower, chosen)
    for k, groups in enumerate((DOM_GROUPS, DOM_GROUPS, SUB_GROUPS, SUB_GROUPS)):
        out = outs[k % 2]
        place = partners(parity_dom, parity_sub, k % 2)[k // 2]
        width = lanes // len(groups)
        values = sent[:, k * lanes:(k + 1) * lanes]
        start, count = groups[0]
        packed = values[0:count * ROWS]
        least = min(count for _, count in groups) * ROWS
        spot = iota((least, lanes), 1)
        head = packed[0:least]
        for g, (start, _) in enumerate(groups):
            if g:
                head = jnp.where(
                    spot >= g * width, values[start * ROWS:start * ROWS + least], head
                )
        out[place, 0:least] = head
        out[place, least:count * ROWS] = packed[least:]


def spread_received(arrived, valid, groups, lanes):
    width = lanes // len(groups)
    parts = []
    for g, (_, count) in enumerate(groups):
        place = iota((count * ROWS, lanes), 1)
        mine = (place >= g * width) & (place < (g + 1) * width) & valid
        parts.append(jnp.where(mine, arrived[0:count * ROWS], 0.0))
    return jnp.concatenate(parts, axis=0)


def pick_local(table, slot, faces):
    chosen = jnp.concatenate([one_hot(slot[f:f + 1], 0, faces) for f in range(4)], axis=1)
    upper, lower = halves(table)
    return dot(upper, chosen) + dot(lower, chosen)


def pick_received(arrived, slot, faces, lanes):
    parity_dom, parity_sub, lower, upper, left, right = grid_spot()
    even_dom, even_sub = parity_dom == 0, parity_sub == 0
    starts = (faces, faces + SLOTS_DOM, faces + 2 * SLOTS_DOM, faces + 2 * SLOTS_DOM + SLOTS_SUB)
    true = parity_dom >= 0
    firsts = (
        jnp.where(even_dom, starts[1], starts[0]), jnp.where(even_dom, starts[0], starts[1]),
        jnp.where(even_sub, starts[3], starts[2]), jnp.where(even_sub, starts[2], starts[3]),
    )
    valid = (
        true, (even_dom & lower) | (~even_dom & upper),
        true, (even_sub & left) | (~even_sub & right),
    )
    widths = (SLOTS_DOM, SLOTS_DOM, SLOTS_SUB, SLOTS_SUB)
    all_groups = (DOM_GROUPS, DOM_GROUPS, SUB_GROUPS, SUB_GROUPS)
    spread = jnp.concatenate(
        [
            spread_received(
                arrived[k % 2][
                    partners(parity_dom, parity_sub, k % 2)[k // 2],
                    0:groups[0][1] * ROWS,
                ],
                valid[k], groups, lanes,
            )
            for k, groups in enumerate(all_groups)
        ],
        axis=1,
    )
    chosen = jnp.concatenate(
        [
            jnp.concatenate(
                [one_hot(slot[f:f + 1], first, lanes, width) for f in range(4)], axis=1
            )
            for first, width in zip(firsts, widths)
        ],
        axis=0,
    )
    upper, lower = halves(spread)
    return dot(upper, chosen) + dot(lower, chosen)


def lift(weights, high, low):
    upper, lower = halves(weights)
    return dot(upper, high) + dot(lower, high) + dot(upper, low)


def local_update(
    base, integral, table, jac, turned_fold, flux, lifting, folded, stiffened, solved, write,
    basis, quants, lanes,
):
    for q in range(quants):
        folded[:, q * lanes:(q + 1) * lanes] = fold_rows(integral(q))
    stiffened[...] = dot(turned_fold, folded[...])

    def keep(f, p, total):
        solved[f * ROWS:(f + 1) * ROWS, p * lanes:(p + 1) * lanes] = total

    mix_faces(table, flux, 0, quants, lanes, keep)
    high, low = halves(solved[...])
    own = lift(lifting, high, low)
    mix_jacobians(
        stiffened, jac, basis, quants, lanes,
        lambda p, total: write(p, base(p) + total - own[:, p * lanes:(p + 1) * lanes]),
    )


def near_lift(picked, flux, orient, lifting, solved, quants, lanes):
    block = 4 * ROWS

    def keep(f, p, total):
        upper = total.astype(BF16).astype(F32)
        lower = total - upper
        for o in range(3):
            mine = orient[f:f + 1] == o
            row = o * block + f * ROWS
            solved[row:row + ROWS, p * lanes:(p + 1) * lanes] = jnp.where(mine, upper, 0.0)
            row += 3 * block
            solved[row:row + ROWS, p * lanes:(p + 1) * lanes] = jnp.where(mine, lower, 0.0)

    mix_faces(picked, flux, 1, quants, lanes, keep)
    depth = 3 * block
    return lift(lifting, solved[0:depth].astype(BF16), solved[depth:2 * depth].astype(BF16))


def near_lifting(own_lifting, rotations):
    count, modes, _ = rotations.shape
    block = 4 * ROWS
    row, column = iota((modes, count * block), 0), iota((modes, count * block), 1)
    turned = jnp.zeros((modes, count * block), F32)
    for o in range(count):
        spot = (lax.rem(column, ROWS) == row) & (lax.div(column, block) == o)
        turned = turned + exact_dot(rotations[o], jnp.where(spot, 1.0, 0.0))
    row, column = iota((block, modes), 0), iota((block, modes), 1)
    tall = exact_dot(jnp.where(lax.rem(row, ROWS) == column, 1.0, 0.0), turned)
    row, column = iota(tall.shape, 0), iota(tall.shape, 1)
    same = lax.div(row, ROWS) == lax.div(lax.rem(column, block), ROWS)
    return exact_dot(own_lifting, jnp.where(same, tall, 0.0))


def first_kernel(*refs):
    inputs, refs = refs[:INPUTS], refs[INPUTS:]
    held, refs = refs[:INPUTS], refs[INPUTS:]
    (first, second, table, padded, stiff_fold, send_even, send_odd,
     folded, stiffened, arrivals) = refs
    copies = [
        pltpu.make_async_copy(source, target, arrivals.at[k])
        for k, (source, target) in enumerate(zip(inputs, held))
    ]
    for copy in copies:
        copy.start()
    state, stiffness, projector, jac, send_row = held[:FIRST_USED]
    for copy in copies[:FIRST_USED]:
        copy.wait()
    quants, basis, lanes = state.shape
    for q in range(quants):
        value = state[q]
        first[q] = value
        second[q] = value
        folded[:, q * lanes:(q + 1) * lanes] = fold_rows(value)
    fill_projector(projector, padded)
    stacked = jnp.concatenate([stiffness[d] for d in range(3)], axis=0)
    fold = fold_columns(stacked)
    stiff_fold[...] = fold.astype(F32)
    predict(fold, jac, folded, stiffened, first, second, basis, quants, lanes)
    for q in range(quants):
        folded[:, q * lanes:(q + 1) * lanes] = fold_rows(first[q])
    project_table(padded, folded, table, basis, quants, lanes)
    pick_sends(table, send_row, (send_even, send_odd), lanes)
    for copy in copies[FIRST_USED:]:
        copy.wait()


def second_kernel(
    state, first, table, jac, stiffness, padded, rotations, flux, slot,
    part, picked, lifting, turned_fold,
    folded, stiffened, solved,
):
    quants, basis, lanes = state.shape
    turned = jnp.concatenate([stiffness[d].T for d in range(3)], axis=0)
    fold = fold_columns(turned)
    turned_fold[...] = fold.astype(F32)
    own_lifting = padded[...].T[0:basis]
    lifting[...] = near_lifting(own_lifting, rotations)
    picked[...] = pick_local(table[...], slot, 4 * lanes)

    def write(p, value):
        part[p] = value

    local_update(
        lambda p: state[p], lambda q: first[q], table, jac, fold, flux, own_lifting,
        folded, stiffened, solved, write, basis, quants, lanes,
    )


def third_kernel(
    state, first, second, part, picked_local, from_even, from_odd,
    jac, stiff_fold, padded, flux, slot, orient, cluster, lifting, send_row,
    middle, integral, picked, table, send_even, send_odd,
    folded, stiffened, solved,
):
    quants, basis, lanes = state.shape
    picked[...] = picked_local[...] + pick_received(
        (from_even, from_odd), slot, 4 * lanes, lanes
    )
    near = near_lift(picked, flux, orient, lifting[...], solved, quants, lanes)
    fine = cluster[...] == 0
    for q in range(quants):
        value = jnp.where(fine, part[q] - near[:, q * lanes:(q + 1) * lanes], state[q])
        middle[q] = value
        integral[q] = value
        folded[:, q * lanes:(q + 1) * lanes] = fold_rows(value)
    predict(
        stiff_fold[...].astype(BF16), jac, folded, stiffened, integral, None,
        basis, quants, lanes,
    )
    for q in range(quants):
        fine_first = integral[q]
        late = jnp.where(fine, fine_first, second[q])
        folded[:, q * lanes:(q + 1) * lanes] = fold_rows(late)
        integral[q] = jnp.where(fine, fine_first, first[q] + second[q])
    project_table(padded, folded, table, basis, quants, lanes)
    pick_sends(table, send_row, (send_even, send_odd), lanes)


def fourth_kernel(
    middle, integral, table_one, table_two, picked_one, jac, turned_fold, padded, flux, slot,
    cluster,
    part, picked,
    folded, stiffened, solved, total_table,
):
    quants, basis, lanes = middle.shape
    own_lifting = padded[...].T[0:basis]
    coarse = jnp.concatenate([cluster[...] != 0] * 4, axis=1)
    total_table[...] = table_two[...] + jnp.where(coarse, table_one[...], 0.0)
    picked[...] = pick_local(table_two[...], slot, 4 * lanes) + jnp.where(
        coarse, picked_one[...], 0.0
    )

    def write(p, value):
        part[p] = value

    local_update(
        lambda p: middle[p], lambda q: integral[q], total_table, jac, turned_fold[...].astype(BF16), flux,
        own_lifting, folded, stiffened, solved, write, basis, quants, lanes,
    )


def fifth_kernel(
    part, picked_local, from_even, from_odd, flux, slot, orient, lifting,
    yield_stress,
    updated,
    solved, picked,
):
    quants, basis, lanes = part.shape
    picked[...] = picked_local[...] + pick_received(
        (from_even, from_odd), slot, 4 * lanes, lanes
    )
    near = near_lift(picked, flux, orient, lifting[...], solved, quants, lanes)
    stepped = [part[q] - near[:, q * lanes:(q + 1) * lanes] for q in range(quants)]
    mean_part = (stepped[0] + stepped[1] + stepped[2]) / 3.0
    spread = [stepped[q] - mean_part for q in range(3)]
    normal = [item[0:1] for item in spread]
    shear = [stepped[q][0:1] for q in range(3, 6)]
    second_inv = 0.5 * (normal[0] ** 2 + normal[1] ** 2 + normal[2] ** 2) + (
        shear[0] ** 2 + shear[1] ** 2 + shear[2] ** 2
    )
    limit = yield_stress[...]
    scaling = limit / jnp.maximum(jnp.sqrt(second_inv), limit)
    for q in range(3):
        updated[q] = mean_part + scaling * spread[q]
    for q in range(3, 6):
        updated[q] = scaling * stepped[q]
    for q in range(6, quants):
        updated[q] = stepped[q]


def run(body, outs, scratch, *operands, space=pltpu.VMEM, grant=32):
    vmem = pl.BlockSpec(memory_space=pltpu.VMEM)
    return pl.pallas_call(
        body,
        out_shape=[
            out if isinstance(out, jax.ShapeDtypeStruct) else jax.ShapeDtypeStruct(out, F32)
            for out in outs
        ],
        in_specs=[pl.BlockSpec(memory_space=space)] * len(operands),
        out_specs=[vmem] * len(outs),
        scratch_shapes=scratch,
        compiler_params=pltpu.CompilerParams(vmem_limit_bytes=grant * 1024 * 1024),
        name=body.__name__,
    )(*operands)


def blocks(shift):
    rows, columns = lax.axis_size("dom"), lax.axis_size("sub")
    groups = []
    for i in range(shift, rows + shift, 2):
        for j in range(shift, columns + shift, 2):
            groups.append(
                [(i + u) % rows * columns + (j + v) % columns for u in (0, 1) for v in (0, 1)]
            )
    return groups


def exchange(sends):
    return [
        lax.all_to_all(value, ("dom", "sub"), 0, 0, axis_index_groups=blocks(shift))
        for shift, value in enumerate(sends)
    ]


def on_device(
    modal_state,
    stiffness,
    jacobians,
    flux_solvers,
    projector,
    rotations,
    yield_stress,
    cluster,
    orient,
    neighbour_slot,
    send_map,
):
    basis, quants, lanes = modal_state.shape
    inputs = [
        jnp.transpose(modal_state, (1, 0, 2)),
        stiffness,
        jnp.transpose(projector, (1, 0, 2)),
        jnp.transpose(jacobians, (1, 2, 0, 3)),
        send_map.reshape(1, -1),
        jnp.transpose(flux_solvers, (0, 2, 3, 1, 4)),
        rotations,
        neighbour_slot,
        orient,
        cluster.reshape(1, lanes),
        yield_stress.reshape(1, lanes),
    ]
    inputs = [pltpu.with_memory_space_constraint(item, pltpu.HBM) for item in inputs]
    held = [jax.ShapeDtypeStruct(item.shape, item.dtype) for item in inputs]

    field = (quants, basis, lanes)
    table = (quants * ROWS, 4 * lanes)
    message = (4, DOM_GROUPS[0][1] * ROWS, lanes)
    depth = fold_depth(basis)
    flat = quants * lanes
    fold = (3 * basis, depth)
    folded = pltpu.VMEM((depth, flat), BF16)
    stiffened = pltpu.VMEM((3 * basis, flat), F32)
    own_solved = pltpu.VMEM((4 * ROWS, flat), F32)
    near_solved = pltpu.VMEM((2 * 3 * 4 * ROWS, flat), F32)

    outs = run(
        first_kernel,
        held + [field, field, table, (4 * ROWS, 128), fold, message, message],
        [folded, stiffened, pltpu.SemaphoreType.DMA((INPUTS,))],
        *inputs, space=pl.ANY, grant=GRANT,
    )
    state, stiff, _, jac, send_row, flux, turns, slot, orient, cluster, limit = outs[:INPUTS]
    first, second, table_one, padded, stiff_fold, *sends = outs[INPUTS:]
    arrived = exchange(sends)
    part_one, local_one, lifting, turned_fold = run(
        second_kernel, [field, table, (basis, 3 * 4 * ROWS), fold],
        [folded, stiffened, own_solved],
        state, first, table_one, jac, stiff, padded, turns, flux, slot,
    )
    middle, integral, picked_one, table_two, *sends = run(
        third_kernel, [field, field, table, table, message, message],
        [folded, stiffened, near_solved],
        state, first, second, part_one, local_one, *arrived,
        jac, stiff_fold, padded, flux, slot, orient, cluster, lifting, send_row,
    )
    arrived = exchange(sends)
    part_two, local_two = run(
        fourth_kernel, [field, table],
        [folded, stiffened, own_solved, pltpu.VMEM(table, F32)],
        middle, integral, table_one, table_two, picked_one, jac, turned_fold, padded, flux,
        slot, cluster,
    )
    updated, = run(
        fifth_kernel, [field], [near_solved, pltpu.VMEM(table, F32)],
        part_two, local_two, *arrived, flux, slot, orient, lifting, limit,
    )
    return jnp.transpose(updated, (1, 0, 2))


def solution(mesh):
    placed = (
        P(None, None, ("dom", "sub")),
        P(),
        P(None, None, None, ("dom", "sub")),
        P(None, None, None, None, ("dom", "sub")),
        P(),
        P(),
        P(("dom", "sub")),
        P(("dom", "sub")),
        P(None, ("dom", "sub")),
        P(None, ("dom", "sub")),
        P(("dom", "sub")),
    )
    return jax.shard_map(
        on_device,
        mesh=mesh,
        in_specs=placed,
        out_specs=P(None, None, ("dom", "sub")),
        check_vma=False,
    )
```

```python
import jax
import jax.numpy as jnp
from jax import lax
from jax.experimental import pallas as pl
from jax.experimental.pallas import tpu as pltpu
from jax.sharding import PartitionSpec as P

ORDER = 6
SLOTS_DOM = 64
SLOTS_SUB = 32
ROWS = 24
GROUP = 3

F32 = jnp.float32
BF16 = jnp.bfloat16
EXACT = lax.Precision.HIGHEST

DOM_GROUPS = ((0, 5), (5, 4))
SUB_GROUPS = ((0, 3), (3, 2), (5, 2), (7, 2))

GRANT = 32
INPUTS = 11
FIRST_USED = 5


def iota(shape, dim):
    return lax.broadcasted_iota(jnp.int32, shape, dim)


def dot(a, b):
    return jnp.dot(a, b, preferred_element_type=F32)


def exact_dot(a, b):
    return jnp.dot(a, b, precision=EXACT, preferred_element_type=F32)


def halves(value):
    high = value.astype(BF16)
    return high, (value - high.astype(F32)).astype(BF16)


def one_hot(index_row, first, count, modulus=None):
    number = iota((count, index_row.shape[1]), 0)
    if modulus is not None:
        number = lax.rem(number, modulus)
    return jnp.where(number + first == index_row, 1.0, 0.0).astype(BF16)


def fold_depth(basis):
    return -(-3 * basis // 64) * 64


def fold_rows(value):
    basis, lanes = value.shape
    high = value.astype(BF16).astype(F32)
    rest = jnp.zeros((fold_depth(basis) - 3 * basis, lanes), F32)
    return jnp.concatenate([high, high, value - high, rest], axis=0).astype(BF16)


def fold_columns(matrix):
    basis = matrix.shape[1]
    depth = fold_depth(basis)
    high, low = halves(matrix)
    row, column = iota((basis, depth), 0), iota((basis, depth), 1)
    outer = jnp.where((column == row) | (column == row + 2 * basis), 1.0, 0.0).astype(BF16)
    inner = jnp.where(column == row + basis, 1.0, 0.0).astype(BF16)
    return (dot(high, outer) + dot(low, inner)).astype(BF16)


def mix_jacobians(stiffened, jac, basis, quants, lanes, write):
    for start in range(0, quants, GROUP):
        totals = [None] * GROUP
        for q in range(quants):
            for d in range(3):
                block = stiffened[d * basis:(d + 1) * basis, q * lanes:(q + 1) * lanes]
                for i in range(GROUP):
                    term = block * jac[q, start + i, d:d + 1, :]
                    totals[i] = term if totals[i] is None else totals[i] + term
        for i in range(GROUP):
            write(start + i, totals[i])


def mix_faces(table, flux, side, quants, lanes, write):
    for f in range(4):
        blocks = [
            table[q * ROWS:(q + 1) * ROWS, f * lanes:(f + 1) * lanes] for q in range(quants)
        ]
        for p in range(quants):
            total = blocks[0] * flux[side, 0, p, f:f + 1, :]
            for q in range(1, quants):
                total = total + blocks[q] * flux[side, q, p, f:f + 1, :]
            write(f, p, total)


def fill_projector(projector, padded):
    modes, faces, basis = projector.shape
    padded[...] = jnp.zeros(padded.shape, F32)
    for f in range(faces):
        for m in range(modes):
            padded[f * ROWS + m:f * ROWS + m + 1, 0:basis] = projector[m, f:f + 1, :]


def predict(stiff_fold, jac, folded, stiffened, first, second, basis, quants, lanes):
    def step(_, scales):
        factor, power, number = scales
        stiffened[...] = dot(stiff_fold, folded[...])

        def write(p, total):
            folded[:, p * lanes:(p + 1) * lanes] = fold_rows(total)
            first[p] = first[p] + factor * total
            if second is not None:
                second[p] = second[p] + (factor * (power - 1.0)) * total

        mix_jacobians(stiffened, jac, basis, quants, lanes, write)
        return factor / (number + 1.0), power * 2.0, number + 1.0

    lax.fori_loop(0, ORDER - 1, step, (jnp.float32(0.5), jnp.float32(4.0), jnp.float32(2.0)))


def project_table(padded, folded, table, basis, quants, lanes):
    flat = dot(fold_columns(padded[:, 0:basis]), folded[...])
    for q in range(quants):
        for f in range(4):
            table[q * ROWS:(q + 1) * ROWS, f * lanes:(f + 1) * lanes] = flat[
                f * ROWS:(f + 1) * ROWS, q * lanes:(q + 1) * lanes
            ]


def grid_spot():
    i, j = lax.axis_index("dom"), lax.axis_index("sub")
    return (
        lax.rem(i, 2), lax.rem(j, 2),
        i > 0, i < lax.axis_size("dom") - 1, j > 0, j < lax.axis_size("sub") - 1,
    )


def partners(parity_dom, parity_sub, tiling):
    u = parity_dom if tiling == 0 else 1 - parity_dom
    v = parity_sub if tiling == 0 else 1 - parity_sub
    return (1 - u) * 2 + v, u * 2 + (1 - v)


def pick_sends(table, send_row, outs, lanes):
    faces = table.shape[1]
    parity_dom, parity_sub, *_ = grid_spot()
    low = jnp.broadcast_to(send_row[:, 0:lanes], (8, lanes))
    lane = iota((8, lanes), 1)
    turned = pltpu.roll(low, SLOTS_DOM, 1)
    to_lower = jnp.where(lane < SLOTS_DOM, low, turned)
    to_upper = jnp.where(lane < SLOTS_DOM, turned, low)
    high = send_row[:, 2 * SLOTS_DOM:2 * SLOTS_DOM + 2 * SLOTS_SUB]
    spread = jnp.broadcast_to(jnp.concatenate([high, high], axis=1), (8, lanes))
    moved = pltpu.roll(spread, SLOTS_SUB, 1)
    left = lax.rem(lane, 2 * SLOTS_SUB) < SLOTS_SUB
    to_left = jnp.where(left, spread, moved)
    to_right = jnp.where(left, moved, spread)
    even_dom, even_sub = parity_dom == 0, parity_sub == 0
    pieces = [
        jnp.where(even_dom, to_upper, to_lower),
        jnp.where(even_dom, to_lower, to_upper),
        jnp.where(even_sub, to_right, to_left),
        jnp.where(even_sub, to_left, to_right),
    ]
    index = jnp.concatenate([piece[0:1] for piece in pieces], axis=1)
    chosen = one_hot(index, 0, faces)
    upper, lower = halves(table[...])
    sent = dot(upper, chosen) + dot(lower, chosen)
    for k, groups in enumerate((DOM_GROUPS, DOM_GROUPS, SUB_GROUPS, SUB_GROUPS)):
        out = outs[k % 2]
        width = lanes // len(groups)
        values = sent[:, k * lanes:(k + 1) * lanes]
        start, count = groups[0]
        packed = values[0:count * ROWS]
        least = min(count for _, count in groups) * ROWS
        spot = iota((least, lanes), 1)
        head = packed[0:least]
        for g, (start, _) in enumerate(groups):
            if g:
                head = jnp.where(
                    spot >= g * width, values[start * ROWS:start * ROWS + least], head
                )
        row = 0 if k < 2 else DOM_GROUPS[0][1] * ROWS
        out[row:row + least] = head
        out[row + least:row + count * ROWS] = packed[least:]


def spread_received(arrived, valid, groups, lanes):
    width = lanes // len(groups)
    parts = []
    for g, (_, count) in enumerate(groups):
        place = iota((count * ROWS, lanes), 1)
        mine = (place >= g * width) & (place < (g + 1) * width) & valid
        parts.append(jnp.where(mine, arrived[0:count * ROWS], 0.0))
    return jnp.concatenate(parts, axis=0)


def pick_local(table, slot, faces):
    chosen = jnp.concatenate([one_hot(slot[f:f + 1], 0, faces) for f in range(4)], axis=1)
    upper, lower = halves(table)
    return dot(upper, chosen) + dot(lower, chosen)


def pick_received(arrived, slot, faces, lanes):
    parity_dom, parity_sub, lower, upper, left, right = grid_spot()
    even_dom, even_sub = parity_dom == 0, parity_sub == 0
    starts = (faces, faces + SLOTS_DOM, faces + 2 * SLOTS_DOM, faces + 2 * SLOTS_DOM + SLOTS_SUB)
    true = parity_dom >= 0
    firsts = (
        jnp.where(even_dom, starts[1], starts[0]), jnp.where(even_dom, starts[0], starts[1]),
        jnp.where(even_sub, starts[3], starts[2]), jnp.where(even_sub, starts[2], starts[3]),
    )
    valid = (
        true, (even_dom & lower) | (~even_dom & upper),
        true, (even_sub & left) | (~even_sub & right),
    )
    widths = (SLOTS_DOM, SLOTS_DOM, SLOTS_SUB, SLOTS_SUB)
    all_groups = (DOM_GROUPS, DOM_GROUPS, SUB_GROUPS, SUB_GROUPS)
    spread = jnp.concatenate(
        [
            spread_received(
                arrived[k % 2][
                    partners(parity_dom, parity_sub, k % 2)[k // 2],
                    pl.ds(
                        0 if k < 2 else DOM_GROUPS[0][1] * ROWS, groups[0][1] * ROWS
                    ),
                ],
                valid[k], groups, lanes,
            )
            for k, groups in enumerate(all_groups)
        ],
        axis=1,
    )
    chosen = jnp.concatenate(
        [
            jnp.concatenate(
                [one_hot(slot[f:f + 1], first, lanes, width) for f in range(4)], axis=1
            )
            for first, width in zip(firsts, widths)
        ],
        axis=0,
    )
    upper, lower = halves(spread)
    return dot(upper, chosen) + dot(lower, chosen)


def lift(weights, high, low):
    upper, lower = halves(weights)
    return dot(upper, high) + dot(lower, high) + dot(upper, low)


def local_update(
    base, integral, table, jac, turned_fold, flux, lifting, folded, stiffened, solved, write,
    basis, quants, lanes,
):
    for q in range(quants):
        folded[:, q * lanes:(q + 1) * lanes] = fold_rows(integral(q))
    stiffened[...] = dot(turned_fold, folded[...])

    def keep(f, p, total):
        solved[f * ROWS:(f + 1) * ROWS, p * lanes:(p + 1) * lanes] = total

    mix_faces(table, flux, 0, quants, lanes, keep)
    high, low = halves(solved[...])
    own = lift(lifting, high, low)
    mix_jacobians(
        stiffened, jac, basis, quants, lanes,
        lambda p, total: write(p, base(p) + total - own[:, p * lanes:(p + 1) * lanes]),
    )


def near_lift(picked, flux, orient, lifting, solved, quants, lanes):
    block = 4 * ROWS

    def keep(f, p, total):
        upper = total.astype(BF16).astype(F32)
        lower = total - upper
        for o in range(3):
            mine = orient[f:f + 1] == o
            row = o * block + f * ROWS
            solved[row:row + ROWS, p * lanes:(p + 1) * lanes] = jnp.where(mine, upper, 0.0)
            row += 3 * block
            solved[row:row + ROWS, p * lanes:(p + 1) * lanes] = jnp.where(mine, lower, 0.0)

    mix_faces(picked, flux, 1, quants, lanes, keep)
    depth = 3 * block
    return lift(lifting, solved[0:depth].astype(BF16), solved[depth:2 * depth].astype(BF16))


def near_lifting(own_lifting, rotations):
    count, modes, _ = rotations.shape
    block = 4 * ROWS
    row, column = iota((modes, count * block), 0), iota((modes, count * block), 1)
    turned = jnp.zeros((modes, count * block), F32)
    for o in range(count):
        spot = (lax.rem(column, ROWS) == row) & (lax.div(column, block) == o)
        turned = turned + exact_dot(rotations[o], jnp.where(spot, 1.0, 0.0))
    row, column = iota((block, modes), 0), iota((block, modes), 1)
    tall = exact_dot(jnp.where(lax.rem(row, ROWS) == column, 1.0, 0.0), turned)
    row, column = iota(tall.shape, 0), iota(tall.shape, 1)
    same = lax.div(row, ROWS) == lax.div(lax.rem(column, block), ROWS)
    return exact_dot(own_lifting, jnp.where(same, tall, 0.0))


def first_kernel(*refs):
    inputs, refs = refs[:INPUTS], refs[INPUTS:]
    held, refs = refs[:INPUTS], refs[INPUTS:]
    (first, second, table, padded, stiff_fold, send_even, send_odd,
     folded, stiffened, arrivals) = refs
    copies = [
        pltpu.make_async_copy(source, target, arrivals.at[k])
        for k, (source, target) in enumerate(zip(inputs, held))
    ]
    for copy in copies:
        copy.start()
    state, stiffness, projector, jac, send_row = held[:FIRST_USED]
    for copy in copies[:FIRST_USED]:
        copy.wait()
    quants, basis, lanes = state.shape
    for q in range(quants):
        value = state[q]
        first[q] = value
        second[q] = value
        folded[:, q * lanes:(q + 1) * lanes] = fold_rows(value)
    fill_projector(projector, padded)
    stacked = jnp.concatenate([stiffness[d] for d in range(3)], axis=0)
    fold = fold_columns(stacked)
    stiff_fold[...] = fold.astype(F32)
    predict(fold, jac, folded, stiffened, first, second, basis, quants, lanes)
    for q in range(quants):
        folded[:, q * lanes:(q + 1) * lanes] = fold_rows(first[q])
    project_table(padded, folded, table, basis, quants, lanes)
    pick_sends(table, send_row, (send_even, send_odd), lanes)
    for copy in copies[FIRST_USED:]:
        copy.wait()


def second_kernel(
    state, first, table, jac, stiffness, padded, rotations, flux, slot,
    part, picked, lifting, turned_fold,
    folded, stiffened, solved,
):
    quants, basis, lanes = state.shape
    turned = jnp.concatenate([stiffness[d].T for d in range(3)], axis=0)
    fold = fold_columns(turned)
    turned_fold[...] = fold.astype(F32)
    own_lifting = padded[...].T[0:basis]
    lifting[...] = near_lifting(own_lifting, rotations)
    picked[...] = pick_local(table[...], slot, 4 * lanes)

    def write(p, value):
        part[p] = value

    local_update(
        lambda p: state[p], lambda q: first[q], table, jac, fold, flux, own_lifting,
        folded, stiffened, solved, write, basis, quants, lanes,
    )


def third_kernel(
    state, first, second, part, picked_local, from_even, from_odd,
    jac, stiff_fold, padded, flux, slot, orient, cluster, lifting, send_row,
    middle, integral, picked, table, send_even, send_odd,
    folded, stiffened, solved,
):
    quants, basis, lanes = state.shape
    picked[...] = picked_local[...] + pick_received(
        (from_even, from_odd), slot, 4 * lanes, lanes
    )
    near = near_lift(picked, flux, orient, lifting[...], solved, quants, lanes)
    fine = cluster[...] == 0
    for q in range(quants):
        value = jnp.where(fine, part[q] - near[:, q * lanes:(q + 1) * lanes], state[q])
        middle[q] = value
        integral[q] = value
        folded[:, q * lanes:(q + 1) * lanes] = fold_rows(value)
    predict(
        stiff_fold[...].astype(BF16), jac, folded, stiffened, integral, None,
        basis, quants, lanes,
    )
    for q in range(quants):
        fine_first = integral[q]
        late = jnp.where(fine, fine_first, second[q])
        folded[:, q * lanes:(q + 1) * lanes] = fold_rows(late)
        integral[q] = jnp.where(fine, fine_first, first[q] + second[q])
    project_table(padded, folded, table, basis, quants, lanes)
    pick_sends(table, send_row, (send_even, send_odd), lanes)


def fourth_kernel(
    middle, integral, table_one, table_two, picked_one, jac, turned_fold, padded, flux, slot,
    cluster,
    part, picked,
    folded, stiffened, solved, total_table,
):
    quants, basis, lanes = middle.shape
    own_lifting = padded[...].T[0:basis]
    coarse = jnp.concatenate([cluster[...] != 0] * 4, axis=1)
    total_table[...] = table_two[...] + jnp.where(coarse, table_one[...], 0.0)
    picked[...] = pick_local(table_two[...], slot, 4 * lanes) + jnp.where(
        coarse, picked_one[...], 0.0
    )

    def write(p, value):
        part[p] = value

    local_update(
        lambda p: middle[p], lambda q: integral[q], total_table, jac, turned_fold[...].astype(BF16), flux,
        own_lifting, folded, stiffened, solved, write, basis, quants, lanes,
    )


def fifth_kernel(
    part, picked_local, from_even, from_odd, flux, slot, orient, lifting,
    yield_stress,
    updated,
    solved, picked,
):
    quants, basis, lanes = part.shape
    picked[...] = picked_local[...] + pick_received(
        (from_even, from_odd), slot, 4 * lanes, lanes
    )
    near = near_lift(picked, flux, orient, lifting[...], solved, quants, lanes)
    stepped = [part[q] - near[:, q * lanes:(q + 1) * lanes] for q in range(quants)]
    mean_part = (stepped[0] + stepped[1] + stepped[2]) / 3.0
    spread = [stepped[q] - mean_part for q in range(3)]
    normal = [item[0:1] for item in spread]
    shear = [stepped[q][0:1] for q in range(3, 6)]
    second_inv = 0.5 * (normal[0] ** 2 + normal[1] ** 2 + normal[2] ** 2) + (
        shear[0] ** 2 + shear[1] ** 2 + shear[2] ** 2
    )
    limit = yield_stress[...]
    scaling = limit / jnp.maximum(jnp.sqrt(second_inv), limit)
    for q in range(3):
        updated[q] = mean_part + scaling * spread[q]
    for q in range(3, 6):
        updated[q] = scaling * stepped[q]
    for q in range(6, quants):
        updated[q] = stepped[q]


def run(body, outs, scratch, *operands, space=pltpu.VMEM, grant=32):
    vmem = pl.BlockSpec(memory_space=pltpu.VMEM)
    return pl.pallas_call(
        body,
        out_shape=[
            out if isinstance(out, jax.ShapeDtypeStruct) else jax.ShapeDtypeStruct(out, F32)
            for out in outs
        ],
        in_specs=[pl.BlockSpec(memory_space=space)] * len(operands),
        out_specs=[vmem] * len(outs),
        scratch_shapes=scratch,
        compiler_params=pltpu.CompilerParams(vmem_limit_bytes=grant * 1024 * 1024),
        name=body.__name__,
    )(*operands)


def blocks(shift):
    rows, columns = lax.axis_size("dom"), lax.axis_size("sub")
    groups = []
    for i in range(shift, rows + shift, 2):
        for j in range(shift, columns + shift, 2):
            groups.append(
                [(i + u) % rows * columns + (j + v) % columns for u in (0, 1) for v in (0, 1)]
            )
    return groups


def exchange(sends):
    return [
        lax.all_gather(value, ("dom", "sub"), axis_index_groups=blocks(shift))
        for shift, value in enumerate(sends)
    ]


def on_device(
    modal_state,
    stiffness,
    jacobians,
    flux_solvers,
    projector,
    rotations,
    yield_stress,
    cluster,
    orient,
    neighbour_slot,
    send_map,
):
    basis, quants, lanes = modal_state.shape
    inputs = [
        jnp.transpose(modal_state, (1, 0, 2)),
        stiffness,
        jnp.transpose(projector, (1, 0, 2)),
        jnp.transpose(jacobians, (1, 2, 0, 3)),
        send_map.reshape(1, -1),
        jnp.transpose(flux_solvers, (0, 2, 3, 1, 4)),
        rotations,
        neighbour_slot,
        orient,
        cluster.reshape(1, lanes),
        yield_stress.reshape(1, lanes),
    ]
    inputs = [pltpu.with_memory_space_constraint(item, pltpu.HBM) for item in inputs]
    held = [jax.ShapeDtypeStruct(item.shape, item.dtype) for item in inputs]

    field = (quants, basis, lanes)
    table = (quants * ROWS, 4 * lanes)
    message = ((DOM_GROUPS[0][1] + SUB_GROUPS[0][1]) * ROWS, lanes)
    depth = fold_depth(basis)
    flat = quants * lanes
    fold = (3 * basis, depth)
    folded = pltpu.VMEM((depth, flat), BF16)
    stiffened = pltpu.VMEM((3 * basis, flat), F32)
    own_solved = pltpu.VMEM((4 * ROWS, flat), F32)
    near_solved = pltpu.VMEM((2 * 3 * 4 * ROWS, flat), F32)

    outs = run(
        first_kernel,
        held + [field, field, table, (4 * ROWS, 128), fold, message, message],
        [folded, stiffened, pltpu.SemaphoreType.DMA((INPUTS,))],
        *inputs, space=pl.ANY, grant=GRANT,
    )
    state, stiff, _, jac, send_row, flux, turns, slot, orient, cluster, limit = outs[:INPUTS]
    first, second, table_one, padded, stiff_fold, *sends = outs[INPUTS:]
    arrived = exchange(sends)
    part_one, local_one, lifting, turned_fold = run(
        second_kernel, [field, table, (basis, 3 * 4 * ROWS), fold],
        [folded, stiffened, own_solved],
        state, first, table_one, jac, stiff, padded, turns, flux, slot,
    )
    middle, integral, picked_one, table_two, *sends = run(
        third_kernel, [field, field, table, table, message, message],
        [folded, stiffened, near_solved],
        state, first, second, part_one, local_one, *arrived,
        jac, stiff_fold, padded, flux, slot, orient, cluster, lifting, send_row,
    )
    arrived = exchange(sends)
    part_two, local_two = run(
        fourth_kernel, [field, table],
        [folded, stiffened, own_solved, pltpu.VMEM(table, F32)],
        middle, integral, table_one, table_two, picked_one, jac, turned_fold, padded, flux,
        slot, cluster,
    )
    updated, = run(
        fifth_kernel, [field], [near_solved, pltpu.VMEM(table, F32)],
        part_two, local_two, *arrived, flux, slot, orient, lifting, limit,
    )
    return jnp.transpose(updated, (1, 0, 2))


def solution(mesh):
    placed = (
        P(None, None, ("dom", "sub")),
        P(),
        P(None, None, None, ("dom", "sub")),
        P(None, None, None, None, ("dom", "sub")),
        P(),
        P(),
        P(("dom", "sub")),
        P(("dom", "sub")),
        P(None, ("dom", "sub")),
        P(None, ("dom", "sub")),
        P(("dom", "sub")),
    )
    return jax.shard_map(
        on_device,
        mesh=mesh,
        in_specs=placed,
        out_specs=P(None, None, ("dom", "sub")),
        check_vma=False,
    )
```

```python
import math

import jax
import jax.numpy as jnp
from jax import lax
from jax.experimental import pallas as pl
from jax.experimental.pallas import tpu as pltpu
from jax.sharding import PartitionSpec as P

ORDER = 6
SLOTS_DOM = 64
SLOTS_SUB = 32
ROWS = 24
GROUP = 3

F32 = jnp.float32
BF16 = jnp.bfloat16
EXACT = lax.Precision.HIGHEST

DOM_GROUPS = ((0, 5), (5, 4))
SUB_GROUPS = ((0, 3), (3, 2), (5, 2), (7, 2))
PACKING = (DOM_GROUPS, DOM_GROUPS, SUB_GROUPS, SUB_GROUPS)

INPUTS = 11
FIRST_USED = 5


def iota(shape, dim):
    return lax.broadcasted_iota(jnp.int32, shape, dim)


def dot(a, b):
    return jnp.dot(a, b, preferred_element_type=F32)


def exact_dot(a, b):
    return jnp.dot(a, b, precision=EXACT, preferred_element_type=F32)


def halves(value):
    high = value.astype(BF16)
    return high, (value - high.astype(F32)).astype(BF16)


def one_hot(index_row, first, count, modulus=None):
    number = iota((count, index_row.shape[1]), 0)
    if modulus is not None:
        number = lax.rem(number, modulus)
    return jnp.where(number + first == index_row, 1.0, 0.0).astype(BF16)


def fold_depth(basis):
    return -(-3 * basis // 64) * 64


def fold_rows(value):
    basis, lanes = value.shape
    high = value.astype(BF16).astype(F32)
    rest = jnp.zeros((fold_depth(basis) - 3 * basis, lanes), F32)
    return jnp.concatenate([high, high, value - high, rest], axis=0).astype(BF16)


def fold_columns(matrix):
    basis = matrix.shape[1]
    depth = fold_depth(basis)
    high, low = halves(matrix)
    row, column = iota((basis, depth), 0), iota((basis, depth), 1)
    outer = jnp.where((column == row) | (column == row + 2 * basis), 1.0, 0.0).astype(BF16)
    inner = jnp.where(column == row + basis, 1.0, 0.0).astype(BF16)
    return (dot(high, outer) + dot(low, inner)).astype(BF16)


def stiffen(stiff_fold, values, target, start, lanes):
    folded = jnp.concatenate([fold_rows(value) for value in values], axis=1)
    target[:, start * lanes:(start + len(values)) * lanes] = dot(stiff_fold, folded)


def mix_jacobians(stiffened, jac, basis, quants, lanes, take):
    for start in range(0, quants, GROUP):
        totals = [None] * GROUP
        for q in range(quants):
            for d in range(3):
                block = stiffened[d * basis:(d + 1) * basis, q * lanes:(q + 1) * lanes]
                for i in range(GROUP):
                    term = block * jac[q, start + i, d:d + 1, :]
                    totals[i] = term if totals[i] is None else totals[i] + term
        take(start, totals)


def mix_faces(table, flux, side, quants, lanes, write):
    for f in range(4):
        blocks = [
            table[q * ROWS:(q + 1) * ROWS, f * lanes:(f + 1) * lanes] for q in range(quants)
        ]
        for p in range(quants):
            total = blocks[0] * flux[side, 0, p, f:f + 1, :]
            for q in range(1, quants):
                total = total + blocks[q] * flux[side, q, p, f:f + 1, :]
            write(f, p, total)


def fill_projector(projector, padded):
    modes, faces, basis = projector.shape
    padded[...] = jnp.zeros(padded.shape, F32)
    for f in range(faces):
        for m in range(modes):
            padded[f * ROWS + m:f * ROWS + m + 1, 0:basis] = projector[m, f:f + 1, :]


def predict(stiff_fold, jac, state, stiffened, first, second, basis, quants, lanes):
    for start in range(0, quants, GROUP):
        values = [state(q) for q in range(start, start + GROUP)]
        stiffen(stiff_fold, values, stiffened.at[0], start, lanes)
    for order in range(1, ORDER):
        factor = 1.0 / math.factorial(order + 1)

        def take(start, totals):
            if order + 1 < ORDER:
                stiffen(stiff_fold, totals, stiffened.at[order % 2], start, lanes)
            for p, total in enumerate(totals, start):
                first[p] = first[p] + factor * total
                if second is not None:
                    second[p] = second[p] + (2.0 ** (order + 1) - 1.0) * factor * total

        mix_jacobians(stiffened.at[(order - 1) % 2], jac, basis, quants, lanes, take)


def project_table(padded, field, table, basis, quants, lanes):
    fold = fold_columns(padded[:, 0:basis])
    for start in range(0, quants, GROUP):
        values = [fold_rows(field(q)) for q in range(start, start + GROUP)]
        flat = dot(fold, jnp.concatenate(values, axis=1))
        for q in range(start, start + GROUP):
            for f in range(4):
                table[q * ROWS:(q + 1) * ROWS, f * lanes:(f + 1) * lanes] = flat[
                    f * ROWS:(f + 1) * ROWS, (q - start) * lanes:(q - start + 1) * lanes
                ]


def pick_sends(table, send_row, outs, lanes):
    faces = table.shape[1]
    low = jnp.broadcast_to(send_row[:, 0:lanes], (8, lanes))
    lane = iota((8, lanes), 1)
    turned = pltpu.roll(low, SLOTS_DOM, 1)
    high = send_row[:, 2 * SLOTS_DOM:2 * SLOTS_DOM + 2 * SLOTS_SUB]
    spread = jnp.broadcast_to(jnp.concatenate([high, high], axis=1), (8, lanes))
    moved = pltpu.roll(spread, SLOTS_SUB, 1)
    left = lax.rem(lane, 2 * SLOTS_SUB) < SLOTS_SUB
    pieces = [
        jnp.where(lane < SLOTS_DOM, low, turned),
        jnp.where(lane < SLOTS_DOM, turned, low),
        jnp.where(left, spread, moved),
        jnp.where(left, moved, spread),
    ]
    index = jnp.concatenate([piece[0:1] for piece in pieces], axis=1)
    chosen = one_hot(index, 0, faces)
    upper, lower = halves(table[...])
    sent = dot(upper, chosen) + dot(lower, chosen)
    for k, (out, groups) in enumerate(zip(outs, PACKING)):
        width = lanes // len(groups)
        values = sent[:, k * lanes:(k + 1) * lanes]
        start, count = groups[0]
        packed = values[0:count * ROWS]
        least = min(count for _, count in groups) * ROWS
        spot = iota((least, lanes), 1)
        head = packed[0:least]
        for g, (start, _) in enumerate(groups):
            if g:
                head = jnp.where(
                    spot >= g * width, values[start * ROWS:start * ROWS + least], head
                )
        out[0:least] = head
        out[least:count * ROWS] = packed[least:]


def spread_received(arrived, groups, lanes):
    width = lanes // len(groups)
    parts = []
    for g, (_, count) in enumerate(groups):
        place = iota((count * ROWS, lanes), 1)
        mine = (place >= g * width) & (place < (g + 1) * width)
        parts.append(jnp.where(mine, arrived[0:count * ROWS], 0.0))
    return jnp.concatenate(parts, axis=0)


def pick_local(table, slot, faces):
    chosen = jnp.concatenate([one_hot(slot[f:f + 1], 0, faces) for f in range(4)], axis=1)
    upper, lower = halves(table)
    return dot(upper, chosen) + dot(lower, chosen)


def pick_received(arrived, slot, faces, lanes):
    spread = jnp.concatenate(
        [spread_received(item[...], groups, lanes) for item, groups in zip(arrived, PACKING)],
        axis=1,
    )
    starts = (faces, faces + SLOTS_DOM, faces + 2 * SLOTS_DOM, faces + 2 * SLOTS_DOM + SLOTS_SUB)
    widths = (SLOTS_DOM, SLOTS_DOM, SLOTS_SUB, SLOTS_SUB)
    chosen = jnp.concatenate(
        [
            jnp.concatenate(
                [one_hot(slot[f:f + 1], first, lanes, width) for f in range(4)], axis=1
            )
            for first, width in zip(starts, widths)
        ],
        axis=0,
    )
    upper, lower = halves(spread)
    return dot(upper, chosen) + dot(lower, chosen)


def lift(weights, high, low):
    upper, lower = halves(weights)
    return dot(upper, high) + dot(lower, high) + dot(upper, low)


def local_update(
    base, integral, table, jac, turned_fold, flux, lifting, stiffened, solved, write,
    basis, quants, lanes,
):
    for start in range(0, quants, GROUP):
        values = [integral(q) for q in range(start, start + GROUP)]
        stiffen(turned_fold, values, stiffened, start, lanes)

    def keep(f, p, total):
        solved[f * ROWS:(f + 1) * ROWS, p * lanes:(p + 1) * lanes] = total

    mix_faces(table, flux, 0, quants, lanes, keep)
    high, low = halves(solved[...])
    own = lift(lifting, high, low)

    def take(start, totals):
        for p, total in enumerate(totals, start):
            write(p, base(p) + total - own[:, p * lanes:(p + 1) * lanes])

    mix_jacobians(stiffened, jac, basis, quants, lanes, take)


def near_lift(picked, flux, orient, lifting, solved, quants, lanes):
    block = 4 * ROWS

    def keep(f, p, total):
        upper = total.astype(BF16).astype(F32)
        lower = total - upper
        for o in range(3):
            mine = orient[f:f + 1] == o
            row = o * block + f * ROWS
            solved[row:row + ROWS, p * lanes:(p + 1) * lanes] = jnp.where(mine, upper, 0.0)
            row += 3 * block
            solved[row:row + ROWS, p * lanes:(p + 1) * lanes] = jnp.where(mine, lower, 0.0)

    mix_faces(picked, flux, 1, quants, lanes, keep)
    depth = 3 * block
    return lift(lifting, solved[0:depth].astype(BF16), solved[depth:2 * depth].astype(BF16))


def near_lifting(own_lifting, rotations):
    count, modes, _ = rotations.shape
    block = 4 * ROWS
    row, column = iota((modes, count * block), 0), iota((modes, count * block), 1)
    turned = jnp.zeros((modes, count * block), F32)
    for o in range(count):
        spot = (lax.rem(column, ROWS) == row) & (lax.div(column, block) == o)
        turned = turned + exact_dot(rotations[o], jnp.where(spot, 1.0, 0.0))
    row, column = iota((block, modes), 0), iota((block, modes), 1)
    tall = exact_dot(jnp.where(lax.rem(row, ROWS) == column, 1.0, 0.0), turned)
    row, column = iota(tall.shape, 0), iota(tall.shape, 1)
    same = lax.div(row, ROWS) == lax.div(lax.rem(column, block), ROWS)
    return exact_dot(own_lifting, jnp.where(same, tall, 0.0))


def first_kernel(*refs):
    inputs, refs = refs[:INPUTS], refs[INPUTS:]
    held, refs = refs[:INPUTS], refs[INPUTS:]
    first, second, table, padded, stiff_fold, *sends, stiffened, arrivals = refs
    copies = [
        pltpu.make_async_copy(source, target, arrivals.at[k])
        for k, (source, target) in enumerate(zip(inputs, held))
    ]
    for copy in copies:
        copy.start()
    state, stiffness, projector, jac, send_row = held[:FIRST_USED]
    for copy in copies[:FIRST_USED]:
        copy.wait()
    quants, basis, lanes = state.shape
    for q in range(quants):
        value = state[q]
        first[q] = value
        second[q] = value
    fill_projector(projector, padded)
    stacked = jnp.concatenate([stiffness[d] for d in range(3)], axis=0)
    fold = fold_columns(stacked)
    stiff_fold[...] = fold.astype(F32)
    predict(
        fold, jac, lambda q: state[q], stiffened, first, second, basis, quants, lanes
    )
    project_table(padded, lambda q: first[q], table, basis, quants, lanes)
    pick_sends(table, send_row, sends, lanes)
    for copy in copies[FIRST_USED:]:
        copy.wait()


def second_kernel(
    state, first, table, jac, stiffness, padded, rotations, flux, slot,
    part, picked, lifting, turned_fold,
    stiffened, solved,
):
    quants, basis, lanes = state.shape
    turned = jnp.concatenate([stiffness[d].T for d in range(3)], axis=0)
    fold = fold_columns(turned)
    turned_fold[...] = fold.astype(F32)
    own_lifting = padded[...].T[0:basis]
    lifting[...] = near_lifting(own_lifting, rotations)
    picked[...] = pick_local(table[...], slot, 4 * lanes)

    def write(p, value):
        part[p] = value

    local_update(
        lambda p: state[p], lambda q: first[q], table, jac, fold, flux, own_lifting,
        stiffened, solved, write, basis, quants, lanes,
    )


def third_kernel(
    state, first, second, part, picked_local, from_lower, from_upper, from_left, from_right,
    jac, stiff_fold, padded, flux, slot, orient, cluster, lifting, send_row,
    middle, integral, picked, table, to_lower, to_upper, to_left, to_right,
    stiffened, solved,
):
    quants, basis, lanes = state.shape
    picked[...] = picked_local[...] + pick_received(
        (from_lower, from_upper, from_left, from_right), slot, 4 * lanes, lanes
    )
    near = near_lift(picked, flux, orient, lifting[...], solved, quants, lanes)
    fine = cluster[...] == 0
    for q in range(quants):
        value = jnp.where(fine, part[q] - near[:, q * lanes:(q + 1) * lanes], state[q])
        middle[q] = value
        integral[q] = value
    predict(
        stiff_fold[...].astype(BF16), jac, lambda q: middle[q], stiffened, integral, None,
        basis, quants, lanes,
    )
    project_table(
        padded, lambda q: jnp.where(fine, integral[q], second[q]), table, basis, quants, lanes
    )
    for q in range(quants):
        integral[q] = jnp.where(fine, integral[q], first[q] + second[q])
    pick_sends(table, send_row, (to_lower, to_upper, to_left, to_right), lanes)


def fourth_kernel(
    middle, integral, table_one, table_two, picked_one, jac, turned_fold, padded, flux, slot,
    cluster,
    part, picked,
    stiffened, solved, total_table,
):
    quants, basis, lanes = middle.shape
    own_lifting = padded[...].T[0:basis]
    coarse = jnp.concatenate([cluster[...] != 0] * 4, axis=1)
    total_table[...] = table_two[...] + jnp.where(coarse, table_one[...], 0.0)
    picked[...] = pick_local(table_two[...], slot, 4 * lanes) + jnp.where(
        coarse, picked_one[...], 0.0
    )

    def write(p, value):
        part[p] = value

    local_update(
        lambda p: middle[p], lambda q: integral[q], total_table, jac, turned_fold[...].astype(BF16), flux,
        own_lifting, stiffened, solved, write, basis, quants, lanes,
    )


def fifth_kernel(
    part, picked_local, from_lower, from_upper, from_left, from_right, flux, slot, orient, lifting,
    yield_stress,
    updated,
    solved, picked,
):
    quants, basis, lanes = part.shape
    picked[...] = picked_local[...] + pick_received(
        (from_lower, from_upper, from_left, from_right), slot, 4 * lanes, lanes
    )
    near = near_lift(picked, flux, orient, lifting[...], solved, quants, lanes)
    stepped = [part[q] - near[:, q * lanes:(q + 1) * lanes] for q in range(quants)]
    mean_part = (stepped[0] + stepped[1] + stepped[2]) / 3.0
    spread = [stepped[q] - mean_part for q in range(3)]
    normal = [item[0:1] for item in spread]
    shear = [stepped[q][0:1] for q in range(3, 6)]
    second_inv = 0.5 * (normal[0] ** 2 + normal[1] ** 2 + normal[2] ** 2) + (
        shear[0] ** 2 + shear[1] ** 2 + shear[2] ** 2
    )
    limit = yield_stress[...]
    scaling = limit / jnp.maximum(jnp.sqrt(second_inv), limit)
    for q in range(3):
        updated[q] = mean_part + scaling * spread[q]
    for q in range(3, 6):
        updated[q] = scaling * stepped[q]
    for q in range(6, quants):
        updated[q] = stepped[q]


def run(body, outs, scratch, *operands, space=pltpu.VMEM):
    vmem = pl.BlockSpec(memory_space=pltpu.VMEM)
    return pl.pallas_call(
        body,
        out_shape=[
            out if isinstance(out, jax.ShapeDtypeStruct) else jax.ShapeDtypeStruct(out, F32)
            for out in outs
        ],
        in_specs=[pl.BlockSpec(memory_space=space)] * len(operands),
        out_specs=[vmem] * len(outs),
        scratch_shapes=scratch,
        compiler_params=pltpu.CompilerParams(vmem_limit_bytes=32 * 1024 * 1024),
        name=body.__name__,
    )(*operands)


def exchange(sends):
    to_lower, to_upper, to_left, to_right = sends

    def shift(value, axis, step):
        size = lax.axis_size(axis)
        pairs = [(i, i + step) for i in range(size) if 0 <= i + step < size]
        return lax.ppermute(value, axis, pairs)

    return (
        shift(to_upper, "dom", 1),
        shift(to_lower, "dom", -1),
        shift(to_right, "sub", 1),
        shift(to_left, "sub", -1),
    )


def on_device(
    modal_state,
    stiffness,
    jacobians,
    flux_solvers,
    projector,
    rotations,
    yield_stress,
    cluster,
    orient,
    neighbour_slot,
    send_map,
):
    basis, quants, lanes = modal_state.shape
    inputs = [
        jnp.transpose(modal_state, (1, 0, 2)),
        stiffness,
        jnp.transpose(projector, (1, 0, 2)),
        jnp.transpose(jacobians, (1, 2, 0, 3)),
        send_map.reshape(1, -1),
        jnp.transpose(flux_solvers, (0, 2, 3, 1, 4)),
        rotations,
        neighbour_slot,
        orient,
        cluster.reshape(1, lanes),
        yield_stress.reshape(1, lanes),
    ]
    inputs = [pltpu.with_memory_space_constraint(item, pltpu.HBM) for item in inputs]
    held = [jax.ShapeDtypeStruct(item.shape, item.dtype) for item in inputs]

    field = (quants, basis, lanes)
    table = (quants * ROWS, 4 * lanes)
    messages = [(groups[0][1] * ROWS, lanes) for groups in PACKING]
    depth = fold_depth(basis)
    flat = quants * lanes
    fold = (3 * basis, depth)
    stiffened = pltpu.VMEM((3 * basis, flat), F32)
    two_stiffened = pltpu.VMEM((2, 3 * basis, flat), F32)
    own_solved = pltpu.VMEM((4 * ROWS, flat), F32)
    near_solved = pltpu.VMEM((2 * 3 * 4 * ROWS, flat), F32)

    outs = run(
        first_kernel,
        held + [field, field, table, (4 * ROWS, 128), fold] + messages,
        [two_stiffened, pltpu.SemaphoreType.DMA((INPUTS,))],
        *inputs, space=pl.ANY,
    )
    state, stiff, _, jac, send_row, flux, turns, slot, orient, cluster, limit = outs[:INPUTS]
    first, second, table_one, padded, stiff_fold, *sends = outs[INPUTS:]
    arrived = exchange(sends)
    part_one, local_one, lifting, turned_fold = run(
        second_kernel, [field, table, (basis, 3 * 4 * ROWS), fold],
        [stiffened, own_solved],
        state, first, table_one, jac, stiff, padded, turns, flux, slot,
    )
    middle, integral, picked_one, table_two, *sends = run(
        third_kernel, [field, field, table, table] + messages,
        [two_stiffened, near_solved],
        state, first, second, part_one, local_one, *arrived,
        jac, stiff_fold, padded, flux, slot, orient, cluster, lifting, send_row,
    )
    arrived = exchange(sends)
    part_two, local_two = run(
        fourth_kernel, [field, table],
        [stiffened, own_solved, pltpu.VMEM(table, F32)],
        middle, integral, table_one, table_two, picked_one, jac, turned_fold, padded, flux,
        slot, cluster,
    )
    updated, = run(
        fifth_kernel, [field], [near_solved, pltpu.VMEM(table, F32)],
        part_two, local_two, *arrived, flux, slot, orient, lifting, limit,
    )
    return jnp.transpose(updated, (1, 0, 2))


def solution(mesh):
    placed = (
        P(None, None, ("dom", "sub")),
        P(),
        P(None, None, None, ("dom", "sub")),
        P(None, None, None, None, ("dom", "sub")),
        P(),
        P(),
        P(("dom", "sub")),
        P(("dom", "sub")),
        P(None, ("dom", "sub")),
        P(None, ("dom", "sub")),
        P(("dom", "sub")),
    )
    return jax.shard_map(
        on_device,
        mesh=mesh,
        in_specs=placed,
        out_specs=P(None, None, ("dom", "sub")),
        check_vma=False,
    )
```

```python
import math

import jax
import jax.numpy as jnp
from jax import lax
from jax.experimental import pallas as pl
from jax.experimental.pallas import tpu as pltpu
from jax.sharding import PartitionSpec as P

ORDER = 6
SLOTS_DOM = 64
SLOTS_SUB = 32
ROWS = 24
GROUP = 3

F32 = jnp.float32
BF16 = jnp.bfloat16
EXACT = lax.Precision.HIGHEST

DOM_GROUPS = ((0, 5), (5, 4))
SUB_GROUPS = ((0, 3), (3, 2), (5, 2), (7, 2))
PACKING = (DOM_GROUPS, DOM_GROUPS, SUB_GROUPS, SUB_GROUPS)

INPUTS = 11
FIRST_USED = 5


def iota(shape, dim):
    return lax.broadcasted_iota(jnp.int32, shape, dim)


def dot(a, b):
    return jnp.dot(a, b, preferred_element_type=F32)


def exact_dot(a, b):
    return jnp.dot(a, b, precision=EXACT, preferred_element_type=F32)


def halves(value):
    high = value.astype(BF16)
    return high, (value - high.astype(F32)).astype(BF16)


def one_hot(index_row, first, count, modulus=None):
    number = iota((count, index_row.shape[1]), 0)
    if modulus is not None:
        number = lax.rem(number, modulus)
    return jnp.where(number + first == index_row, 1.0, 0.0).astype(BF16)


def fold_step(basis):
    return -(-basis // 16) * 16


def fold_rows(value):
    basis, lanes = value.shape
    rest = jnp.zeros((fold_step(basis) - basis, lanes), F32)
    value = jnp.concatenate([value, rest], axis=0)
    high, low = halves(value)
    return jnp.concatenate([high, high, low], axis=0)


def fold_columns(matrix):
    basis = matrix.shape[1]
    step = fold_step(basis)
    high, low = halves(matrix)
    row, column = iota((basis, 3 * step), 0), iota((basis, 3 * step), 1)
    outer = jnp.where((column == row) | (column == row + 2 * step), 1.0, 0.0).astype(BF16)
    inner = jnp.where(column == row + step, 1.0, 0.0).astype(BF16)
    return (dot(high, outer) + dot(low, inner)).astype(BF16)


def stiffen(stiff_fold, values, target, start, lanes):
    folded = jnp.concatenate([fold_rows(value) for value in values], axis=1)
    target[:, start * lanes:(start + len(values)) * lanes] = dot(stiff_fold, folded)


def mix_jacobians(stiffened, jac, basis, quants, lanes, take):
    for start in range(0, quants, GROUP):
        totals = [None] * GROUP
        for q in range(quants):
            for d in range(3):
                block = stiffened[d * basis:(d + 1) * basis, q * lanes:(q + 1) * lanes]
                block = block.reshape(basis // 8, 8, lanes)
                for i in range(GROUP):
                    term = block * jac[q, start + i, pl.ds(d, 8, stride=0), :]
                    totals[i] = term if totals[i] is None else totals[i] + term
        take(start, [total.reshape(basis, lanes) for total in totals])


def mix_faces(table, flux, side, quants, lanes, write):
    for f in range(4):
        blocks = [
            table[q * ROWS:(q + 1) * ROWS, f * lanes:(f + 1) * lanes].reshape(
                ROWS // 8, 8, lanes
            )
            for q in range(quants)
        ]
        for p in range(quants):
            total = blocks[0] * flux[side, 0, p, pl.ds(f, 8, stride=0), :]
            for q in range(1, quants):
                total = total + blocks[q] * flux[side, q, p, pl.ds(f, 8, stride=0), :]
            write(f, p, total.reshape(ROWS, lanes))


def fill_projector(projector, padded):
    modes, faces, basis = projector.shape
    padded[...] = jnp.zeros(padded.shape, F32)
    for f in range(faces):
        for m in range(modes):
            padded[f * ROWS + m:f * ROWS + m + 1, 0:basis] = projector[m, f:f + 1, :]


def predict(stiff_fold, jac, state, stiffened, first, second, basis, quants, lanes):
    for start in range(0, quants, GROUP):
        values = [state(q) for q in range(start, start + GROUP)]
        stiffen(stiff_fold, values, stiffened.at[0], start, lanes)
    for order in range(1, ORDER):
        factor = 1.0 / math.factorial(order + 1)

        def take(start, totals):
            if order + 1 < ORDER:
                stiffen(stiff_fold, totals, stiffened.at[order % 2], start, lanes)
            for p, total in enumerate(totals, start):
                first[p] = first[p] + factor * total
                if second is not None:
                    second[p] = second[p] + (2.0 ** (order + 1) - 1.0) * factor * total

        mix_jacobians(stiffened.at[(order - 1) % 2], jac, basis, quants, lanes, take)


def project_table(padded, field, table, basis, quants, lanes):
    fold = fold_columns(padded[:, 0:basis])
    for start in range(0, quants, GROUP):
        values = [fold_rows(field(q)) for q in range(start, start + GROUP)]
        flat = dot(fold, jnp.concatenate(values, axis=1))
        for q in range(start, start + GROUP):
            for f in range(4):
                table[q * ROWS:(q + 1) * ROWS, f * lanes:(f + 1) * lanes] = flat[
                    f * ROWS:(f + 1) * ROWS, (q - start) * lanes:(q - start + 1) * lanes
                ]


def even_spot():
    return [lax.rem(lax.axis_index(axis), 2) == 0 for axis in ("dom", "sub")]


def pick_sends(table, send_row, outs, lanes):
    faces = table.shape[1]
    low = jnp.broadcast_to(send_row[:, 0:lanes], (8, lanes))
    lane = iota((8, lanes), 1)
    turned = pltpu.roll(low, SLOTS_DOM, 1)
    high = send_row[:, 2 * SLOTS_DOM:2 * SLOTS_DOM + 2 * SLOTS_SUB]
    spread = jnp.broadcast_to(jnp.concatenate([high, high], axis=1), (8, lanes))
    moved = pltpu.roll(spread, SLOTS_SUB, 1)
    left = lax.rem(lane, 2 * SLOTS_SUB) < SLOTS_SUB
    pieces = [
        jnp.where(lane < SLOTS_DOM, low, turned),
        jnp.where(lane < SLOTS_DOM, turned, low),
        jnp.where(left, spread, moved),
        jnp.where(left, moved, spread),
    ]
    even_dom, even_sub = even_spot()
    pieces = [
        jnp.where(even_dom, pieces[1], pieces[0]),
        jnp.where(even_dom, pieces[0], pieces[1]),
        jnp.where(even_sub, pieces[3], pieces[2]),
        jnp.where(even_sub, pieces[2], pieces[3]),
    ]
    index = jnp.concatenate([piece[0:1] for piece in pieces], axis=1)
    chosen = one_hot(index, 0, faces)
    upper, lower = halves(table[...])
    sent = dot(upper, chosen) + dot(lower, chosen)
    for k, (out, groups) in enumerate(zip(outs, PACKING)):
        width = lanes // len(groups)
        values = sent[:, k * lanes:(k + 1) * lanes]
        start, count = groups[0]
        packed = values[0:count * ROWS]
        least = min(count for _, count in groups) * ROWS
        spot = iota((least, lanes), 1)
        head = packed[0:least]
        for g, (start, _) in enumerate(groups):
            if g:
                head = jnp.where(
                    spot >= g * width, values[start * ROWS:start * ROWS + least], head
                )
        out[0:least] = head
        out[least:count * ROWS] = packed[least:]


def spread_received(arrived, groups, lanes):
    width = lanes // len(groups)
    parts = []
    for g, (_, count) in enumerate(groups):
        place = iota((count * ROWS, lanes), 1)
        mine = (place >= g * width) & (place < (g + 1) * width)
        parts.append(jnp.where(mine, arrived[0:count * ROWS], 0.0))
    return jnp.concatenate(parts, axis=0)


def pick_local(table, slot, faces):
    chosen = jnp.concatenate([one_hot(slot[f:f + 1], 0, faces) for f in range(4)], axis=1)
    upper, lower = halves(table)
    return dot(upper, chosen) + dot(lower, chosen)


def pick_received(arrived, slot, faces, lanes):
    spread = jnp.concatenate(
        [spread_received(item[...], groups, lanes) for item, groups in zip(arrived, PACKING)],
        axis=1,
    )
    even_dom, even_sub = even_spot()
    starts = (
        jnp.where(even_dom, faces + SLOTS_DOM, faces),
        jnp.where(even_dom, faces, faces + SLOTS_DOM),
        faces + 2 * SLOTS_DOM + jnp.where(even_sub, SLOTS_SUB, 0),
        faces + 2 * SLOTS_DOM + jnp.where(even_sub, 0, SLOTS_SUB),
    )
    widths = (SLOTS_DOM, SLOTS_DOM, SLOTS_SUB, SLOTS_SUB)
    chosen = jnp.concatenate(
        [
            jnp.concatenate(
                [one_hot(slot[f:f + 1], first, lanes, width) for f in range(4)], axis=1
            )
            for first, width in zip(starts, widths)
        ],
        axis=0,
    )
    upper, lower = halves(spread)
    return dot(upper, chosen) + dot(lower, chosen)


def lift(weights, high, low):
    upper, lower = halves(weights)
    return dot(upper, high) + dot(lower, high) + dot(upper, low)


def local_update(
    base, integral, table, jac, turned_fold, flux, lifting, stiffened, solved, write,
    basis, quants, lanes,
):
    for start in range(0, quants, GROUP):
        values = [integral(q) for q in range(start, start + GROUP)]
        stiffen(turned_fold, values, stiffened, start, lanes)

    def keep(f, p, total):
        solved[f * ROWS:(f + 1) * ROWS, p * lanes:(p + 1) * lanes] = total

    mix_faces(table, flux, 0, quants, lanes, keep)
    high, low = halves(solved[...])
    own = lift(lifting, high, low)

    def take(start, totals):
        for p, total in enumerate(totals, start):
            write(p, base(p) + total - own[:, p * lanes:(p + 1) * lanes])

    mix_jacobians(stiffened, jac, basis, quants, lanes, take)


def near_lift(picked, flux, orient, lifting, solved, quants, lanes):
    block = 4 * ROWS

    def keep(f, p, total):
        upper = total.astype(BF16).astype(F32)
        lower = total - upper
        for o in range(3):
            mine = orient[f:f + 1] == o
            row = o * block + f * ROWS
            solved[row:row + ROWS, p * lanes:(p + 1) * lanes] = jnp.where(mine, upper, 0.0)
            row += 3 * block
            solved[row:row + ROWS, p * lanes:(p + 1) * lanes] = jnp.where(mine, lower, 0.0)

    mix_faces(picked, flux, 1, quants, lanes, keep)
    depth = 3 * block
    return lift(lifting, solved[0:depth].astype(BF16), solved[depth:2 * depth].astype(BF16))


def near_lifting(own_lifting, rotations):
    count, modes, _ = rotations.shape
    block = 4 * ROWS
    row, column = iota((modes, count * block), 0), iota((modes, count * block), 1)
    turned = jnp.zeros((modes, count * block), F32)
    for o in range(count):
        spot = (lax.rem(column, ROWS) == row) & (lax.div(column, block) == o)
        turned = turned + exact_dot(rotations[o], jnp.where(spot, 1.0, 0.0))
    row, column = iota((block, modes), 0), iota((block, modes), 1)
    tall = exact_dot(jnp.where(lax.rem(row, ROWS) == column, 1.0, 0.0), turned)
    row, column = iota(tall.shape, 0), iota(tall.shape, 1)
    same = lax.div(row, ROWS) == lax.div(lax.rem(column, block), ROWS)
    return exact_dot(own_lifting, jnp.where(same, tall, 0.0))


def first_kernel(*refs):
    inputs, refs = refs[:INPUTS], refs[INPUTS:]
    held, refs = refs[:INPUTS], refs[INPUTS:]
    first, second, table, padded, stiff_fold, *sends, stiffened, arrivals = refs
    copies = [
        pltpu.make_async_copy(source, target, arrivals.at[k])
        for k, (source, target) in enumerate(zip(inputs, held))
    ]
    for copy in copies:
        copy.start()
    state, stiffness, projector, jac, send_row = held[:FIRST_USED]
    for copy in copies[:FIRST_USED]:
        copy.wait()
    quants, basis, lanes = state.shape
    for q in range(quants):
        value = state[q]
        first[q] = value
        second[q] = value
    fill_projector(projector, padded)
    stacked = jnp.concatenate([stiffness[d] for d in range(3)], axis=0)
    fold = fold_columns(stacked)
    stiff_fold[...] = fold.astype(F32)
    predict(
        fold, jac, lambda q: state[q], stiffened, first, second, basis, quants, lanes
    )
    project_table(padded, lambda q: first[q], table, basis, quants, lanes)
    pick_sends(table, send_row, sends, lanes)
    for copy in copies[FIRST_USED:]:
        copy.wait()


def second_kernel(
    state, first, table, jac, stiffness, padded, rotations, flux, slot,
    part, picked, lifting, turned_fold,
    stiffened, solved,
):
    quants, basis, lanes = state.shape
    turned = jnp.concatenate([stiffness[d].T for d in range(3)], axis=0)
    fold = fold_columns(turned)
    turned_fold[...] = fold.astype(F32)
    own_lifting = padded[...].T[0:basis]
    lifting[...] = near_lifting(own_lifting, rotations)
    picked[...] = pick_local(table[...], slot, 4 * lanes)

    def write(p, value):
        part[p] = value

    local_update(
        lambda p: state[p], lambda q: first[q], table, jac, fold, flux, own_lifting,
        stiffened, solved, write, basis, quants, lanes,
    )


def third_kernel(
    state, first, second, part, picked_local, dom_even, dom_odd, sub_even, sub_odd,
    jac, stiff_fold, padded, flux, slot, orient, cluster, lifting, send_row,
    middle, integral, picked, table, send_dom_even, send_dom_odd, send_sub_even, send_sub_odd,
    stiffened, solved,
):
    quants, basis, lanes = state.shape
    picked[...] = picked_local[...] + pick_received(
        (dom_even, dom_odd, sub_even, sub_odd), slot, 4 * lanes, lanes
    )
    near = near_lift(picked, flux, orient, lifting[...], solved, quants, lanes)
    fine = cluster[...] == 0
    for q in range(quants):
        value = jnp.where(fine, part[q] - near[:, q * lanes:(q + 1) * lanes], state[q])
        middle[q] = value
        integral[q] = value
    predict(
        stiff_fold[...].astype(BF16), jac, lambda q: middle[q], stiffened, integral, None,
        basis, quants, lanes,
    )
    project_table(
        padded, lambda q: jnp.where(fine, integral[q], second[q]), table, basis, quants, lanes
    )
    for q in range(quants):
        integral[q] = jnp.where(fine, integral[q], first[q] + second[q])
    pick_sends(
        table, send_row, (send_dom_even, send_dom_odd, send_sub_even, send_sub_odd), lanes
    )


def fourth_kernel(
    middle, integral, table_one, table_two, picked_one, jac, turned_fold, padded, flux, slot,
    cluster,
    part, picked,
    stiffened, solved, total_table,
):
    quants, basis, lanes = middle.shape
    own_lifting = padded[...].T[0:basis]
    coarse = jnp.concatenate([cluster[...] != 0] * 4, axis=1)
    total_table[...] = table_two[...] + jnp.where(coarse, table_one[...], 0.0)
    picked[...] = pick_local(table_two[...], slot, 4 * lanes) + jnp.where(
        coarse, picked_one[...], 0.0
    )

    def write(p, value):
        part[p] = value

    local_update(
        lambda p: middle[p], lambda q: integral[q], total_table, jac, turned_fold[...].astype(BF16), flux,
        own_lifting, stiffened, solved, write, basis, quants, lanes,
    )


def fifth_kernel(
    part, picked_local, dom_even, dom_odd, sub_even, sub_odd, flux, slot, orient, lifting,
    yield_stress,
    updated,
    solved, picked,
):
    quants, basis, lanes = part.shape
    picked[...] = picked_local[...] + pick_received(
        (dom_even, dom_odd, sub_even, sub_odd), slot, 4 * lanes, lanes
    )
    near = near_lift(picked, flux, orient, lifting[...], solved, quants, lanes)
    stepped = [part[q] - near[:, q * lanes:(q + 1) * lanes] for q in range(quants)]
    mean_part = (stepped[0] + stepped[1] + stepped[2]) / 3.0
    spread = [stepped[q] - mean_part for q in range(3)]
    normal = [item[0:1] for item in spread]
    shear = [stepped[q][0:1] for q in range(3, 6)]
    second_inv = 0.5 * (normal[0] ** 2 + normal[1] ** 2 + normal[2] ** 2) + (
        shear[0] ** 2 + shear[1] ** 2 + shear[2] ** 2
    )
    limit = yield_stress[...]
    scaling = limit / jnp.maximum(jnp.sqrt(second_inv), limit)
    for q in range(3):
        updated[q] = mean_part + scaling * spread[q]
    for q in range(3, 6):
        updated[q] = scaling * stepped[q]
    for q in range(6, quants):
        updated[q] = stepped[q]


def run(body, outs, scratch, *operands, space=pltpu.VMEM):
    vmem = pl.BlockSpec(memory_space=pltpu.VMEM)
    return pl.pallas_call(
        body,
        out_shape=[
            out if isinstance(out, jax.ShapeDtypeStruct) else jax.ShapeDtypeStruct(out, F32)
            for out in outs
        ],
        in_specs=[pl.BlockSpec(memory_space=space)] * len(operands),
        out_specs=[vmem] * len(outs),
        scratch_shapes=scratch,
        compiler_params=pltpu.CompilerParams(vmem_limit_bytes=32 * 1024 * 1024),
        name=body.__name__,
    )(*operands)


def exchange(sends):
    def swap(value, axis, first):
        size = lax.axis_size(axis)
        lower = range(first, size - 1, 2)
        return lax.ppermute(
            value, axis, [(i, i + 1) for i in lower] + [(i + 1, i) for i in lower]
        )

    dom_odd = swap(sends[1], "dom", 1)
    sub_odd = swap(sends[3], "sub", 1)
    sub_even = swap(sends[2], "sub", 0)
    dom_even = swap(sends[0], "dom", 0)
    return dom_even, dom_odd, sub_even, sub_odd


def on_device(
    modal_state,
    stiffness,
    jacobians,
    flux_solvers,
    projector,
    rotations,
    yield_stress,
    cluster,
    orient,
    neighbour_slot,
    send_map,
):
    basis, quants, lanes = modal_state.shape
    inputs = [
        jnp.transpose(modal_state, (1, 0, 2)),
        stiffness,
        jnp.transpose(projector, (1, 0, 2)),
        jnp.transpose(jacobians, (1, 2, 0, 3)),
        send_map.reshape(1, -1),
        jnp.transpose(flux_solvers, (0, 2, 3, 1, 4)),
        rotations,
        neighbour_slot,
        orient,
        cluster.reshape(1, lanes),
        yield_stress.reshape(1, lanes),
    ]
    inputs = [pltpu.with_memory_space_constraint(item, pltpu.HBM) for item in inputs]
    held = [jax.ShapeDtypeStruct(item.shape, item.dtype) for item in inputs]

    field = (quants, basis, lanes)
    table = (quants * ROWS, 4 * lanes)
    messages = [(groups[0][1] * ROWS, lanes) for groups in PACKING]
    flat = quants * lanes
    fold = (3 * basis, 3 * fold_step(basis))
    stiffened = pltpu.VMEM((3 * basis, flat), F32)
    two_stiffened = pltpu.VMEM((2, 3 * basis, flat), F32)
    own_solved = pltpu.VMEM((4 * ROWS, flat), F32)
    near_solved = pltpu.VMEM((2 * 3 * 4 * ROWS, flat), F32)

    outs = run(
        first_kernel,
        held + [field, field, table, (4 * ROWS, 128), fold] + messages,
        [two_stiffened, pltpu.SemaphoreType.DMA((INPUTS,))],
        *inputs, space=pl.ANY,
    )
    state, stiff, _, jac, send_row, flux, turns, slot, orient, cluster, limit = outs[:INPUTS]
    first, second, table_one, padded, stiff_fold, *sends = outs[INPUTS:]
    arrived = exchange(sends)
    part_one, local_one, lifting, turned_fold = run(
        second_kernel, [field, table, (basis, 3 * 4 * ROWS), fold],
        [stiffened, own_solved],
        state, first, table_one, jac, stiff, padded, turns, flux, slot,
    )
    middle, integral, picked_one, table_two, *sends = run(
        third_kernel, [field, field, table, table] + messages,
        [two_stiffened, near_solved],
        state, first, second, part_one, local_one, *arrived,
        jac, stiff_fold, padded, flux, slot, orient, cluster, lifting, send_row,
    )
    arrived = exchange(sends)
    part_two, local_two = run(
        fourth_kernel, [field, table],
        [stiffened, own_solved, pltpu.VMEM(table, F32)],
        middle, integral, table_one, table_two, picked_one, jac, turned_fold, padded, flux,
        slot, cluster,
    )
    updated, = run(
        fifth_kernel, [field], [near_solved, pltpu.VMEM(table, F32)],
        part_two, local_two, *arrived, flux, slot, orient, lifting, limit,
    )
    return jnp.transpose(updated, (1, 0, 2))


def solution(mesh):
    placed = (
        P(None, None, ("dom", "sub")),
        P(),
        P(None, None, None, ("dom", "sub")),
        P(None, None, None, None, ("dom", "sub")),
        P(),
        P(),
        P(("dom", "sub")),
        P(("dom", "sub")),
        P(None, ("dom", "sub")),
        P(None, ("dom", "sub")),
        P(("dom", "sub")),
    )
    return jax.shard_map(
        on_device,
        mesh=mesh,
        in_specs=placed,
        out_specs=P(None, None, ("dom", "sub")),
        check_vma=False,
    )
```

```python
import math

import jax
import jax.numpy as jnp
from jax import lax
from jax.experimental import pallas as pl
from jax.experimental.pallas import tpu as pltpu
from jax.sharding import PartitionSpec as P

ORDER = 6
SLOTS_DOM = 64
SLOTS_SUB = 32
ROWS = 24
GROUP = 3

F32 = jnp.float32
BF16 = jnp.bfloat16
EXACT = lax.Precision.HIGHEST

DOM_GROUPS = ((0, 5), (5, 4))
SUB_GROUPS = ((0, 3), (3, 2), (5, 2), (7, 2))
PACKING = (DOM_GROUPS, DOM_GROUPS, SUB_GROUPS, SUB_GROUPS)

SWAPS = (("dom", 0), ("dom", 1), ("sub", 0), ("sub", 1))
FIRST_TURNS = (3, 1, 2, 0)
SECOND_TURNS = (3, 0, 1, 2)


def by_swap(items, turns):
    return [items[turns.index(k)] for k in range(len(turns))]


INPUTS = 11
FIRST_USED = 5


def iota(shape, dim):
    return lax.broadcasted_iota(jnp.int32, shape, dim)


def dot(a, b):
    return jnp.dot(a, b, preferred_element_type=F32)


def exact_dot(a, b):
    return jnp.dot(a, b, precision=EXACT, preferred_element_type=F32)


def halves(value):
    high = value.astype(BF16)
    return high, (value - high.astype(F32)).astype(BF16)


def one_hot(index_row, first, count, modulus=None):
    number = iota((count, index_row.shape[1]), 0)
    if modulus is not None:
        number = lax.rem(number, modulus)
    return jnp.where(number + first == index_row, 1.0, 0.0).astype(BF16)


def fold_step(basis):
    return -(-basis // 16) * 16


def fold_rows(value):
    basis, lanes = value.shape
    rest = jnp.zeros((fold_step(basis) - basis, lanes), F32)
    value = jnp.concatenate([value, rest], axis=0)
    high, low = halves(value)
    return jnp.concatenate([high, high, low], axis=0)


def fold_columns(matrix):
    basis = matrix.shape[1]
    step = fold_step(basis)
    high, low = halves(matrix)
    row, column = iota((basis, 3 * step), 0), iota((basis, 3 * step), 1)
    outer = jnp.where((column == row) | (column == row + 2 * step), 1.0, 0.0).astype(BF16)
    inner = jnp.where(column == row + step, 1.0, 0.0).astype(BF16)
    return (dot(high, outer) + dot(low, inner)).astype(BF16)


def stiffen(stiff_fold, values, target, start, lanes):
    folded = jnp.concatenate([fold_rows(value) for value in values], axis=1)
    target[:, start * lanes:(start + len(values)) * lanes] = dot(stiff_fold, folded)


def mix_jacobians(stiffened, jac, basis, quants, lanes, take):
    for start in range(0, quants, GROUP):
        totals = [None] * GROUP
        for q in range(quants):
            for d in range(3):
                block = stiffened[d * basis:(d + 1) * basis, q * lanes:(q + 1) * lanes]
                for i in range(GROUP):
                    term = block * jac[q, start + i, d:d + 1, :]
                    totals[i] = term if totals[i] is None else totals[i] + term
        take(start, totals)


def mix_faces(table, flux, side, quants, lanes, write):
    for f in range(4):
        blocks = [
            table[q * ROWS:(q + 1) * ROWS, f * lanes:(f + 1) * lanes] for q in range(quants)
        ]
        for p in range(quants):
            total = blocks[0] * flux[side, 0, p, f:f + 1, :]
            for q in range(1, quants):
                total = total + blocks[q] * flux[side, q, p, f:f + 1, :]
            write(f, p, total)


def fill_projector(projector, padded):
    modes, faces, basis = projector.shape
    padded[...] = jnp.zeros(padded.shape, F32)
    for f in range(faces):
        for m in range(modes):
            padded[f * ROWS + m:f * ROWS + m + 1, 0:basis] = projector[m, f:f + 1, :]


def predict(stiff_fold, jac, state, stiffened, first, second, basis, quants, lanes):
    for start in range(0, quants, GROUP):
        values = [state(q) for q in range(start, start + GROUP)]
        stiffen(stiff_fold, values, stiffened.at[0], start, lanes)
    for order in range(1, ORDER):
        factor = 1.0 / math.factorial(order + 1)

        def take(start, totals):
            if order + 1 < ORDER:
                stiffen(stiff_fold, totals, stiffened.at[order % 2], start, lanes)
            for p, total in enumerate(totals, start):
                first[p] = first[p] + factor * total
                if second is not None:
                    second[p] = second[p] + (2.0 ** (order + 1) - 1.0) * factor * total

        mix_jacobians(stiffened.at[(order - 1) % 2], jac, basis, quants, lanes, take)


def project_table(padded, field, table, basis, quants, lanes):
    fold = fold_columns(padded[:, 0:basis])
    for start in range(0, quants, GROUP):
        values = [fold_rows(field(q)) for q in range(start, start + GROUP)]
        flat = dot(fold, jnp.concatenate(values, axis=1))
        for q in range(start, start + GROUP):
            for f in range(4):
                table[q * ROWS:(q + 1) * ROWS, f * lanes:(f + 1) * lanes] = flat[
                    f * ROWS:(f + 1) * ROWS, (q - start) * lanes:(q - start + 1) * lanes
                ]


def even_spot():
    return [lax.rem(lax.axis_index(axis), 2) == 0 for axis in ("dom", "sub")]


def pick_sends(table, send_row, outs, lanes):
    faces = table.shape[1]
    low = jnp.broadcast_to(send_row[:, 0:lanes], (8, lanes))
    lane = iota((8, lanes), 1)
    turned = pltpu.roll(low, SLOTS_DOM, 1)
    high = send_row[:, 2 * SLOTS_DOM:2 * SLOTS_DOM + 2 * SLOTS_SUB]
    spread = jnp.broadcast_to(jnp.concatenate([high, high], axis=1), (8, lanes))
    moved = pltpu.roll(spread, SLOTS_SUB, 1)
    left = lax.rem(lane, 2 * SLOTS_SUB) < SLOTS_SUB
    pieces = [
        jnp.where(lane < SLOTS_DOM, low, turned),
        jnp.where(lane < SLOTS_DOM, turned, low),
        jnp.where(left, spread, moved),
        jnp.where(left, moved, spread),
    ]
    even_dom, even_sub = even_spot()
    pieces = [
        jnp.where(even_dom, pieces[1], pieces[0]),
        jnp.where(even_dom, pieces[0], pieces[1]),
        jnp.where(even_sub, pieces[3], pieces[2]),
        jnp.where(even_sub, pieces[2], pieces[3]),
    ]
    index = jnp.concatenate([piece[0:1] for piece in pieces], axis=1)
    chosen = one_hot(index, 0, faces)
    upper, lower = halves(table[...])
    sent = dot(upper, chosen) + dot(lower, chosen)
    for k, (out, groups) in enumerate(zip(outs, PACKING)):
        width = lanes // len(groups)
        values = sent[:, k * lanes:(k + 1) * lanes]
        start, count = groups[0]
        packed = values[0:count * ROWS]
        least = min(count for _, count in groups) * ROWS
        spot = iota((least, lanes), 1)
        head = packed[0:least]
        for g, (start, _) in enumerate(groups):
            if g:
                head = jnp.where(
                    spot >= g * width, values[start * ROWS:start * ROWS + least], head
                )
        out[0:least] = head
        out[least:count * ROWS] = packed[least:]


def spread_received(arrived, groups, lanes):
    width = lanes // len(groups)
    parts = []
    for g, (_, count) in enumerate(groups):
        place = iota((count * ROWS, lanes), 1)
        mine = (place >= g * width) & (place < (g + 1) * width)
        parts.append(jnp.where(mine, arrived[0:count * ROWS], 0.0))
    return jnp.concatenate(parts, axis=0)


def pick_local(table, slot, faces):
    chosen = jnp.concatenate([one_hot(slot[f:f + 1], 0, faces) for f in range(4)], axis=1)
    upper, lower = halves(table)
    return dot(upper, chosen) + dot(lower, chosen)


def pick_received(arrived, slot, faces, lanes):
    spread = jnp.concatenate(
        [spread_received(item[...], groups, lanes) for item, groups in zip(arrived, PACKING)],
        axis=1,
    )
    even_dom, even_sub = even_spot()
    starts = (
        jnp.where(even_dom, faces + SLOTS_DOM, faces),
        jnp.where(even_dom, faces, faces + SLOTS_DOM),
        faces + 2 * SLOTS_DOM + jnp.where(even_sub, SLOTS_SUB, 0),
        faces + 2 * SLOTS_DOM + jnp.where(even_sub, 0, SLOTS_SUB),
    )
    widths = (SLOTS_DOM, SLOTS_DOM, SLOTS_SUB, SLOTS_SUB)
    chosen = jnp.concatenate(
        [
            jnp.concatenate(
                [one_hot(slot[f:f + 1], first, lanes, width) for f in range(4)], axis=1
            )
            for first, width in zip(starts, widths)
        ],
        axis=0,
    )
    upper, lower = halves(spread)
    return dot(upper, chosen) + dot(lower, chosen)


def lift(weights, high, low):
    upper, lower = halves(weights)
    return dot(upper, high) + dot(lower, high) + dot(upper, low)


def local_update(
    base, integral, table, jac, turned_fold, flux, lifting, stiffened, solved, write,
    basis, quants, lanes,
):
    for start in range(0, quants, GROUP):
        values = [integral(q) for q in range(start, start + GROUP)]
        stiffen(turned_fold, values, stiffened, start, lanes)

    def keep(f, p, total):
        solved[f * ROWS:(f + 1) * ROWS, p * lanes:(p + 1) * lanes] = total

    mix_faces(table, flux, 0, quants, lanes, keep)
    high, low = halves(solved[...])
    own = lift(lifting, high, low)

    def take(start, totals):
        for p, total in enumerate(totals, start):
            write(p, base(p) + total - own[:, p * lanes:(p + 1) * lanes])

    mix_jacobians(stiffened, jac, basis, quants, lanes, take)


def near_lift(picked, flux, orient, lifting, solved, quants, lanes):
    block = 4 * ROWS

    def keep(f, p, total):
        upper = total.astype(BF16).astype(F32)
        lower = total - upper
        for o in range(3):
            mine = orient[f:f + 1] == o
            row = o * block + f * ROWS
            solved[row:row + ROWS, p * lanes:(p + 1) * lanes] = jnp.where(mine, upper, 0.0)
            row += 3 * block
            solved[row:row + ROWS, p * lanes:(p + 1) * lanes] = jnp.where(mine, lower, 0.0)

    mix_faces(picked, flux, 1, quants, lanes, keep)
    depth = 3 * block
    return lift(lifting, solved[0:depth].astype(BF16), solved[depth:2 * depth].astype(BF16))


def near_lifting(own_lifting, rotations):
    count, modes, _ = rotations.shape
    block = 4 * ROWS
    row, column = iota((modes, count * block), 0), iota((modes, count * block), 1)
    turned = jnp.zeros((modes, count * block), F32)
    for o in range(count):
        spot = (lax.rem(column, ROWS) == row) & (lax.div(column, block) == o)
        turned = turned + exact_dot(rotations[o], jnp.where(spot, 1.0, 0.0))
    row, column = iota((block, modes), 0), iota((block, modes), 1)
    tall = exact_dot(jnp.where(lax.rem(row, ROWS) == column, 1.0, 0.0), turned)
    row, column = iota(tall.shape, 0), iota(tall.shape, 1)
    same = lax.div(row, ROWS) == lax.div(lax.rem(column, block), ROWS)
    return exact_dot(own_lifting, jnp.where(same, tall, 0.0))


def first_kernel(*refs):
    inputs, refs = refs[:INPUTS], refs[INPUTS:]
    held, refs = refs[:INPUTS], refs[INPUTS:]
    first, second, table, padded, stiff_fold, *sends, stiffened, arrivals = refs
    copies = [
        pltpu.make_async_copy(source, target, arrivals.at[k])
        for k, (source, target) in enumerate(zip(inputs, held))
    ]
    for copy in copies:
        copy.start()
    state, stiffness, projector, jac, send_row = held[:FIRST_USED]
    for copy in copies[:FIRST_USED]:
        copy.wait()
    quants, basis, lanes = state.shape
    for q in range(quants):
        value = state[q]
        first[q] = value
        second[q] = value
    fill_projector(projector, padded)
    stacked = jnp.concatenate([stiffness[d] for d in range(3)], axis=0)
    fold = fold_columns(stacked)
    stiff_fold[...] = fold.astype(F32)
    predict(
        fold, jac, lambda q: state[q], stiffened, first, second, basis, quants, lanes
    )
    project_table(padded, lambda q: first[q], table, basis, quants, lanes)
    pick_sends(table, send_row, by_swap(sends, FIRST_TURNS), lanes)
    for copy in copies[FIRST_USED:]:
        copy.wait()


def second_kernel(
    state, first, table, jac, stiffness, padded, rotations, flux, slot,
    part, picked, lifting, turned_fold,
    stiffened, solved,
):
    quants, basis, lanes = state.shape
    turned = jnp.concatenate([stiffness[d].T for d in range(3)], axis=0)
    fold = fold_columns(turned)
    turned_fold[...] = fold.astype(F32)
    own_lifting = padded[...].T[0:basis]
    lifting[...] = near_lifting(own_lifting, rotations)
    picked[...] = pick_local(table[...], slot, 4 * lanes)

    def write(p, value):
        part[p] = value

    local_update(
        lambda p: state[p], lambda q: first[q], table, jac, fold, flux, own_lifting,
        stiffened, solved, write, basis, quants, lanes,
    )


def third_kernel(
    state, first, second, part, picked_local, got_a, got_b, got_c, got_d,
    jac, stiff_fold, padded, flux, slot, orient, cluster, lifting, send_row,
    middle, integral, picked, table, send_a, send_b, send_c, send_d,
    stiffened, solved,
):
    quants, basis, lanes = state.shape
    picked[...] = picked_local[...] + pick_received(
        by_swap((got_a, got_b, got_c, got_d), FIRST_TURNS), slot, 4 * lanes, lanes
    )
    near = near_lift(picked, flux, orient, lifting[...], solved, quants, lanes)
    fine = cluster[...] == 0
    for q in range(quants):
        value = jnp.where(fine, part[q] - near[:, q * lanes:(q + 1) * lanes], state[q])
        middle[q] = value
        integral[q] = value
    predict(
        stiff_fold[...].astype(BF16), jac, lambda q: middle[q], stiffened, integral, None,
        basis, quants, lanes,
    )
    project_table(
        padded, lambda q: jnp.where(fine, integral[q], second[q]), table, basis, quants, lanes
    )
    for q in range(quants):
        integral[q] = jnp.where(fine, integral[q], first[q] + second[q])
    sends = by_swap((send_a, send_b, send_c, send_d), SECOND_TURNS)
    pick_sends(table, send_row, sends, lanes)


def fourth_kernel(
    middle, integral, table_one, table_two, picked_one, jac, turned_fold, padded, flux, slot,
    cluster,
    part, picked,
    stiffened, solved, total_table,
):
    quants, basis, lanes = middle.shape
    own_lifting = padded[...].T[0:basis]
    coarse = jnp.concatenate([cluster[...] != 0] * 4, axis=1)
    total_table[...] = table_two[...] + jnp.where(coarse, table_one[...], 0.0)
    picked[...] = pick_local(table_two[...], slot, 4 * lanes) + jnp.where(
        coarse, picked_one[...], 0.0
    )

    def write(p, value):
        part[p] = value

    local_update(
        lambda p: middle[p], lambda q: integral[q], total_table, jac, turned_fold[...].astype(BF16), flux,
        own_lifting, stiffened, solved, write, basis, quants, lanes,
    )


def fifth_kernel(
    part, picked_local, got_a, got_b, got_c, got_d, flux, slot, orient, lifting,
    yield_stress,
    updated,
    solved, picked,
):
    quants, basis, lanes = part.shape
    picked[...] = picked_local[...] + pick_received(
        by_swap((got_a, got_b, got_c, got_d), SECOND_TURNS), slot, 4 * lanes, lanes
    )
    near = near_lift(picked, flux, orient, lifting[...], solved, quants, lanes)
    stepped = [part[q] - near[:, q * lanes:(q + 1) * lanes] for q in range(quants)]
    mean_part = (stepped[0] + stepped[1] + stepped[2]) / 3.0
    spread = [stepped[q] - mean_part for q in range(3)]
    normal = [item[0:1] for item in spread]
    shear = [stepped[q][0:1] for q in range(3, 6)]
    second_inv = 0.5 * (normal[0] ** 2 + normal[1] ** 2 + normal[2] ** 2) + (
        shear[0] ** 2 + shear[1] ** 2 + shear[2] ** 2
    )
    limit = yield_stress[...]
    scaling = limit / jnp.maximum(jnp.sqrt(second_inv), limit)
    for q in range(3):
        updated[q] = mean_part + scaling * spread[q]
    for q in range(3, 6):
        updated[q] = scaling * stepped[q]
    for q in range(6, quants):
        updated[q] = stepped[q]


def run(body, outs, scratch, *operands, space=pltpu.VMEM):
    vmem = pl.BlockSpec(memory_space=pltpu.VMEM)
    return pl.pallas_call(
        body,
        out_shape=[
            out if isinstance(out, jax.ShapeDtypeStruct) else jax.ShapeDtypeStruct(out, F32)
            for out in outs
        ],
        in_specs=[pl.BlockSpec(memory_space=space)] * len(operands),
        out_specs=[vmem] * len(outs),
        scratch_shapes=scratch,
        compiler_params=pltpu.CompilerParams(vmem_limit_bytes=32 * 1024 * 1024),
        name=body.__name__,
    )(*operands)


def exchange(sends, turns):
    def swap(value, axis, first):
        lower = range(first, lax.axis_size(axis) - 1, 2)
        return lax.ppermute(
            value, axis, [(i, i + 1) for i in lower] + [(i + 1, i) for i in lower]
        )

    return [swap(value, *SWAPS[k]) for value, k in zip(sends, turns)]


def on_device(
    modal_state,
    stiffness,
    jacobians,
    flux_solvers,
    projector,
    rotations,
    yield_stress,
    cluster,
    orient,
    neighbour_slot,
    send_map,
):
    basis, quants, lanes = modal_state.shape
    inputs = [
        jnp.transpose(modal_state, (1, 0, 2)),
        stiffness,
        jnp.transpose(projector, (1, 0, 2)),
        jnp.transpose(jacobians, (1, 2, 0, 3)),
        send_map.reshape(1, -1),
        jnp.transpose(flux_solvers, (0, 2, 3, 1, 4)),
        rotations,
        neighbour_slot,
        orient,
        cluster.reshape(1, lanes),
        yield_stress.reshape(1, lanes),
    ]
    inputs = [pltpu.with_memory_space_constraint(item, pltpu.HBM) for item in inputs]
    held = [jax.ShapeDtypeStruct(item.shape, item.dtype) for item in inputs]

    field = (quants, basis, lanes)
    table = (quants * ROWS, 4 * lanes)
    messages = [(groups[0][1] * ROWS, lanes) for groups in PACKING]
    first_messages = [messages[k] for k in FIRST_TURNS]
    second_messages = [messages[k] for k in SECOND_TURNS]
    flat = quants * lanes
    fold = (3 * basis, 3 * fold_step(basis))
    stiffened = pltpu.VMEM((3 * basis, flat), F32)
    two_stiffened = pltpu.VMEM((2, 3 * basis, flat), F32)
    own_solved = pltpu.VMEM((4 * ROWS, flat), F32)
    near_solved = pltpu.VMEM((2 * 3 * 4 * ROWS, flat), F32)

    outs = run(
        first_kernel,
        held + [field, field, table, (4 * ROWS, 128), fold] + first_messages,
        [two_stiffened, pltpu.SemaphoreType.DMA((INPUTS,))],
        *inputs, space=pl.ANY,
    )
    state, stiff, _, jac, send_row, flux, turns, slot, orient, cluster, limit = outs[:INPUTS]
    first, second, table_one, padded, stiff_fold, *sends = outs[INPUTS:]
    arrived = exchange(sends, FIRST_TURNS)
    part_one, local_one, lifting, turned_fold = run(
        second_kernel, [field, table, (basis, 3 * 4 * ROWS), fold],
        [stiffened, own_solved],
        state, first, table_one, jac, stiff, padded, turns, flux, slot,
    )
    middle, integral, picked_one, table_two, *sends = run(
        third_kernel, [field, field, table, table] + second_messages,
        [two_stiffened, near_solved],
        state, first, second, part_one, local_one, *arrived,
        jac, stiff_fold, padded, flux, slot, orient, cluster, lifting, send_row,
    )
    arrived = exchange(sends, SECOND_TURNS)
    part_two, local_two = run(
        fourth_kernel, [field, table],
        [stiffened, own_solved, pltpu.VMEM(table, F32)],
        middle, integral, table_one, table_two, picked_one, jac, turned_fold, padded, flux,
        slot, cluster,
    )
    updated, = run(
        fifth_kernel, [field], [near_solved, pltpu.VMEM(table, F32)],
        part_two, local_two, *arrived, flux, slot, orient, lifting, limit,
    )
    return jnp.transpose(updated, (1, 0, 2))


def solution(mesh):
    placed = (
        P(None, None, ("dom", "sub")),
        P(),
        P(None, None, None, ("dom", "sub")),
        P(None, None, None, None, ("dom", "sub")),
        P(),
        P(),
        P(("dom", "sub")),
        P(("dom", "sub")),
        P(None, ("dom", "sub")),
        P(None, ("dom", "sub")),
        P(("dom", "sub")),
    )
    return jax.shard_map(
        on_device,
        mesh=mesh,
        in_specs=placed,
        out_specs=P(None, None, ("dom", "sub")),
        check_vma=False,
    )
```

```python
import math

import jax
import jax.numpy as jnp
from jax import lax
from jax.experimental import pallas as pl
from jax.experimental.pallas import tpu as pltpu
from jax.sharding import PartitionSpec as P

ORDER = 6
SLOTS_DOM = 64
SLOTS_SUB = 32
ROWS = 24
GROUP = 3

F32 = jnp.float32
BF16 = jnp.bfloat16
EXACT = lax.Precision.HIGHEST

DOM_GROUPS = ((0, 5), (5, 4))
SUB_GROUPS = ((0, 3), (3, 2), (5, 2), (7, 2))
PACKING = (DOM_GROUPS, DOM_GROUPS, SUB_GROUPS, SUB_GROUPS)

SUB_ROWS = SUB_GROUPS[0][1] * ROWS

FIRST_TURNS = (1, 0)
SECOND_TURNS = (1, 0)


INPUTS = 11
FIRST_USED = 5


def iota(shape, dim):
    return lax.broadcasted_iota(jnp.int32, shape, dim)


def dot(a, b):
    return jnp.dot(a, b, preferred_element_type=F32)


def exact_dot(a, b):
    return jnp.dot(a, b, precision=EXACT, preferred_element_type=F32)


def halves(value):
    high = value.astype(BF16)
    return high, (value - high.astype(F32)).astype(BF16)


def one_hot(index_row, first, count, modulus=None):
    number = iota((count, index_row.shape[1]), 0)
    if modulus is not None:
        number = lax.rem(number, modulus)
    return jnp.where(number + first == index_row, 1.0, 0.0).astype(BF16)


def fold_step(basis):
    return -(-basis // 16) * 16


def fold_rows(value):
    basis, lanes = value.shape
    rest = jnp.zeros((fold_step(basis) - basis, lanes), F32)
    value = jnp.concatenate([value, rest], axis=0)
    high, low = halves(value)
    return jnp.concatenate([high, high, low], axis=0)


def fold_columns(matrix):
    basis = matrix.shape[1]
    step = fold_step(basis)
    high, low = halves(matrix)
    row, column = iota((basis, 3 * step), 0), iota((basis, 3 * step), 1)
    outer = jnp.where((column == row) | (column == row + 2 * step), 1.0, 0.0).astype(BF16)
    inner = jnp.where(column == row + step, 1.0, 0.0).astype(BF16)
    return (dot(high, outer) + dot(low, inner)).astype(BF16)


def stiffen(stiff_fold, values, target, start, lanes):
    folded = jnp.concatenate([fold_rows(value) for value in values], axis=1)
    target[:, start * lanes:(start + len(values)) * lanes] = dot(stiff_fold, folded)


def mix_jacobians(stiffened, jac, basis, quants, lanes, take):
    for start in range(0, quants, GROUP):
        totals = [None] * GROUP
        for q in range(quants):
            for d in range(3):
                block = stiffened[d * basis:(d + 1) * basis, q * lanes:(q + 1) * lanes]
                for i in range(GROUP):
                    term = block * jac[q, start + i, d:d + 1, :]
                    totals[i] = term if totals[i] is None else totals[i] + term
        take(start, totals)


def mix_faces(table, flux, side, start, quants, lanes):
    totals = [[] for _ in range(GROUP)]
    for f in range(4):
        blocks = [
            table[q * ROWS:(q + 1) * ROWS, f * lanes:(f + 1) * lanes] for q in range(quants)
        ]
        for i in range(GROUP):
            total = blocks[0] * flux[side, 0, start + i, f:f + 1, :]
            for q in range(1, quants):
                total = total + blocks[q] * flux[side, q, start + i, f:f + 1, :]
            totals[i].append(total)
    return [jnp.concatenate(total, axis=0) for total in totals]


def fill_projector(projector, padded):
    modes, faces, basis = projector.shape
    padded[...] = jnp.zeros(padded.shape, F32)
    for f in range(faces):
        for m in range(modes):
            padded[f * ROWS + m:f * ROWS + m + 1, 0:basis] = projector[m, f:f + 1, :]


def predict(stiff_fold, jac, state, stiffened, first, second, basis, quants, lanes):
    for start in range(0, quants, GROUP):
        values = [state(q) for q in range(start, start + GROUP)]
        stiffen(stiff_fold, values, stiffened.at[0], start, lanes)
    for order in range(1, ORDER):
        factor = 1.0 / math.factorial(order + 1)

        def take(start, totals):
            if order + 1 < ORDER:
                stiffen(stiff_fold, totals, stiffened.at[order % 2], start, lanes)
            for p, total in enumerate(totals, start):
                first[p] = first[p] + factor * total
                if second is not None:
                    second[p] = second[p] + (2.0 ** (order + 1) - 1.0) * factor * total

        mix_jacobians(stiffened.at[(order - 1) % 2], jac, basis, quants, lanes, take)


def project_table(padded, field, table, basis, quants, lanes):
    fold = fold_columns(padded[:, 0:basis])
    for start in range(0, quants, GROUP):
        values = [fold_rows(field(q)) for q in range(start, start + GROUP)]
        flat = dot(fold, jnp.concatenate(values, axis=1))
        for q in range(start, start + GROUP):
            for f in range(4):
                table[q * ROWS:(q + 1) * ROWS, f * lanes:(f + 1) * lanes] = flat[
                    f * ROWS:(f + 1) * ROWS, (q - start) * lanes:(q - start + 1) * lanes
                ]


def even_spot():
    return [lax.rem(lax.axis_index(axis), 2) == 0 for axis in ("dom", "sub")]


def send_choice(send_row, faces, lanes):
    low = jnp.broadcast_to(send_row[:, 0:lanes], (8, lanes))
    lane = iota((8, lanes), 1)
    turned = pltpu.roll(low, SLOTS_DOM, 1)
    high = send_row[:, 2 * SLOTS_DOM:2 * SLOTS_DOM + 2 * SLOTS_SUB]
    spread = jnp.broadcast_to(jnp.concatenate([high, high], axis=1), (8, lanes))
    moved = pltpu.roll(spread, SLOTS_SUB, 1)
    left = lax.rem(lane, 2 * SLOTS_SUB) < SLOTS_SUB
    pieces = [
        jnp.where(lane < SLOTS_DOM, low, turned),
        jnp.where(lane < SLOTS_DOM, turned, low),
        jnp.where(left, spread, moved),
        jnp.where(left, moved, spread),
    ]
    even_dom, even_sub = even_spot()
    pieces = [
        jnp.where(even_dom, pieces[1], pieces[0]),
        jnp.where(even_dom, pieces[0], pieces[1]),
        jnp.where(even_sub, pieces[3], pieces[2]),
        jnp.where(even_sub, pieces[2], pieces[3]),
    ]
    return one_hot(jnp.concatenate([piece[0:1] for piece in pieces], axis=1), 0, faces)


def pick_sends(table, chosen, outs, turns, lanes):
    upper, lower = halves(table[...])
    sent = dot(upper, chosen) + dot(lower, chosen)
    for k, groups in enumerate(PACKING):
        out = outs[turns.index(k)] if k < 2 else outs[2]
        row = SUB_ROWS if k == 3 else 0
        width = lanes // len(groups)
        values = sent[:, k * lanes:(k + 1) * lanes]
        start, count = groups[0]
        packed = values[0:count * ROWS]
        least = min(count for _, count in groups) * ROWS
        spot = iota((least, lanes), 1)
        head = packed[0:least]
        for g, (start, _) in enumerate(groups):
            if g:
                head = jnp.where(
                    spot >= g * width, values[start * ROWS:start * ROWS + least], head
                )
        out[row:row + least] = head
        out[row + least:row + count * ROWS] = packed[least:]


def spread_received(arrived, groups, lanes):
    width = lanes // len(groups)
    parts = []
    for g, (_, count) in enumerate(groups):
        place = iota((count * ROWS, lanes), 1)
        mine = (place >= g * width) & (place < (g + 1) * width)
        parts.append(jnp.where(mine, arrived[0:count * ROWS], 0.0))
    return jnp.concatenate(parts, axis=0)


def pick_local(table, slot, faces):
    chosen = jnp.concatenate([one_hot(slot[f:f + 1], 0, faces) for f in range(4)], axis=1)
    upper, lower = halves(table)
    return dot(upper, chosen) + dot(lower, chosen)


def received_choice(slot, faces, lanes):
    even_dom, even_sub = even_spot()
    starts = (
        jnp.where(even_dom, faces + SLOTS_DOM, faces),
        jnp.where(even_dom, faces, faces + SLOTS_DOM),
        faces + 2 * SLOTS_DOM + jnp.where(even_sub, SLOTS_SUB, 0),
        faces + 2 * SLOTS_DOM + jnp.where(even_sub, 0, SLOTS_SUB),
    )
    widths = (SLOTS_DOM, SLOTS_DOM, SLOTS_SUB, SLOTS_SUB)
    return jnp.concatenate(
        [
            jnp.concatenate(
                [one_hot(slot[f:f + 1], first, lanes, width) for f in range(4)], axis=1
            )
            for first, width in zip(starts, widths)
        ],
        axis=0,
    )


def pick_received(doms, near, far, chosen, lanes):
    spot, count = lax.axis_index("sub"), lax.axis_size("sub")
    met = jnp.where(lax.rem(spot, 2) == 0, spot > 0, spot < count - 1)
    pieces = [
        doms[0][...],
        doms[1][...],
        near[0:SUB_ROWS],
        jnp.where(met, far[...], 0.0),
    ]
    spread = jnp.concatenate(
        [spread_received(item, groups, lanes) for item, groups in zip(pieces, PACKING)],
        axis=1,
    )
    upper, lower = halves(spread)
    return dot(upper, chosen) + dot(lower, chosen)


def lift(upper, lower, high, low):
    return dot(upper, high) + dot(lower, high) + dot(upper, low)


def local_update(
    base, integral, table, jac, turned_fold, flux, lifting, stiffened, part,
    basis, quants, lanes,
):
    for start in range(0, quants, GROUP):
        values = [integral(q) for q in range(start, start + GROUP)]
        stiffen(turned_fold, values, stiffened, start, lanes)
    upper, lower = halves(lifting)
    for start in range(0, quants, GROUP):
        solved = mix_faces(table, flux, 0, start, quants, lanes)
        high, low = halves(jnp.concatenate(solved, axis=1))
        own = lift(upper, lower, high, low)
        for i in range(GROUP):
            part[start + i] = base(start + i) - own[:, i * lanes:(i + 1) * lanes]

    def take(start, totals):
        for p, total in enumerate(totals, start):
            part[p] = part[p] + total

    mix_jacobians(stiffened, jac, basis, quants, lanes, take)


def near_lift(picked, flux, orient, lifting, quants, lanes, take):
    upper, lower = halves(lifting)
    masks = [
        jnp.concatenate(
            [
                jnp.broadcast_to(jnp.where(orient[f:f + 1] == o, 1.0, 0.0), (ROWS, lanes))
                for f in range(4)
            ],
            axis=0,
        ).astype(BF16)
        for o in range(3)
    ]
    for start in range(0, quants, GROUP):
        highs, lows = [], []
        for solved in mix_faces(picked, flux, 1, start, quants, lanes):
            high, low = halves(solved)
            highs.append(jnp.concatenate([high * mask for mask in masks], axis=0))
            lows.append(jnp.concatenate([low * mask for mask in masks], axis=0))
        near = lift(
            upper, lower, jnp.concatenate(highs, axis=1), jnp.concatenate(lows, axis=1)
        )
        for i in range(GROUP):
            take(start + i, near[:, i * lanes:(i + 1) * lanes])


def near_lifting(own_lifting, rotations):
    count, modes, _ = rotations.shape
    block = 4 * ROWS
    row, column = iota((modes, count * block), 0), iota((modes, count * block), 1)
    turned = jnp.zeros((modes, count * block), F32)
    for o in range(count):
        spot = (lax.rem(column, ROWS) == row) & (lax.div(column, block) == o)
        turned = turned + exact_dot(rotations[o], jnp.where(spot, 1.0, 0.0))
    row, column = iota((block, modes), 0), iota((block, modes), 1)
    tall = exact_dot(jnp.where(lax.rem(row, ROWS) == column, 1.0, 0.0), turned)
    row, column = iota(tall.shape, 0), iota(tall.shape, 1)
    same = lax.div(row, ROWS) == lax.div(lax.rem(column, block), ROWS)
    return exact_dot(own_lifting, jnp.where(same, tall, 0.0))


def first_kernel(*refs):
    inputs, refs = refs[:INPUTS], refs[INPUTS:]
    held, refs = refs[:INPUTS], refs[INPUTS:]
    first, second, table, padded, stiff_fold, choice, *sends, stiffened, arrivals = refs
    copies = [
        pltpu.make_async_copy(source, target, arrivals.at[k])
        for k, (source, target) in enumerate(zip(inputs, held))
    ]
    for copy in copies:
        copy.start()
    send_row, projector, stiffness, state, jac = held[:FIRST_USED]
    quants, basis, lanes = state.shape
    copies[0].wait()
    choice[...] = send_choice(send_row, 4 * lanes, lanes)
    copies[1].wait()
    fill_projector(projector, padded)
    copies[2].wait()
    fold = fold_columns(jnp.concatenate([stiffness[d] for d in range(3)], axis=0))
    stiff_fold[...] = fold.astype(F32)
    copies[3].wait()
    for q in range(quants):
        value = state[q]
        first[q] = value
        second[q] = value
    copies[4].wait()
    predict(
        fold, jac, lambda q: state[q], stiffened, first, second, basis, quants, lanes
    )
    project_table(padded, lambda q: first[q], table, basis, quants, lanes)
    pick_sends(table, choice[...], sends, FIRST_TURNS, lanes)
    for copy in copies[FIRST_USED:]:
        copy.wait()


def second_kernel(
    state, first, table, jac, stiffness, padded, rotations, flux, slot,
    part, picked, lifting, turned_fold, choice,
    stiffened,
):
    quants, basis, lanes = state.shape
    turned = jnp.concatenate([stiffness[d].T for d in range(3)], axis=0)
    fold = fold_columns(turned)
    turned_fold[...] = fold.astype(F32)
    own_lifting = padded[...].T[0:basis]
    lifting[...] = near_lifting(own_lifting, rotations)
    picked[...] = pick_local(table[...], slot, 4 * lanes)
    choice[...] = received_choice(slot, 4 * lanes, lanes)
    local_update(
        lambda p: state[p], lambda q: first[q], table, jac, fold, flux, own_lifting,
        stiffened, part, basis, quants, lanes,
    )


def third_kernel(
    state, first, second, part, picked_local, dom_a, dom_b, sub_near, sub_far,
    jac, stiff_fold, padded, flux, orient, cluster, lifting, received, choice,
    middle, integral, picked, table, *refs,
):
    *sends, stiffened = refs
    quants, basis, lanes = state.shape
    doms = [(dom_a, dom_b)[FIRST_TURNS.index(k)] for k in (0, 1)]
    picked[...] = picked_local[...] + pick_received(
        doms, sub_near, sub_far, received[...], lanes
    )
    fine = cluster[...] == 0

    def take(p, near):
        value = jnp.where(fine, part[p] - near, state[p])
        middle[p] = value
        integral[p] = value

    near_lift(picked, flux, orient, lifting[...], quants, lanes, take)
    predict(
        stiff_fold[...].astype(BF16), jac, lambda q: middle[q], stiffened, integral, None,
        basis, quants, lanes,
    )
    project_table(
        padded, lambda q: jnp.where(fine, integral[q], second[q]), table, basis, quants, lanes
    )
    for q in range(quants):
        integral[q] = jnp.where(fine, integral[q], first[q] + second[q])
    pick_sends(table, choice[...], sends, SECOND_TURNS, lanes)


def fourth_kernel(
    middle, integral, table_one, table_two, picked_one, jac, turned_fold, padded, flux, slot,
    cluster,
    part, picked,
    stiffened, total_table,
):
    quants, basis, lanes = middle.shape
    own_lifting = padded[...].T[0:basis]
    coarse = jnp.concatenate([cluster[...] != 0] * 4, axis=1)
    total_table[...] = table_two[...] + jnp.where(coarse, table_one[...], 0.0)
    picked[...] = pick_local(table_two[...], slot, 4 * lanes) + jnp.where(
        coarse, picked_one[...], 0.0
    )
    local_update(
        lambda p: middle[p], lambda q: integral[q], total_table, jac,
        turned_fold[...].astype(BF16), flux, own_lifting,
        stiffened, part, basis, quants, lanes,
    )


def fifth_kernel(
    part, picked_local, dom_a, dom_b, sub_near, sub_far, flux, orient, lifting, received,
    yield_stress,
    updated,
    picked,
):
    quants, basis, lanes = part.shape
    doms = [(dom_a, dom_b)[SECOND_TURNS.index(k)] for k in (0, 1)]
    picked[...] = picked_local[...] + pick_received(
        doms, sub_near, sub_far, received[...], lanes
    )
    stepped = [None] * quants

    def take(p, near):
        stepped[p] = part[p] - near

    near_lift(picked, flux, orient, lifting[...], quants, lanes, take)
    mean_part = (stepped[0] + stepped[1] + stepped[2]) / 3.0
    spread = [stepped[q] - mean_part for q in range(3)]
    normal = [item[0:1] for item in spread]
    shear = [stepped[q][0:1] for q in range(3, 6)]
    second_inv = 0.5 * (normal[0] ** 2 + normal[1] ** 2 + normal[2] ** 2) + (
        shear[0] ** 2 + shear[1] ** 2 + shear[2] ** 2
    )
    limit = yield_stress[...]
    scaling = limit / jnp.maximum(jnp.sqrt(second_inv), limit)
    for q in range(3):
        updated[q] = mean_part + scaling * spread[q]
    for q in range(3, 6):
        updated[q] = scaling * stepped[q]
    for q in range(6, quants):
        updated[q] = stepped[q]


def run(body, outs, scratch, *operands, space=pltpu.VMEM):
    vmem = pl.BlockSpec(memory_space=pltpu.VMEM)
    return pl.pallas_call(
        body,
        out_shape=[
            out if isinstance(out, jax.ShapeDtypeStruct) else jax.ShapeDtypeStruct(out, F32)
            for out in outs
        ],
        in_specs=[pl.BlockSpec(memory_space=space)] * len(operands),
        out_specs=[vmem] * len(outs),
        scratch_shapes=scratch,
        compiler_params=pltpu.CompilerParams(vmem_limit_bytes=32 * 1024 * 1024),
        name=body.__name__,
    )(*operands)


def hand_on(near, dom, onward):
    onward[...] = near[SUB_ROWS:2 * SUB_ROWS]


def exchange(sends, turns):
    def swap(value, axis, first):
        lower = range(first, lax.axis_size(axis) - 1, 2)
        return lax.ppermute(
            value, axis, [(i, i + 1) for i in lower] + [(i + 1, i) for i in lower]
        )

    count = lax.axis_size("sub")
    near = swap(sends[2], "sub", 0)
    doms = [swap(value, "dom", first) for value, first in zip(sends, turns)]
    kept, = run(hand_on, [(SUB_ROWS, near.shape[1])], [], near, doms[turns.index(0)])
    onward = [(i, (i + (2 if i % 2 == 0 else -2)) % count) for i in range(count)]
    return doms + [near, lax.ppermute(kept, "sub", onward)]


def on_device(
    modal_state,
    stiffness,
    jacobians,
    flux_solvers,
    projector,
    rotations,
    yield_stress,
    cluster,
    orient,
    neighbour_slot,
    send_map,
):
    basis, quants, lanes = modal_state.shape
    inputs = [
        send_map.reshape(1, -1),
        jnp.transpose(projector, (1, 0, 2)),
        stiffness,
        jnp.transpose(modal_state, (1, 0, 2)),
        jnp.transpose(jacobians, (1, 2, 0, 3)),
        jnp.transpose(flux_solvers, (0, 2, 3, 1, 4)),
        rotations,
        neighbour_slot,
        orient,
        cluster.reshape(1, lanes),
        yield_stress.reshape(1, lanes),
    ]
    inputs = [pltpu.with_memory_space_constraint(item, pltpu.HBM) for item in inputs]
    held = [jax.ShapeDtypeStruct(item.shape, item.dtype) for item in inputs]

    field = (quants, basis, lanes)
    table = (quants * ROWS, 4 * lanes)
    dom_message = (DOM_GROUPS[0][1] * ROWS, lanes)
    messages = [dom_message, dom_message, (2 * SUB_ROWS, lanes)]
    choice = jax.ShapeDtypeStruct((4 * lanes, 4 * lanes), BF16)
    flat = quants * lanes
    fold = (3 * basis, 3 * fold_step(basis))
    stiffened = pltpu.VMEM((3 * basis, flat), F32)
    two_stiffened = pltpu.VMEM((2, 3 * basis, flat), F32)

    outs = run(
        first_kernel,
        held + [field, field, table, (4 * ROWS, 128), fold, choice] + messages,
        [two_stiffened, pltpu.SemaphoreType.DMA((INPUTS,))],
        *inputs, space=pl.ANY,
    )
    _, _, stiff, state, jac, flux, turns, slot, orient, cluster, limit = outs[:INPUTS]
    first, second, table_one, padded, stiff_fold, sending, *sends = outs[INPUTS:]
    arrived = exchange(sends, FIRST_TURNS)
    part_one, local_one, lifting, turned_fold, received = run(
        second_kernel, [field, table, (basis, 3 * 4 * ROWS), fold, choice], [stiffened],
        state, first, table_one, jac, stiff, padded, turns, flux, slot,
    )
    middle, integral, picked_one, table_two, *sends = run(
        third_kernel, [field, field, table, table] + messages, [two_stiffened],
        state, first, second, part_one, local_one, *arrived,
        jac, stiff_fold, padded, flux, orient, cluster, lifting, received, sending,
    )
    arrived = exchange(sends, SECOND_TURNS)
    part_two, local_two = run(
        fourth_kernel, [field, table], [stiffened, pltpu.VMEM(table, F32)],
        middle, integral, table_one, table_two, picked_one, jac, turned_fold, padded, flux,
        slot, cluster,
    )
    updated, = run(
        fifth_kernel, [field], [pltpu.VMEM(table, F32)],
        part_two, local_two, *arrived, flux, orient, lifting, received, limit,
    )
    return jnp.transpose(updated, (1, 0, 2))


def solution(mesh):
    placed = (
        P(None, None, ("dom", "sub")),
        P(),
        P(None, None, None, ("dom", "sub")),
        P(None, None, None, None, ("dom", "sub")),
        P(),
        P(),
        P(("dom", "sub")),
        P(("dom", "sub")),
        P(None, ("dom", "sub")),
        P(None, ("dom", "sub")),
        P(("dom", "sub")),
    )
    return jax.shard_map(
        on_device,
        mesh=mesh,
        in_specs=placed,
        out_specs=P(None, None, ("dom", "sub")),
        check_vma=False,
    )
```

```python
import math

import jax
import jax.numpy as jnp
from jax import lax
from jax.experimental import pallas as pl
from jax.experimental.pallas import tpu as pltpu
from jax.sharding import PartitionSpec as P

ORDER = 6
SLOTS_DOM = 64
SLOTS_SUB = 32
ROWS = 24
GROUP = 3

F32 = jnp.float32
BF16 = jnp.bfloat16
EXACT = lax.Precision.HIGHEST

DOM_GROUPS = ((0, 5), (5, 4))
SUB_GROUPS = ((0, 3), (3, 2), (5, 2), (7, 2))
PACKING = (DOM_GROUPS, DOM_GROUPS, SUB_GROUPS, SUB_GROUPS)

SUB_ROWS = SUB_GROUPS[0][1] * ROWS

FIRST_TURNS = (1, 0)
SECOND_TURNS = (0, 1)


INPUTS = 11
FIRST_USED = 5


def iota(shape, dim):
    return lax.broadcasted_iota(jnp.int32, shape, dim)


def dot(a, b):
    return jnp.dot(a, b, preferred_element_type=F32)


def exact_dot(a, b):
    return jnp.dot(a, b, precision=EXACT, preferred_element_type=F32)


def halves(value):
    high = value.astype(BF16)
    return high, (value - high.astype(F32)).astype(BF16)


def one_hot(index_row, first, count, modulus=None):
    number = iota((count, index_row.shape[1]), 0)
    if modulus is not None:
        number = lax.rem(number, modulus)
    return jnp.where(number + first == index_row, 1.0, 0.0).astype(BF16)


def stack_rows(value):
    high = value.astype(BF16).astype(F32)
    return jnp.concatenate([high, value - high], axis=0).astype(BF16)


def gather(table, chosen):
    rows = table.shape[0]
    both = dot(stack_rows(table), chosen)
    return both[0:rows] + both[rows:2 * rows]


def fold_step(basis):
    return -(-basis // 16) * 16


def fold_rows(value):
    basis, lanes = value.shape
    rest = jnp.zeros((fold_step(basis) - basis, lanes), F32)
    value = jnp.concatenate([value, rest], axis=0)
    high, low = halves(value)
    return jnp.concatenate([high, high, low], axis=0)


def fold_columns(matrix):
    basis = matrix.shape[1]
    step = fold_step(basis)
    high, low = halves(matrix)
    row, column = iota((basis, 3 * step), 0), iota((basis, 3 * step), 1)
    outer = jnp.where((column == row) | (column == row + 2 * step), 1.0, 0.0).astype(BF16)
    inner = jnp.where(column == row + step, 1.0, 0.0).astype(BF16)
    return (dot(high, outer) + dot(low, inner)).astype(BF16)


def stiffen(stiff_fold, values, target, start, lanes):
    folded = jnp.concatenate([fold_rows(value) for value in values], axis=1)
    target[:, start * lanes:(start + len(values)) * lanes] = dot(stiff_fold, folded)


def mix_jacobians(stiffened, jac, basis, quants, lanes, take):
    for start in range(0, quants, GROUP):
        totals = [None] * GROUP
        for q in range(quants):
            for d in range(3):
                block = stiffened[d * basis:(d + 1) * basis, q * lanes:(q + 1) * lanes]
                for i in range(GROUP):
                    term = block * jac[q, start + i, d:d + 1, :]
                    totals[i] = term if totals[i] is None else totals[i] + term
        take(start, totals)


def mix_faces(table, flux, side, start, quants, lanes):
    totals = [[] for _ in range(GROUP)]
    for f in range(4):
        blocks = [
            table[q * ROWS:(q + 1) * ROWS, f * lanes:(f + 1) * lanes] for q in range(quants)
        ]
        for i in range(GROUP):
            total = blocks[0] * flux[side, 0, start + i, f:f + 1, :]
            for q in range(1, quants):
                total = total + blocks[q] * flux[side, q, start + i, f:f + 1, :]
            totals[i].append(total)
    return [jnp.concatenate(total, axis=0) for total in totals]


def fill_projector(projector, padded):
    modes, faces, basis = projector.shape
    padded[...] = jnp.zeros(padded.shape, F32)
    for f in range(faces):
        for m in range(modes):
            padded[f * ROWS + m:f * ROWS + m + 1, 0:basis] = projector[m, f:f + 1, :]


def predict(stiff_fold, jac, state, stiffened, first, second, basis, quants, lanes):
    for start in range(0, quants, GROUP):
        values = [state(q) for q in range(start, start + GROUP)]
        stiffen(stiff_fold, values, stiffened.at[0], start, lanes)
    for order in range(1, ORDER):
        factor = 1.0 / math.factorial(order + 1)

        def take(start, totals):
            if order + 1 < ORDER:
                stiffen(stiff_fold, totals, stiffened.at[order % 2], start, lanes)
            for p, total in enumerate(totals, start):
                first[p] = first[p] + factor * total
                if second is not None:
                    second[p] = second[p] + (2.0 ** (order + 1) - 1.0) * factor * total

        mix_jacobians(stiffened.at[(order - 1) % 2], jac, basis, quants, lanes, take)


def project_table(padded, field, table, basis, quants, lanes):
    fold = fold_columns(padded[:, 0:basis])
    for start in range(0, quants, GROUP):
        values = [fold_rows(field(q)) for q in range(start, start + GROUP)]
        flat = dot(fold, jnp.concatenate(values, axis=1))
        for q in range(start, start + GROUP):
            for f in range(4):
                table[q * ROWS:(q + 1) * ROWS, f * lanes:(f + 1) * lanes] = flat[
                    f * ROWS:(f + 1) * ROWS, (q - start) * lanes:(q - start + 1) * lanes
                ]


def even_spot():
    return [lax.rem(lax.axis_index(axis), 2) == 0 for axis in ("dom", "sub")]


def send_choice(send_row, faces, lanes):
    low = jnp.broadcast_to(send_row[:, 0:lanes], (8, lanes))
    lane = iota((8, lanes), 1)
    turned = pltpu.roll(low, SLOTS_DOM, 1)
    high = send_row[:, 2 * SLOTS_DOM:2 * SLOTS_DOM + 2 * SLOTS_SUB]
    spread = jnp.broadcast_to(jnp.concatenate([high, high], axis=1), (8, lanes))
    moved = pltpu.roll(spread, SLOTS_SUB, 1)
    left = lax.rem(lane, 2 * SLOTS_SUB) < SLOTS_SUB
    pieces = [
        jnp.where(lane < SLOTS_DOM, low, turned),
        jnp.where(lane < SLOTS_DOM, turned, low),
        jnp.where(left, spread, moved),
        jnp.where(left, moved, spread),
    ]
    even_dom, even_sub = even_spot()
    pieces = [
        jnp.where(even_dom, pieces[1], pieces[0]),
        jnp.where(even_dom, pieces[0], pieces[1]),
        jnp.where(even_sub, pieces[3], pieces[2]),
        jnp.where(even_sub, pieces[2], pieces[3]),
    ]
    return one_hot(jnp.concatenate([piece[0:1] for piece in pieces], axis=1), 0, faces)


def pick_sends(table, chosen, outs, turns, lanes):
    sent = gather(table[...], chosen)
    for k, groups in enumerate(PACKING):
        out = outs[turns.index(k)] if k < 2 else outs[2]
        row = SUB_ROWS if k == 3 else 0
        width = lanes // len(groups)
        values = sent[:, k * lanes:(k + 1) * lanes]
        start, count = groups[0]
        packed = values[0:count * ROWS]
        least = min(count for _, count in groups) * ROWS
        spot = iota((least, lanes), 1)
        head = packed[0:least]
        for g, (start, _) in enumerate(groups):
            if g:
                head = jnp.where(
                    spot >= g * width, values[start * ROWS:start * ROWS + least], head
                )
        out[row:row + least] = head
        out[row + least:row + count * ROWS] = packed[least:]


def spread_received(arrived, groups, lanes):
    width = lanes // len(groups)
    parts = []
    for g, (_, count) in enumerate(groups):
        place = iota((count * ROWS, lanes), 1)
        mine = (place >= g * width) & (place < (g + 1) * width)
        parts.append(jnp.where(mine, arrived[0:count * ROWS], 0.0))
    return jnp.concatenate(parts, axis=0)


def pick_local(table, slot, faces):
    chosen = jnp.concatenate([one_hot(slot[f:f + 1], 0, faces) for f in range(4)], axis=1)
    return gather(table, chosen)


def received_choice(slot, faces, lanes):
    even_dom, even_sub = even_spot()
    starts = (
        jnp.where(even_dom, faces + SLOTS_DOM, faces),
        jnp.where(even_dom, faces, faces + SLOTS_DOM),
        faces + 2 * SLOTS_DOM + jnp.where(even_sub, SLOTS_SUB, 0),
        faces + 2 * SLOTS_DOM + jnp.where(even_sub, 0, SLOTS_SUB),
    )
    widths = (SLOTS_DOM, SLOTS_DOM, SLOTS_SUB, SLOTS_SUB)
    return jnp.concatenate(
        [
            jnp.concatenate(
                [one_hot(slot[f:f + 1], first, lanes, width) for f in range(4)], axis=1
            )
            for first, width in zip(starts, widths)
        ],
        axis=0,
    )


def pick_received(doms, near, far, chosen, lanes):
    spot, count = lax.axis_index("sub"), lax.axis_size("sub")
    met = jnp.where(lax.rem(spot, 2) == 0, spot > 0, spot < count - 1)
    pieces = [
        doms[0][...],
        doms[1][...],
        near[0:SUB_ROWS],
        jnp.where(met, far[...], 0.0),
    ]
    spread = jnp.concatenate(
        [spread_received(item, groups, lanes) for item, groups in zip(pieces, PACKING)],
        axis=1,
    )
    return gather(spread, chosen)


def lift_weights(lifting):
    basis, depth = lifting.shape
    rest = jnp.zeros((fold_step(basis) - basis, depth), F32)
    high, low = halves(jnp.concatenate([lifting, rest], axis=0))
    return jnp.concatenate([high, low], axis=0)


def lift(weights, high, low, basis):
    step = fold_step(basis)
    both = dot(weights, high)
    return both[0:basis] + both[step:step + basis] + dot(weights[0:step], low)[0:basis]


def local_update(
    base, integral, table, jac, turned_fold, flux, lifting, stiffened, part,
    basis, quants, lanes,
):
    for start in range(0, quants, GROUP):
        values = [integral(q) for q in range(start, start + GROUP)]
        stiffen(turned_fold, values, stiffened, start, lanes)
    weights = lift_weights(lifting)
    for start in range(0, quants, GROUP):
        solved = mix_faces(table, flux, 0, start, quants, lanes)
        high, low = halves(jnp.concatenate(solved, axis=1))
        own = lift(weights, high, low, basis)
        for i in range(GROUP):
            part[start + i] = base(start + i) - own[:, i * lanes:(i + 1) * lanes]

    def take(start, totals):
        for p, total in enumerate(totals, start):
            part[p] = part[p] + total

    mix_jacobians(stiffened, jac, basis, quants, lanes, take)


def near_lift(picked, flux, orient, lifting, quants, lanes, take):
    weights = lift_weights(lifting)
    masks = [
        jnp.concatenate(
            [
                jnp.broadcast_to(jnp.where(orient[f:f + 1] == o, 1.0, 0.0), (ROWS, lanes))
                for f in range(4)
            ],
            axis=0,
        ).astype(BF16)
        for o in range(3)
    ]
    for start in range(0, quants, GROUP):
        highs, lows = [], []
        for solved in mix_faces(picked, flux, 1, start, quants, lanes):
            high, low = halves(solved)
            highs.append(jnp.concatenate([high * mask for mask in masks], axis=0))
            lows.append(jnp.concatenate([low * mask for mask in masks], axis=0))
        near = lift(
            weights, jnp.concatenate(highs, axis=1), jnp.concatenate(lows, axis=1),
            lifting.shape[0],
        )
        for i in range(GROUP):
            take(start + i, near[:, i * lanes:(i + 1) * lanes])


def near_lifting(own_lifting, rotations):
    count, modes, _ = rotations.shape
    block = 4 * ROWS
    row, column = iota((modes, count * block), 0), iota((modes, count * block), 1)
    turned = jnp.zeros((modes, count * block), F32)
    for o in range(count):
        spot = (lax.rem(column, ROWS) == row) & (lax.div(column, block) == o)
        turned = turned + exact_dot(rotations[o], jnp.where(spot, 1.0, 0.0))
    row, column = iota((block, modes), 0), iota((block, modes), 1)
    tall = exact_dot(jnp.where(lax.rem(row, ROWS) == column, 1.0, 0.0), turned)
    row, column = iota(tall.shape, 0), iota(tall.shape, 1)
    same = lax.div(row, ROWS) == lax.div(lax.rem(column, block), ROWS)
    return exact_dot(own_lifting, jnp.where(same, tall, 0.0))


def first_kernel(*refs):
    inputs, refs = refs[:INPUTS], refs[INPUTS:]
    held, refs = refs[:INPUTS], refs[INPUTS:]
    first, second, table, padded, stiff_fold, choice, *sends, stiffened, arrivals = refs
    copies = [
        pltpu.make_async_copy(source, target, arrivals.at[k])
        for k, (source, target) in enumerate(zip(inputs, held))
    ]
    for copy in copies:
        copy.start()
    send_row, projector, stiffness, state, jac = held[:FIRST_USED]
    quants, basis, lanes = state.shape
    copies[0].wait()
    choice[...] = send_choice(send_row, 4 * lanes, lanes)
    copies[1].wait()
    fill_projector(projector, padded)
    copies[2].wait()
    fold = fold_columns(jnp.concatenate([stiffness[d] for d in range(3)], axis=0))
    stiff_fold[...] = fold.astype(F32)
    copies[3].wait()
    for q in range(quants):
        value = state[q]
        first[q] = value
        second[q] = value
    copies[4].wait()
    predict(
        fold, jac, lambda q: state[q], stiffened, first, second, basis, quants, lanes
    )
    project_table(padded, lambda q: first[q], table, basis, quants, lanes)
    pick_sends(table, choice[...], sends, FIRST_TURNS, lanes)
    for copy in copies[FIRST_USED:]:
        copy.wait()


def second_kernel(
    state, first, table, jac, stiffness, padded, rotations, flux, slot,
    part, picked, lifting, turned_fold, choice,
    stiffened,
):
    quants, basis, lanes = state.shape
    turned = jnp.concatenate([stiffness[d].T for d in range(3)], axis=0)
    fold = fold_columns(turned)
    turned_fold[...] = fold.astype(F32)
    own_lifting = padded[...].T[0:basis]
    lifting[...] = near_lifting(own_lifting, rotations)
    picked[...] = pick_local(table[...], slot, 4 * lanes)
    choice[...] = received_choice(slot, 4 * lanes, lanes)
    local_update(
        lambda p: state[p], lambda q: first[q], table, jac, fold, flux, own_lifting,
        stiffened, part, basis, quants, lanes,
    )


def third_kernel(
    state, first, second, part, picked_local, dom_a, dom_b, sub_near, sub_far,
    jac, stiff_fold, padded, flux, orient, cluster, lifting, received, choice,
    middle, integral, picked, table, *refs,
):
    *sends, stiffened = refs
    quants, basis, lanes = state.shape
    doms = [(dom_a, dom_b)[FIRST_TURNS.index(k)] for k in (0, 1)]
    picked[...] = picked_local[...] + pick_received(
        doms, sub_near, sub_far, received[...], lanes
    )
    fine = cluster[...] == 0

    def take(p, near):
        value = jnp.where(fine, part[p] - near, state[p])
        middle[p] = value
        integral[p] = value

    near_lift(picked, flux, orient, lifting[...], quants, lanes, take)
    predict(
        stiff_fold[...].astype(BF16), jac, lambda q: middle[q], stiffened, integral, None,
        basis, quants, lanes,
    )
    project_table(
        padded, lambda q: jnp.where(fine, integral[q], second[q]), table, basis, quants, lanes
    )
    for q in range(quants):
        integral[q] = jnp.where(fine, integral[q], first[q] + second[q])
    pick_sends(table, choice[...], sends, SECOND_TURNS, lanes)


def fourth_kernel(
    middle, integral, table_one, table_two, picked_one, jac, turned_fold, padded, flux, slot,
    cluster,
    part, picked,
    stiffened, total_table,
):
    quants, basis, lanes = middle.shape
    own_lifting = padded[...].T[0:basis]
    coarse = jnp.concatenate([cluster[...] != 0] * 4, axis=1)
    total_table[...] = table_two[...] + jnp.where(coarse, table_one[...], 0.0)
    picked[...] = pick_local(table_two[...], slot, 4 * lanes) + jnp.where(
        coarse, picked_one[...], 0.0
    )
    local_update(
        lambda p: middle[p], lambda q: integral[q], total_table, jac,
        turned_fold[...].astype(BF16), flux, own_lifting,
        stiffened, part, basis, quants, lanes,
    )


def fifth_kernel(
    part, picked_local, dom_a, dom_b, sub_near, sub_far, flux, orient, lifting, received,
    yield_stress,
    updated,
    picked,
):
    quants, basis, lanes = part.shape
    doms = [(dom_a, dom_b)[SECOND_TURNS.index(k)] for k in (0, 1)]
    picked[...] = picked_local[...] + pick_received(
        doms, sub_near, sub_far, received[...], lanes
    )
    stepped = [None] * quants

    def take(p, near):
        stepped[p] = part[p] - near

    near_lift(picked, flux, orient, lifting[...], quants, lanes, take)
    mean_part = (stepped[0] + stepped[1] + stepped[2]) / 3.0
    spread = [stepped[q] - mean_part for q in range(3)]
    normal = [item[0:1] for item in spread]
    shear = [stepped[q][0:1] for q in range(3, 6)]
    second_inv = 0.5 * (normal[0] ** 2 + normal[1] ** 2 + normal[2] ** 2) + (
        shear[0] ** 2 + shear[1] ** 2 + shear[2] ** 2
    )
    limit = yield_stress[...]
    scaling = limit / jnp.maximum(jnp.sqrt(second_inv), limit)
    for q in range(3):
        updated[q] = mean_part + scaling * spread[q]
    for q in range(3, 6):
        updated[q] = scaling * stepped[q]
    for q in range(6, quants):
        updated[q] = stepped[q]


def run(body, outs, scratch, *operands, space=pltpu.VMEM):
    vmem = pl.BlockSpec(memory_space=pltpu.VMEM)
    return pl.pallas_call(
        body,
        out_shape=[
            out if isinstance(out, jax.ShapeDtypeStruct) else jax.ShapeDtypeStruct(out, F32)
            for out in outs
        ],
        in_specs=[pl.BlockSpec(memory_space=space)] * len(operands),
        out_specs=[vmem] * len(outs),
        scratch_shapes=scratch,
        compiler_params=pltpu.CompilerParams(vmem_limit_bytes=32 * 1024 * 1024),
        name=body.__name__,
    )(*operands)


def hand_on(near, dom, onward):
    onward[...] = near[SUB_ROWS:2 * SUB_ROWS]


def exchange(sends, turns):
    def swap(value, axis, first):
        lower = range(first, lax.axis_size(axis) - 1, 2)
        return lax.ppermute(
            value, axis, [(i, i + 1) for i in lower] + [(i + 1, i) for i in lower]
        )

    count = lax.axis_size("sub")
    near = swap(sends[2], "sub", 0)
    doms = [swap(value, "dom", first) for value, first in zip(sends, turns)]
    kept, = run(hand_on, [(SUB_ROWS, near.shape[1])], [], near, doms[0])
    onward = [(i, (i + (2 if i % 2 == 0 else -2)) % count) for i in range(count)]
    return doms + [near, lax.ppermute(kept, "sub", onward)]


def on_device(
    modal_state,
    stiffness,
    jacobians,
    flux_solvers,
    projector,
    rotations,
    yield_stress,
    cluster,
    orient,
    neighbour_slot,
    send_map,
):
    basis, quants, lanes = modal_state.shape
    inputs = [
        send_map.reshape(1, -1),
        jnp.transpose(projector, (1, 0, 2)),
        stiffness,
        jnp.transpose(modal_state, (1, 0, 2)),
        jnp.transpose(jacobians, (1, 2, 0, 3)),
        jnp.transpose(flux_solvers, (0, 2, 3, 1, 4)),
        rotations,
        neighbour_slot,
        orient,
        cluster.reshape(1, lanes),
        yield_stress.reshape(1, lanes),
    ]
    inputs = [pltpu.with_memory_space_constraint(item, pltpu.HBM) for item in inputs]
    held = [jax.ShapeDtypeStruct(item.shape, item.dtype) for item in inputs]

    field = (quants, basis, lanes)
    table = (quants * ROWS, 4 * lanes)
    dom_message = (DOM_GROUPS[0][1] * ROWS, lanes)
    messages = [dom_message, dom_message, (2 * SUB_ROWS, lanes)]
    choice = jax.ShapeDtypeStruct((4 * lanes, 4 * lanes), BF16)
    flat = quants * lanes
    fold = (3 * basis, 3 * fold_step(basis))
    stiffened = pltpu.VMEM((3 * basis, flat), F32)
    two_stiffened = pltpu.VMEM((2, 3 * basis, flat), F32)

    outs = run(
        first_kernel,
        held + [field, field, table, (4 * ROWS, 128), fold, choice] + messages,
        [two_stiffened, pltpu.SemaphoreType.DMA((INPUTS,))],
        *inputs, space=pl.ANY,
    )
    _, _, stiff, state, jac, flux, turns, slot, orient, cluster, limit = outs[:INPUTS]
    first, second, table_one, padded, stiff_fold, sending, *sends = outs[INPUTS:]
    arrived = exchange(sends, FIRST_TURNS)
    part_one, local_one, lifting, turned_fold, received = run(
        second_kernel, [field, table, (basis, 3 * 4 * ROWS), fold, choice], [stiffened],
        state, first, table_one, jac, stiff, padded, turns, flux, slot,
    )
    middle, integral, picked_one, table_two, *sends = run(
        third_kernel, [field, field, table, table] + messages, [two_stiffened],
        state, first, second, part_one, local_one, *arrived,
        jac, stiff_fold, padded, flux, orient, cluster, lifting, received, sending,
    )
    arrived = exchange(sends, SECOND_TURNS)
    part_two, local_two = run(
        fourth_kernel, [field, table], [stiffened, pltpu.VMEM(table, F32)],
        middle, integral, table_one, table_two, picked_one, jac, turned_fold, padded, flux,
        slot, cluster,
    )
    updated, = run(
        fifth_kernel, [field], [pltpu.VMEM(table, F32)],
        part_two, local_two, *arrived, flux, orient, lifting, received, limit,
    )
    return jnp.transpose(updated, (1, 0, 2))


def solution(mesh):
    placed = (
        P(None, None, ("dom", "sub")),
        P(),
        P(None, None, None, ("dom", "sub")),
        P(None, None, None, None, ("dom", "sub")),
        P(),
        P(),
        P(("dom", "sub")),
        P(("dom", "sub")),
        P(None, ("dom", "sub")),
        P(None, ("dom", "sub")),
        P(("dom", "sub")),
    )
    return jax.shard_map(
        on_device,
        mesh=mesh,
        in_specs=placed,
        out_specs=P(None, None, ("dom", "sub")),
        check_vma=False,
    )
```

```python
import math

import jax
import jax.numpy as jnp
from jax import lax
from jax.experimental import pallas as pl
from jax.experimental.pallas import tpu as pltpu
from jax.sharding import PartitionSpec as P

ORDER = 6
SLOTS_DOM = 64
SLOTS_SUB = 32
ROWS = 24
GROUP = 3

F32 = jnp.float32
BF16 = jnp.bfloat16
EXACT = lax.Precision.HIGHEST

PACKING = (2, 2, 4, 4)

FIRST_TURNS = (1, 0)
SECOND_TURNS = (1, 0)


INPUTS = 11
FIRST_USED = 5


def iota(shape, dim):
    return lax.broadcasted_iota(jnp.int32, shape, dim)


def dot(a, b):
    return jnp.dot(a, b, preferred_element_type=F32)


def exact_dot(a, b):
    return jnp.dot(a, b, precision=EXACT, preferred_element_type=F32)


def halves(value):
    high = value.astype(BF16)
    return high, (value - high.astype(F32)).astype(BF16)


def one_hot(index_row, first, count, modulus=None):
    number = iota((count, index_row.shape[1]), 0)
    if modulus is not None:
        number = lax.rem(number, modulus)
    return jnp.where(number + first == index_row, 1.0, 0.0).astype(BF16)


def stack_rows(value):
    high = value.astype(BF16).astype(F32)
    return jnp.concatenate([high, value - high], axis=0).astype(BF16)


def gather(table, chosen):
    rows = table.shape[0]
    both = dot(stack_rows(table), chosen)
    return both[0:rows] + both[rows:2 * rows]


def fold_step(basis):
    return -(-basis // 16) * 16


def fold_rows(value):
    basis, lanes = value.shape
    rest = jnp.zeros((fold_step(basis) - basis, lanes), F32)
    value = jnp.concatenate([value, rest], axis=0)
    high, low = halves(value)
    return jnp.concatenate([high, high, low], axis=0)


def fold_columns(matrix):
    basis = matrix.shape[1]
    step = fold_step(basis)
    high, low = halves(matrix)
    row, column = iota((basis, 3 * step), 0), iota((basis, 3 * step), 1)
    outer = jnp.where((column == row) | (column == row + 2 * step), 1.0, 0.0).astype(BF16)
    inner = jnp.where(column == row + step, 1.0, 0.0).astype(BF16)
    return (dot(high, outer) + dot(low, inner)).astype(BF16)


def stiffen(stiff_fold, values, target, start, lanes):
    folded = jnp.concatenate([fold_rows(value) for value in values], axis=1)
    target[:, start * lanes:(start + len(values)) * lanes] = dot(stiff_fold, folded)


def mix_jacobians(stiffened, jac, basis, quants, lanes, take):
    for start in range(0, quants, GROUP):
        totals = [None] * GROUP
        for q in range(quants):
            for d in range(3):
                block = stiffened[d * basis:(d + 1) * basis, q * lanes:(q + 1) * lanes]
                for i in range(GROUP):
                    term = block * jac[q, start + i, d:d + 1, :]
                    totals[i] = term if totals[i] is None else totals[i] + term
        take(start, totals)


def mix_faces(table, flux, side, start, quants, lanes):
    totals = [[] for _ in range(GROUP)]
    for f in range(4):
        blocks = [
            table[q * ROWS:(q + 1) * ROWS, f * lanes:(f + 1) * lanes] for q in range(quants)
        ]
        for i in range(GROUP):
            total = blocks[0] * flux[side, 0, start + i, f:f + 1, :]
            for q in range(1, quants):
                total = total + blocks[q] * flux[side, q, start + i, f:f + 1, :]
            totals[i].append(total)
    return [jnp.concatenate(total, axis=0) for total in totals]


def fill_projector(projector, padded):
    modes, faces, basis = projector.shape
    padded[...] = jnp.zeros(padded.shape, F32)
    for f in range(faces):
        for m in range(modes):
            padded[f * ROWS + m:f * ROWS + m + 1, 0:basis] = projector[m, f:f + 1, :]


def predict(stiff_fold, jac, state, stiffened, first, second, basis, quants, lanes):
    for start in range(0, quants, GROUP):
        values = [state(q) for q in range(start, start + GROUP)]
        stiffen(stiff_fold, values, stiffened.at[0], start, lanes)
    for order in range(1, ORDER):
        factor = 1.0 / math.factorial(order + 1)

        def take(start, totals):
            if order + 1 < ORDER:
                stiffen(stiff_fold, totals, stiffened.at[order % 2], start, lanes)
            for p, total in enumerate(totals, start):
                first[p] = first[p] + factor * total
                if second is not None:
                    second[p] = second[p] + (2.0 ** (order + 1) - 1.0) * factor * total

        mix_jacobians(stiffened.at[(order - 1) % 2], jac, basis, quants, lanes, take)


def dense_rows(quants, modes):
    return -(-quants * modes // 32) * 32


def project_table(padded, field, table, dense, basis, quants, lanes, modes):
    fold = fold_columns(padded[:, 0:basis])
    last = dense.shape[0]
    dense[last - 8:last] = jnp.zeros((8, dense.shape[1]), F32)
    for start in range(0, quants, GROUP):
        values = [fold_rows(field(q)) for q in range(start, start + GROUP)]
        flat = dot(fold, jnp.concatenate(values, axis=1))
        for q in range(start, start + GROUP):
            for f in range(4):
                block = flat[f * ROWS:(f + 1) * ROWS, (q - start) * lanes:(q - start + 1) * lanes]
                columns = slice(f * lanes, (f + 1) * lanes)
                table[q * ROWS:(q + 1) * ROWS, columns] = block
                dense[q * modes:(q + 1) * modes, columns] = block[0:modes]


def even_spot():
    return [lax.rem(lax.axis_index(axis), 2) == 0 for axis in ("dom", "sub")]


def send_choice(send_row, faces, lanes):
    low = jnp.broadcast_to(send_row[:, 0:lanes], (8, lanes))
    lane = iota((8, lanes), 1)
    turned = pltpu.roll(low, SLOTS_DOM, 1)
    high = send_row[:, 2 * SLOTS_DOM:2 * SLOTS_DOM + 2 * SLOTS_SUB]
    spread = jnp.broadcast_to(jnp.concatenate([high, high], axis=1), (8, lanes))
    moved = pltpu.roll(spread, SLOTS_SUB, 1)
    left = lax.rem(lane, 2 * SLOTS_SUB) < SLOTS_SUB
    pieces = [
        jnp.where(lane < SLOTS_DOM, low, turned),
        jnp.where(lane < SLOTS_DOM, turned, low),
        jnp.where(left, spread, moved),
        jnp.where(left, moved, spread),
    ]
    even_dom, even_sub = even_spot()
    pieces = [
        jnp.where(even_dom, pieces[1], pieces[0]),
        jnp.where(even_dom, pieces[0], pieces[1]),
        jnp.where(even_sub, pieces[3], pieces[2]),
        jnp.where(even_sub, pieces[2], pieces[3]),
    ]
    return one_hot(jnp.concatenate([piece[0:1] for piece in pieces], axis=1), 0, faces)


def pick_sends(dense, chosen, outs, turns, lanes):
    sent = gather(dense[...], chosen)
    for k, count in enumerate(PACKING):
        out = outs[turns.index(k)] if k < 2 else outs[2]
        rows = sent.shape[0] // count
        values = sent[:, k * lanes:(k + 1) * lanes]
        spot = iota((rows, lanes), 1)
        packed = values[0:rows]
        for g in range(1, count):
            packed = jnp.where(
                spot >= g * (lanes // count), values[g * rows:(g + 1) * rows], packed
            )
        row = rows if k == 3 else 0
        out[row:row + rows] = packed


def spread_received(arrived, count, lanes):
    width = lanes // count
    place = iota(arrived.shape, 1)
    return jnp.concatenate(
        [
            jnp.where((place >= g * width) & (place < (g + 1) * width), arrived, 0.0)
            for g in range(count)
        ],
        axis=0,
    )


def pick_local(table, slot, faces):
    chosen = jnp.concatenate([one_hot(slot[f:f + 1], 0, faces) for f in range(4)], axis=1)
    return gather(table, chosen)


def received_choice(slot, faces, lanes):
    even_dom, even_sub = even_spot()
    starts = (
        jnp.where(even_dom, faces + SLOTS_DOM, faces),
        jnp.where(even_dom, faces, faces + SLOTS_DOM),
        faces + 2 * SLOTS_DOM + jnp.where(even_sub, SLOTS_SUB, 0),
        faces + 2 * SLOTS_DOM + jnp.where(even_sub, 0, SLOTS_SUB),
    )
    widths = (SLOTS_DOM, SLOTS_DOM, SLOTS_SUB, SLOTS_SUB)
    return jnp.concatenate(
        [
            jnp.concatenate(
                [one_hot(slot[f:f + 1], first, lanes, width) for f in range(4)], axis=1
            )
            for first, width in zip(starts, widths)
        ],
        axis=0,
    )


def pick_received(picked, local, doms, near, far, chosen, dense, quants, modes, lanes):
    spot, count = lax.axis_index("sub"), lax.axis_size("sub")
    met = jnp.where(lax.rem(spot, 2) == 0, spot > 0, spot < count - 1)
    half = near.shape[0] // 2
    pieces = [
        doms[0][...],
        doms[1][...],
        near[0:half],
        jnp.where(met, far[half:2 * half], 0.0),
    ]
    spread = jnp.concatenate(
        [spread_received(item, groups, lanes) for item, groups in zip(pieces, PACKING)],
        axis=1,
    )
    dense[...] = gather(spread, chosen)
    for q in range(quants):
        row = q * ROWS
        picked[row + modes:row + ROWS] = local[row + modes:row + ROWS]
        picked[row:row + modes] = local[row:row + modes] + dense[q * modes:(q + 1) * modes]


def lift_weights(lifting):
    basis, depth = lifting.shape
    rest = jnp.zeros((fold_step(basis) - basis, depth), F32)
    high, low = halves(jnp.concatenate([lifting, rest], axis=0))
    return jnp.concatenate([high, low], axis=0)


def lift(weights, high, low, basis):
    step = fold_step(basis)
    both = dot(weights, high)
    return both[0:basis] + both[step:step + basis] + dot(weights[0:step], low)[0:basis]


def local_update(
    base, integral, table, jac, turned_fold, flux, lifting, stiffened, part,
    basis, quants, lanes,
):
    for start in range(0, quants, GROUP):
        values = [integral(q) for q in range(start, start + GROUP)]
        stiffen(turned_fold, values, stiffened, start, lanes)
    weights = lift_weights(lifting)
    for start in range(0, quants, GROUP):
        solved = mix_faces(table, flux, 0, start, quants, lanes)
        high, low = halves(jnp.concatenate(solved, axis=1))
        own = lift(weights, high, low, basis)
        for i in range(GROUP):
            part[start + i] = base(start + i) - own[:, i * lanes:(i + 1) * lanes]

    def take(start, totals):
        for p, total in enumerate(totals, start):
            part[p] = part[p] + total

    mix_jacobians(stiffened, jac, basis, quants, lanes, take)


def near_lift(picked, flux, orient, lifting, quants, lanes, take):
    weights = lift_weights(lifting)
    masks = [
        jnp.concatenate(
            [
                jnp.broadcast_to(jnp.where(orient[f:f + 1] == o, 1.0, 0.0), (ROWS, lanes))
                for f in range(4)
            ],
            axis=0,
        ).astype(BF16)
        for o in range(3)
    ]
    for start in range(0, quants, GROUP):
        highs, lows = [], []
        for solved in mix_faces(picked, flux, 1, start, quants, lanes):
            high, low = halves(solved)
            highs.append(jnp.concatenate([high * mask for mask in masks], axis=0))
            lows.append(jnp.concatenate([low * mask for mask in masks], axis=0))
        near = lift(
            weights, jnp.concatenate(highs, axis=1), jnp.concatenate(lows, axis=1),
            lifting.shape[0],
        )
        for i in range(GROUP):
            take(start + i, near[:, i * lanes:(i + 1) * lanes])


def near_lifting(own_lifting, rotations):
    count, modes, _ = rotations.shape
    block = 4 * ROWS
    row, column = iota((modes, count * block), 0), iota((modes, count * block), 1)
    turned = jnp.zeros((modes, count * block), F32)
    for o in range(count):
        spot = (lax.rem(column, ROWS) == row) & (lax.div(column, block) == o)
        turned = turned + exact_dot(rotations[o], jnp.where(spot, 1.0, 0.0))
    row, column = iota((block, modes), 0), iota((block, modes), 1)
    tall = exact_dot(jnp.where(lax.rem(row, ROWS) == column, 1.0, 0.0), turned)
    row, column = iota(tall.shape, 0), iota(tall.shape, 1)
    same = lax.div(row, ROWS) == lax.div(lax.rem(column, block), ROWS)
    return exact_dot(own_lifting, jnp.where(same, tall, 0.0))


def first_kernel(*refs):
    inputs, refs = refs[:INPUTS], refs[INPUTS:]
    held, refs = refs[:INPUTS], refs[INPUTS:]
    first, second, table, padded, stiff_fold, choice, *sends, stiffened, dense, arrivals = refs
    copies = [
        pltpu.make_async_copy(source, target, arrivals.at[k])
        for k, (source, target) in enumerate(zip(inputs, held))
    ]
    for copy in copies:
        copy.start()
    send_row, projector, stiffness, state, jac = held[:FIRST_USED]
    quants, basis, lanes = state.shape
    modes = projector.shape[0]
    copies[0].wait()
    choice[...] = send_choice(send_row, 4 * lanes, lanes)
    copies[1].wait()
    fill_projector(projector, padded)
    copies[2].wait()
    fold = fold_columns(jnp.concatenate([stiffness[d] for d in range(3)], axis=0))
    stiff_fold[...] = fold.astype(F32)
    copies[3].wait()
    for q in range(quants):
        value = state[q]
        first[q] = value
        second[q] = value
    copies[4].wait()
    predict(
        fold, jac, lambda q: state[q], stiffened, first, second, basis, quants, lanes
    )
    project_table(
        padded, lambda q: first[q], table, dense, basis, quants, lanes, modes
    )
    pick_sends(dense, choice[...], sends, FIRST_TURNS, lanes)
    for copy in copies[FIRST_USED:]:
        copy.wait()


def second_kernel(
    state, first, table, jac, stiffness, padded, rotations, flux, slot,
    part, picked, lifting, turned_fold, choice,
    stiffened,
):
    quants, basis, lanes = state.shape
    turned = jnp.concatenate([stiffness[d].T for d in range(3)], axis=0)
    fold = fold_columns(turned)
    turned_fold[...] = fold.astype(F32)
    own_lifting = padded[...].T[0:basis]
    lifting[...] = near_lifting(own_lifting, rotations)
    picked[...] = pick_local(table[...], slot, 4 * lanes)
    choice[...] = received_choice(slot, 4 * lanes, lanes)
    local_update(
        lambda p: state[p], lambda q: first[q], table, jac, fold, flux, own_lifting,
        stiffened, part, basis, quants, lanes,
    )


def third_kernel(
    state, first, second, part, picked_local, sub_far, dom_a, dom_b, sub_near,
    rotations, jac, stiff_fold, padded, flux, orient, cluster, lifting, received, choice,
    middle, integral, picked, table, *refs,
):
    *sends, stiffened, dense = refs
    quants, basis, lanes = state.shape
    modes = rotations.shape[1]
    doms = [(dom_a, dom_b)[FIRST_TURNS.index(k)] for k in (0, 1)]
    pick_received(
        picked, picked_local, doms, sub_near, sub_far, received[...], dense,
        quants, modes, lanes,
    )
    fine = cluster[...] == 0

    def take(p, near):
        value = jnp.where(fine, part[p] - near, state[p])
        middle[p] = value
        integral[p] = value

    near_lift(picked, flux, orient, lifting[...], quants, lanes, take)
    predict(
        stiff_fold[...].astype(BF16), jac, lambda q: middle[q], stiffened, integral, None,
        basis, quants, lanes,
    )
    project_table(
        padded, lambda q: jnp.where(fine, integral[q], second[q]), table, dense,
        basis, quants, lanes, modes,
    )
    for q in range(quants):
        integral[q] = jnp.where(fine, integral[q], first[q] + second[q])
    pick_sends(dense, choice[...], sends, SECOND_TURNS, lanes)


def fourth_kernel(
    middle, integral, table_one, table_two, picked_one, jac, turned_fold, padded, flux, slot,
    cluster,
    part, picked,
    stiffened, total_table,
):
    quants, basis, lanes = middle.shape
    own_lifting = padded[...].T[0:basis]
    coarse = jnp.concatenate([cluster[...] != 0] * 4, axis=1)
    total_table[...] = table_two[...] + jnp.where(coarse, table_one[...], 0.0)
    picked[...] = pick_local(table_two[...], slot, 4 * lanes) + jnp.where(
        coarse, picked_one[...], 0.0
    )
    local_update(
        lambda p: middle[p], lambda q: integral[q], total_table, jac,
        turned_fold[...].astype(BF16), flux, own_lifting,
        stiffened, part, basis, quants, lanes,
    )


def fifth_kernel(
    part, picked_local, sub_far, dom_a, dom_b, sub_near, rotations, flux, orient, lifting,
    received, yield_stress,
    updated,
    picked, dense,
):
    quants, basis, lanes = part.shape
    modes = rotations.shape[1]
    doms = [(dom_a, dom_b)[SECOND_TURNS.index(k)] for k in (0, 1)]
    pick_received(
        picked, picked_local, doms, sub_near, sub_far, received[...], dense,
        quants, modes, lanes,
    )
    stepped = [None] * quants

    def take(p, near):
        stepped[p] = part[p] - near

    near_lift(picked, flux, orient, lifting[...], quants, lanes, take)
    mean_part = (stepped[0] + stepped[1] + stepped[2]) / 3.0
    spread = [stepped[q] - mean_part for q in range(3)]
    normal = [item[0:1] for item in spread]
    shear = [stepped[q][0:1] for q in range(3, 6)]
    second_inv = 0.5 * (normal[0] ** 2 + normal[1] ** 2 + normal[2] ** 2) + (
        shear[0] ** 2 + shear[1] ** 2 + shear[2] ** 2
    )
    limit = yield_stress[...]
    scaling = limit / jnp.maximum(jnp.sqrt(second_inv), limit)
    for q in range(3):
        updated[q] = mean_part + scaling * spread[q]
    for q in range(3, 6):
        updated[q] = scaling * stepped[q]
    for q in range(6, quants):
        updated[q] = stepped[q]


def run(body, outs, scratch, *operands, space=pltpu.VMEM):
    vmem = pl.BlockSpec(memory_space=pltpu.VMEM)
    return pl.pallas_call(
        body,
        out_shape=[
            out if isinstance(out, jax.ShapeDtypeStruct) else jax.ShapeDtypeStruct(out, F32)
            for out in outs
        ],
        in_specs=[pl.BlockSpec(memory_space=space)] * len(operands),
        out_specs=[vmem] * len(outs),
        scratch_shapes=scratch,
        compiler_params=pltpu.CompilerParams(vmem_limit_bytes=32 * 1024 * 1024),
        name=body.__name__,
    )(*operands)


def hand_on(near, dom, onward):
    onward[...] = near[...]


def exchange(sends, turns):
    def swap(value, axis, first):
        lower = range(first, lax.axis_size(axis) - 1, 2)
        return lax.ppermute(
            value, axis, [(i, i + 1) for i in lower] + [(i + 1, i) for i in lower]
        )

    count = lax.axis_size("sub")
    near = swap(sends[2], "sub", 0)
    dom_even = swap(sends[turns.index(0)], "dom", 0)
    kept, = run(hand_on, [near.shape], [], near, dom_even)
    onward = [(i, (i + (2 if i % 2 == 0 else -2)) % count) for i in range(count)]
    far = lax.ppermute(kept, "sub", onward)
    dom_odd = swap(sends[turns.index(1)], "dom", 1)
    doms = (dom_even, dom_odd)
    return [far] + [doms[k] for k in turns] + [near]


def on_device(
    modal_state,
    stiffness,
    jacobians,
    flux_solvers,
    projector,
    rotations,
    yield_stress,
    cluster,
    orient,
    neighbour_slot,
    send_map,
):
    basis, quants, lanes = modal_state.shape
    inputs = [
        send_map.reshape(1, -1),
        jnp.transpose(projector, (1, 0, 2)),
        stiffness,
        jnp.transpose(modal_state, (1, 0, 2)),
        jnp.transpose(jacobians, (1, 2, 0, 3)),
        jnp.transpose(flux_solvers, (0, 2, 3, 1, 4)),
        rotations,
        neighbour_slot,
        orient,
        cluster.reshape(1, lanes),
        yield_stress.reshape(1, lanes),
    ]
    inputs = [pltpu.with_memory_space_constraint(item, pltpu.HBM) for item in inputs]
    held = [jax.ShapeDtypeStruct(item.shape, item.dtype) for item in inputs]

    field = (quants, basis, lanes)
    table = (quants * ROWS, 4 * lanes)
    rows = dense_rows(quants, projector.shape[1])
    dense = pltpu.VMEM((rows, 4 * lanes), F32)
    messages = [(rows // 2, lanes)] * 3
    choice = jax.ShapeDtypeStruct((4 * lanes, 4 * lanes), BF16)
    flat = quants * lanes
    fold = (3 * basis, 3 * fold_step(basis))
    stiffened = pltpu.VMEM((3 * basis, flat), F32)
    two_stiffened = pltpu.VMEM((2, 3 * basis, flat), F32)

    outs = run(
        first_kernel,
        held + [field, field, table, (4 * ROWS, 128), fold, choice] + messages,
        [two_stiffened, dense, pltpu.SemaphoreType.DMA((INPUTS,))],
        *inputs, space=pl.ANY,
    )
    _, _, stiff, state, jac, flux, turns, slot, orient, cluster, limit = outs[:INPUTS]
    first, second, table_one, padded, stiff_fold, sending, *sends = outs[INPUTS:]
    arrived = exchange(sends, FIRST_TURNS)
    part_one, local_one, lifting, turned_fold, received = run(
        second_kernel, [field, table, (basis, 3 * 4 * ROWS), fold, choice], [stiffened],
        state, first, table_one, jac, stiff, padded, turns, flux, slot,
    )
    middle, integral, picked_one, table_two, *sends = run(
        third_kernel, [field, field, table, table] + messages, [two_stiffened, dense],
        state, first, second, part_one, local_one, *arrived, turns,
        jac, stiff_fold, padded, flux, orient, cluster, lifting, received, sending,
    )
    arrived = exchange(sends, SECOND_TURNS)
    part_two, local_two = run(
        fourth_kernel, [field, table], [stiffened, pltpu.VMEM(table, F32)],
        middle, integral, table_one, table_two, picked_one, jac, turned_fold, padded, flux,
        slot, cluster,
    )
    updated, = run(
        fifth_kernel, [field], [pltpu.VMEM(table, F32), dense],
        part_two, local_two, *arrived, turns, flux, orient, lifting, received, limit,
    )
    return jnp.transpose(updated, (1, 0, 2))


def solution(mesh):
    placed = (
        P(None, None, ("dom", "sub")),
        P(),
        P(None, None, None, ("dom", "sub")),
        P(None, None, None, None, ("dom", "sub")),
        P(),
        P(),
        P(("dom", "sub")),
        P(("dom", "sub")),
        P(None, ("dom", "sub")),
        P(None, ("dom", "sub")),
        P(("dom", "sub")),
    )
    return jax.shard_map(
        on_device,
        mesh=mesh,
        in_specs=placed,
        out_specs=P(None, None, ("dom", "sub")),
        check_vma=False,
    )
```

```python
import math

import jax
import jax.numpy as jnp
from jax import lax
from jax.experimental import pallas as pl
from jax.experimental.pallas import tpu as pltpu
from jax.sharding import PartitionSpec as P

ORDER = 6
SLOTS_DOM = 64
SLOTS_SUB = 32
ROWS = 24
GROUP = 3

F32 = jnp.float32
BF16 = jnp.bfloat16
EXACT = lax.Precision.HIGHEST

PACKING = (2, 2, 4, 4)

FIRST_TURNS = (1, 0)
SECOND_TURNS = (1, 0)


INPUT_PARTS = (1, 1, 3, 3, 3, 1, 1, 1, 1, 1, 1)
INPUTS = 11
FIRST_USED = 5


def iota(shape, dim):
    return lax.broadcasted_iota(jnp.int32, shape, dim)


def dot(a, b):
    return jnp.dot(a, b, preferred_element_type=F32)


def exact_dot(a, b):
    return jnp.dot(a, b, precision=EXACT, preferred_element_type=F32)


def halves(value):
    high = value.astype(BF16)
    return high, (value - high.astype(F32)).astype(BF16)


def one_hot(index_row, first, count, modulus=None):
    number = iota((count, index_row.shape[1]), 0)
    if modulus is not None:
        number = lax.rem(number, modulus)
    return jnp.where(number + first == index_row, 1.0, 0.0).astype(BF16)


def stack_rows(value):
    high = value.astype(BF16).astype(F32)
    return jnp.concatenate([high, value - high], axis=0).astype(BF16)


def gather(table, chosen):
    rows = table.shape[0]
    both = dot(stack_rows(table), chosen)
    return both[0:rows] + both[rows:2 * rows]


def fold_step(basis):
    return -(-basis // 16) * 16


def fold_rows(value):
    basis, lanes = value.shape
    rest = jnp.zeros((fold_step(basis) - basis, lanes), F32)
    value = jnp.concatenate([value, rest], axis=0)
    high, low = halves(value)
    return jnp.concatenate([high, high, low], axis=0)


def fold_columns(matrix):
    basis = matrix.shape[1]
    step = fold_step(basis)
    high, low = halves(matrix)
    row, column = iota((basis, 3 * step), 0), iota((basis, 3 * step), 1)
    outer = jnp.where((column == row) | (column == row + 2 * step), 1.0, 0.0).astype(BF16)
    inner = jnp.where(column == row + step, 1.0, 0.0).astype(BF16)
    return (dot(high, outer) + dot(low, inner)).astype(BF16)


def stiffen(stiff_fold, values, target, start, lanes):
    folded = jnp.concatenate([fold_rows(value) for value in values], axis=1)
    target[:, start * lanes:(start + len(values)) * lanes] = dot(stiff_fold, folded)


def mix_jacobians(stiffened, jac, basis, quants, lanes, take):
    for start in range(0, quants, GROUP):
        totals = [None] * GROUP
        for q in range(quants):
            for d in range(3):
                block = stiffened[d * basis:(d + 1) * basis, q * lanes:(q + 1) * lanes]
                for i in range(GROUP):
                    term = block * jac[q, start + i, d:d + 1, :]
                    totals[i] = term if totals[i] is None else totals[i] + term
        take(start, totals)


def mix_faces(table, flux, side, start, quants, lanes):
    totals = [[] for _ in range(GROUP)]
    for f in range(4):
        blocks = [
            table[q * ROWS:(q + 1) * ROWS, f * lanes:(f + 1) * lanes] for q in range(quants)
        ]
        for i in range(GROUP):
            total = blocks[0] * flux[side, 0, start + i, f:f + 1, :]
            for q in range(1, quants):
                total = total + blocks[q] * flux[side, q, start + i, f:f + 1, :]
            totals[i].append(total)
    return [jnp.concatenate(total, axis=0) for total in totals]


def fill_projector(projector, padded):
    modes, faces, basis = projector.shape
    padded[...] = jnp.zeros(padded.shape, F32)
    for f in range(faces):
        for m in range(modes):
            padded[f * ROWS + m:f * ROWS + m + 1, 0:basis] = projector[m, f:f + 1, :]


def predict(stiff_fold, jac, state, stiffened, first, second, basis, quants, lanes):
    for start in range(0, quants, GROUP):
        values = [state(q) for q in range(start, start + GROUP)]
        stiffen(stiff_fold, values, stiffened.at[0], start, lanes)
    for order in range(1, ORDER):
        factor = 1.0 / math.factorial(order + 1)

        def take(start, totals):
            if order + 1 < ORDER:
                stiffen(stiff_fold, totals, stiffened.at[order % 2], start, lanes)
            for p, total in enumerate(totals, start):
                first[p] = first[p] + factor * total
                if second is not None:
                    second[p] = second[p] + (2.0 ** (order + 1) - 1.0) * factor * total

        mix_jacobians(stiffened.at[(order - 1) % 2], jac, basis, quants, lanes, take)


def dense_rows(quants, modes):
    return -(-quants * modes // 32) * 32


def project_table(padded, field, table, dense, basis, quants, lanes, modes):
    fold = fold_columns(padded[:, 0:basis])
    last = dense.shape[0]
    dense[last - 8:last] = jnp.zeros((8, dense.shape[1]), F32)
    for start in range(0, quants, GROUP):
        values = [fold_rows(field(q)) for q in range(start, start + GROUP)]
        flat = dot(fold, jnp.concatenate(values, axis=1))
        for q in range(start, start + GROUP):
            for f in range(4):
                block = flat[f * ROWS:(f + 1) * ROWS, (q - start) * lanes:(q - start + 1) * lanes]
                columns = slice(f * lanes, (f + 1) * lanes)
                table[q * ROWS:(q + 1) * ROWS, columns] = block
                dense[q * modes:(q + 1) * modes, columns] = block[0:modes]


def even_spot():
    return [lax.rem(lax.axis_index(axis), 2) == 0 for axis in ("dom", "sub")]


def send_choice(send_row, faces, lanes):
    low = jnp.broadcast_to(send_row[:, 0:lanes], (8, lanes))
    lane = iota((8, lanes), 1)
    turned = pltpu.roll(low, SLOTS_DOM, 1)
    high = send_row[:, 2 * SLOTS_DOM:2 * SLOTS_DOM + 2 * SLOTS_SUB]
    spread = jnp.broadcast_to(jnp.concatenate([high, high], axis=1), (8, lanes))
    moved = pltpu.roll(spread, SLOTS_SUB, 1)
    left = lax.rem(lane, 2 * SLOTS_SUB) < SLOTS_SUB
    pieces = [
        jnp.where(lane < SLOTS_DOM, low, turned),
        jnp.where(lane < SLOTS_DOM, turned, low),
        jnp.where(left, spread, moved),
        jnp.where(left, moved, spread),
    ]
    even_dom, even_sub = even_spot()
    pieces = [
        jnp.where(even_dom, pieces[1], pieces[0]),
        jnp.where(even_dom, pieces[0], pieces[1]),
        jnp.where(even_sub, pieces[3], pieces[2]),
        jnp.where(even_sub, pieces[2], pieces[3]),
    ]
    return one_hot(jnp.concatenate([piece[0:1] for piece in pieces], axis=1), 0, faces)


def pick_sends(dense, chosen, outs, turns, lanes):
    sent = gather(dense[...], chosen)
    for k, count in enumerate(PACKING):
        out = outs[turns.index(k)] if k < 2 else outs[2]
        rows = sent.shape[0] // count
        values = sent[:, k * lanes:(k + 1) * lanes]
        spot = iota((rows, lanes), 1)
        packed = values[0:rows]
        for g in range(1, count):
            packed = jnp.where(
                spot >= g * (lanes // count), values[g * rows:(g + 1) * rows], packed
            )
        row = rows if k == 3 else 0
        out[row:row + rows] = packed


def spread_received(arrived, count, lanes):
    width = lanes // count
    place = iota(arrived.shape, 1)
    return jnp.concatenate(
        [
            jnp.where((place >= g * width) & (place < (g + 1) * width), arrived, 0.0)
            for g in range(count)
        ],
        axis=0,
    )


def pick_local(table, slot, faces):
    chosen = jnp.concatenate([one_hot(slot[f:f + 1], 0, faces) for f in range(4)], axis=1)
    return gather(table, chosen)


def received_choice(slot, faces, lanes):
    even_dom, even_sub = even_spot()
    starts = (
        jnp.where(even_dom, faces + SLOTS_DOM, faces),
        jnp.where(even_dom, faces, faces + SLOTS_DOM),
        faces + 2 * SLOTS_DOM + jnp.where(even_sub, SLOTS_SUB, 0),
        faces + 2 * SLOTS_DOM + jnp.where(even_sub, 0, SLOTS_SUB),
    )
    widths = (SLOTS_DOM, SLOTS_DOM, SLOTS_SUB, SLOTS_SUB)
    return jnp.concatenate(
        [
            jnp.concatenate(
                [one_hot(slot[f:f + 1], first, lanes, width) for f in range(4)], axis=1
            )
            for first, width in zip(starts, widths)
        ],
        axis=0,
    )


def pick_received(picked, local, doms, near, far, chosen, dense, quants, modes, lanes):
    spot, count = lax.axis_index("sub"), lax.axis_size("sub")
    met = jnp.where(lax.rem(spot, 2) == 0, spot > 0, spot < count - 1)
    half = near.shape[0] // 2
    pieces = [
        doms[0][...],
        doms[1][...],
        near[0:half],
        jnp.where(met, far[...], 0.0),
    ]
    spread = jnp.concatenate(
        [spread_received(item, groups, lanes) for item, groups in zip(pieces, PACKING)],
        axis=1,
    )
    dense[...] = gather(spread, chosen)
    for q in range(quants):
        row = q * ROWS
        picked[row + modes:row + ROWS] = local[row + modes:row + ROWS]
        picked[row:row + modes] = local[row:row + modes] + dense[q * modes:(q + 1) * modes]


def lift_weights(lifting):
    basis, depth = lifting.shape
    rest = jnp.zeros((fold_step(basis) - basis, depth), F32)
    high, low = halves(jnp.concatenate([lifting, rest], axis=0))
    return jnp.concatenate([high, low], axis=0)


def lift(weights, high, low, basis):
    step = fold_step(basis)
    both = dot(weights, high)
    return both[0:basis] + both[step:step + basis] + dot(weights[0:step], low)[0:basis]


def local_update(
    base, integral, table, jac, turned_fold, flux, lifting, stiffened, part,
    basis, quants, lanes,
):
    for start in range(0, quants, GROUP):
        values = [integral(q) for q in range(start, start + GROUP)]
        stiffen(turned_fold, values, stiffened, start, lanes)
    weights = lift_weights(lifting)
    for start in range(0, quants, GROUP):
        solved = mix_faces(table, flux, 0, start, quants, lanes)
        high, low = halves(jnp.concatenate(solved, axis=1))
        own = lift(weights, high, low, basis)
        for i in range(GROUP):
            part[start + i] = base(start + i) - own[:, i * lanes:(i + 1) * lanes]

    def take(start, totals):
        for p, total in enumerate(totals, start):
            part[p] = part[p] + total

    mix_jacobians(stiffened, jac, basis, quants, lanes, take)


def near_lift(picked, flux, orient, lifting, quants, lanes, take):
    weights = lift_weights(lifting)
    masks = [
        jnp.concatenate(
            [
                jnp.broadcast_to(jnp.where(orient[f:f + 1] == o, 1.0, 0.0), (ROWS, lanes))
                for f in range(4)
            ],
            axis=0,
        ).astype(BF16)
        for o in range(3)
    ]
    for start in range(0, quants, GROUP):
        highs, lows = [], []
        for solved in mix_faces(picked, flux, 1, start, quants, lanes):
            high, low = halves(solved)
            highs.append(jnp.concatenate([high * mask for mask in masks], axis=0))
            lows.append(jnp.concatenate([low * mask for mask in masks], axis=0))
        near = lift(
            weights, jnp.concatenate(highs, axis=1), jnp.concatenate(lows, axis=1),
            lifting.shape[0],
        )
        for i in range(GROUP):
            take(start + i, near[:, i * lanes:(i + 1) * lanes])


def near_lifting(own_lifting, rotations):
    count, modes, _ = rotations.shape
    block = 4 * ROWS
    row, column = iota((modes, count * block), 0), iota((modes, count * block), 1)
    turned = jnp.zeros((modes, count * block), F32)
    for o in range(count):
        spot = (lax.rem(column, ROWS) == row) & (lax.div(column, block) == o)
        turned = turned + exact_dot(rotations[o], jnp.where(spot, 1.0, 0.0))
    row, column = iota((block, modes), 0), iota((block, modes), 1)
    tall = exact_dot(jnp.where(lax.rem(row, ROWS) == column, 1.0, 0.0), turned)
    row, column = iota(tall.shape, 0), iota(tall.shape, 1)
    same = lax.div(row, ROWS) == lax.div(lax.rem(column, block), ROWS)
    return exact_dot(own_lifting, jnp.where(same, tall, 0.0))


def first_kernel(*refs):
    inputs, refs = refs[:INPUTS], refs[INPUTS:]
    held, refs = refs[:INPUTS], refs[INPUTS:]
    first, second, table, padded, stiff_fold, choice, *sends, stiffened, dense, arrivals = refs
    copies, count = [], 0
    for source, target, parts in zip(inputs, held, INPUT_PARTS):
        step = source.shape[0] // parts
        group = []
        for k in range(parts):
            part = (source, target)
            if parts > 1:
                part = [item.at[pl.ds(k * step, step)] for item in part]
            group.append(pltpu.make_async_copy(*part, arrivals.at[count]))
            count += 1
        copies.append(group)

    def start(groups):
        for group in groups:
            for copy in group:
                copy.start()

    def finish(groups):
        for group in groups:
            for copy in group:
                copy.wait()

    start(copies[:FIRST_USED])
    send_row, projector, stiffness, state, jac = held[:FIRST_USED]
    quants, basis, lanes = state.shape
    modes = projector.shape[0]
    finish(copies[0:1])
    choice[...] = send_choice(send_row, 4 * lanes, lanes)
    finish(copies[1:2])
    fill_projector(projector, padded)
    finish(copies[2:3])
    fold = fold_columns(jnp.concatenate([stiffness[d] for d in range(3)], axis=0))
    stiff_fold[...] = fold.astype(F32)
    finish(copies[3:4])
    for q in range(quants):
        value = state[q]
        first[q] = value
        second[q] = value
    finish(copies[4:5])
    start(copies[FIRST_USED:])
    predict(
        fold, jac, lambda q: state[q], stiffened, first, second, basis, quants, lanes
    )
    project_table(
        padded, lambda q: first[q], table, dense, basis, quants, lanes, modes
    )
    pick_sends(dense, choice[...], sends, FIRST_TURNS, lanes)
    finish(copies[FIRST_USED:])


def second_kernel(
    state, first, table, jac, stiffness, padded, rotations, flux, slot,
    part, picked, lifting, turned_fold, choice,
    stiffened,
):
    quants, basis, lanes = state.shape
    turned = jnp.concatenate([stiffness[d].T for d in range(3)], axis=0)
    fold = fold_columns(turned)
    turned_fold[...] = fold.astype(F32)
    own_lifting = padded[...].T[0:basis]
    lifting[...] = near_lifting(own_lifting, rotations)
    picked[...] = pick_local(table[...], slot, 4 * lanes)
    choice[...] = received_choice(slot, 4 * lanes, lanes)
    local_update(
        lambda p: state[p], lambda q: first[q], table, jac, fold, flux, own_lifting,
        stiffened, part, basis, quants, lanes,
    )


def third_kernel(
    state, first, second, part, picked_local, sub_far, dom_a, dom_b, sub_near,
    rotations, jac, stiff_fold, padded, flux, orient, cluster, lifting, received, choice,
    middle, integral, picked, table, *refs,
):
    *sends, stiffened, dense = refs
    quants, basis, lanes = state.shape
    modes = rotations.shape[1]
    doms = [(dom_a, dom_b)[FIRST_TURNS.index(k)] for k in (0, 1)]
    pick_received(
        picked, picked_local, doms, sub_near, sub_far, received[...], dense,
        quants, modes, lanes,
    )
    fine = cluster[...] == 0

    def take(p, near):
        value = jnp.where(fine, part[p] - near, state[p])
        middle[p] = value
        integral[p] = value

    near_lift(picked, flux, orient, lifting[...], quants, lanes, take)
    predict(
        stiff_fold[...].astype(BF16), jac, lambda q: middle[q], stiffened, integral, None,
        basis, quants, lanes,
    )
    project_table(
        padded, lambda q: jnp.where(fine, integral[q], second[q]), table, dense,
        basis, quants, lanes, modes,
    )
    for q in range(quants):
        integral[q] = jnp.where(fine, integral[q], first[q] + second[q])
    pick_sends(dense, choice[...], sends, SECOND_TURNS, lanes)


def fourth_kernel(
    middle, integral, table_one, table_two, picked_one, jac, turned_fold, padded, flux, slot,
    cluster,
    part, picked,
    stiffened, total_table,
):
    quants, basis, lanes = middle.shape
    own_lifting = padded[...].T[0:basis]
    coarse = jnp.concatenate([cluster[...] != 0] * 4, axis=1)
    total_table[...] = table_two[...] + jnp.where(coarse, table_one[...], 0.0)
    picked[...] = pick_local(table_two[...], slot, 4 * lanes) + jnp.where(
        coarse, picked_one[...], 0.0
    )
    local_update(
        lambda p: middle[p], lambda q: integral[q], total_table, jac,
        turned_fold[...].astype(BF16), flux, own_lifting,
        stiffened, part, basis, quants, lanes,
    )


def fifth_kernel(
    part, picked_local, sub_far, dom_a, dom_b, sub_near, rotations, flux, orient, lifting,
    received, yield_stress,
    updated,
    picked, dense,
):
    quants, basis, lanes = part.shape
    modes = rotations.shape[1]
    doms = [(dom_a, dom_b)[SECOND_TURNS.index(k)] for k in (0, 1)]
    pick_received(
        picked, picked_local, doms, sub_near, sub_far, received[...], dense,
        quants, modes, lanes,
    )
    stepped = [None] * quants

    def take(p, near):
        stepped[p] = part[p] - near

    near_lift(picked, flux, orient, lifting[...], quants, lanes, take)
    mean_part = (stepped[0] + stepped[1] + stepped[2]) / 3.0
    spread = [stepped[q] - mean_part for q in range(3)]
    normal = [item[0:1] for item in spread]
    shear = [stepped[q][0:1] for q in range(3, 6)]
    second_inv = 0.5 * (normal[0] ** 2 + normal[1] ** 2 + normal[2] ** 2) + (
        shear[0] ** 2 + shear[1] ** 2 + shear[2] ** 2
    )
    limit = yield_stress[...]
    scaling = limit / jnp.maximum(jnp.sqrt(second_inv), limit)
    for q in range(3):
        updated[q] = mean_part + scaling * spread[q]
    for q in range(3, 6):
        updated[q] = scaling * stepped[q]
    for q in range(6, quants):
        updated[q] = stepped[q]


def run(body, outs, scratch, *operands, space=pltpu.VMEM):
    vmem = pl.BlockSpec(memory_space=pltpu.VMEM)
    return pl.pallas_call(
        body,
        out_shape=[
            out if isinstance(out, jax.ShapeDtypeStruct) else jax.ShapeDtypeStruct(out, F32)
            for out in outs
        ],
        in_specs=[pl.BlockSpec(memory_space=space)] * len(operands),
        out_specs=[vmem] * len(outs),
        scratch_shapes=scratch,
        compiler_params=pltpu.CompilerParams(vmem_limit_bytes=32 * 1024 * 1024),
        name=body.__name__,
    )(*operands)


def hand_on(near, dom, onward):
    rows = onward.shape[0]
    onward[...] = near[rows:2 * rows]


def exchange(sends, turns):
    def swap(value, axis, first):
        lower = range(first, lax.axis_size(axis) - 1, 2)
        return lax.ppermute(
            value, axis, [(i, i + 1) for i in lower] + [(i + 1, i) for i in lower]
        )

    count = lax.axis_size("sub")
    near = swap(sends[2], "sub", 0)
    dom_even = swap(sends[turns.index(0)], "dom", 0)
    kept, = run(hand_on, [(near.shape[0] // 2, near.shape[1])], [], near, dom_even)
    onward = [(i, (i + (2 if i % 2 == 0 else -2)) % count) for i in range(count)]
    far = lax.ppermute(kept, "sub", onward)
    dom_odd = swap(sends[turns.index(1)], "dom", 1)
    doms = (dom_even, dom_odd)
    return [far] + [doms[k] for k in turns] + [near]


def on_device(
    modal_state,
    stiffness,
    jacobians,
    flux_solvers,
    projector,
    rotations,
    yield_stress,
    cluster,
    orient,
    neighbour_slot,
    send_map,
):
    basis, quants, lanes = modal_state.shape
    inputs = [
        send_map.reshape(1, -1),
        jnp.transpose(projector, (1, 0, 2)),
        stiffness,
        jnp.transpose(modal_state, (1, 0, 2)),
        jnp.transpose(jacobians, (1, 2, 0, 3)),
        jnp.transpose(flux_solvers, (0, 2, 3, 1, 4)),
        rotations,
        neighbour_slot,
        orient,
        cluster.reshape(1, lanes),
        yield_stress.reshape(1, lanes),
    ]
    inputs = [pltpu.with_memory_space_constraint(item, pltpu.HBM) for item in inputs]
    held = [jax.ShapeDtypeStruct(item.shape, item.dtype) for item in inputs]

    field = (quants, basis, lanes)
    table = (quants * ROWS, 4 * lanes)
    rows = dense_rows(quants, projector.shape[1])
    dense = pltpu.VMEM((rows, 4 * lanes), F32)
    messages = [(rows // 2, lanes)] * 3
    choice = jax.ShapeDtypeStruct((4 * lanes, 4 * lanes), BF16)
    flat = quants * lanes
    fold = (3 * basis, 3 * fold_step(basis))
    stiffened = pltpu.VMEM((3 * basis, flat), F32)
    two_stiffened = pltpu.VMEM((2, 3 * basis, flat), F32)

    outs = run(
        first_kernel,
        held + [field, field, table, (4 * ROWS, 128), fold, choice] + messages,
        [two_stiffened, dense, pltpu.SemaphoreType.DMA((sum(INPUT_PARTS),))],
        *inputs, space=pl.ANY,
    )
    _, _, stiff, state, jac, flux, turns, slot, orient, cluster, limit = outs[:INPUTS]
    first, second, table_one, padded, stiff_fold, sending, *sends = outs[INPUTS:]
    arrived = exchange(sends, FIRST_TURNS)
    part_one, local_one, lifting, turned_fold, received = run(
        second_kernel, [field, table, (basis, 3 * 4 * ROWS), fold, choice], [stiffened],
        state, first, table_one, jac, stiff, padded, turns, flux, slot,
    )
    middle, integral, picked_one, table_two, *sends = run(
        third_kernel, [field, field, table, table] + messages, [two_stiffened, dense],
        state, first, second, part_one, local_one, *arrived, turns,
        jac, stiff_fold, padded, flux, orient, cluster, lifting, received, sending,
    )
    arrived = exchange(sends, SECOND_TURNS)
    part_two, local_two = run(
        fourth_kernel, [field, table], [stiffened, pltpu.VMEM(table, F32)],
        middle, integral, table_one, table_two, picked_one, jac, turned_fold, padded, flux,
        slot, cluster,
    )
    updated, = run(
        fifth_kernel, [field], [pltpu.VMEM(table, F32), dense],
        part_two, local_two, *arrived, turns, flux, orient, lifting, received, limit,
    )
    return jnp.transpose(updated, (1, 0, 2))


def solution(mesh):
    placed = (
        P(None, None, ("dom", "sub")),
        P(),
        P(None, None, None, ("dom", "sub")),
        P(None, None, None, None, ("dom", "sub")),
        P(),
        P(),
        P(("dom", "sub")),
        P(("dom", "sub")),
        P(None, ("dom", "sub")),
        P(None, ("dom", "sub")),
        P(("dom", "sub")),
    )
    return jax.shard_map(
        on_device,
        mesh=mesh,
        in_specs=placed,
        out_specs=P(None, None, ("dom", "sub")),
        check_vma=False,
    )
```

```python
import math

import jax
import jax.numpy as jnp
from jax import lax
from jax.experimental import pallas as pl
from jax.experimental.pallas import tpu as pltpu
from jax.sharding import PartitionSpec as P

ORDER = 6
SLOTS_DOM = 64
SLOTS_SUB = 32
ROWS = 24
GROUP = 3

F32 = jnp.float32
BF16 = jnp.bfloat16
EXACT = lax.Precision.HIGHEST

PACKING = (2, 2, 4, 4)

INPUTS = 11
FIRST_USED = 5


def iota(shape, dim):
    return lax.broadcasted_iota(jnp.int32, shape, dim)


def dot(a, b):
    return jnp.dot(a, b, preferred_element_type=F32)


def exact_dot(a, b):
    return jnp.dot(a, b, precision=EXACT, preferred_element_type=F32)


def halves(value):
    high = value.astype(BF16)
    return high, (value - high.astype(F32)).astype(BF16)


def one_hot(index_row, first, count, modulus=None):
    number = iota((count, index_row.shape[1]), 0)
    if modulus is not None:
        number = lax.rem(number, modulus)
    return jnp.where(number + first == index_row, 1.0, 0.0).astype(BF16)


def stack_rows(value):
    high = value.astype(BF16).astype(F32)
    return jnp.concatenate([high, value - high], axis=0).astype(BF16)


def gather(table, chosen):
    rows = table.shape[0]
    both = dot(stack_rows(table), chosen)
    return both[0:rows] + both[rows:2 * rows]


def fold_step(basis):
    return -(-basis // 16) * 16


def fold_rows(value):
    basis, lanes = value.shape
    rest = jnp.zeros((fold_step(basis) - basis, lanes), F32)
    value = jnp.concatenate([value, rest], axis=0)
    high, low = halves(value)
    return jnp.concatenate([high, high, low], axis=0)


def fold_columns(matrix):
    basis = matrix.shape[1]
    step = fold_step(basis)
    high, low = halves(matrix)
    row, column = iota((basis, 3 * step), 0), iota((basis, 3 * step), 1)
    outer = jnp.where((column == row) | (column == row + 2 * step), 1.0, 0.0).astype(BF16)
    inner = jnp.where(column == row + step, 1.0, 0.0).astype(BF16)
    return (dot(high, outer) + dot(low, inner)).astype(BF16)


def stiffen(stiff_fold, values, target, start, lanes):
    folded = jnp.concatenate([fold_rows(value) for value in values], axis=1)
    target[:, start * lanes:(start + len(values)) * lanes] = dot(stiff_fold, folded)


def mix_jacobians(stiffened, jac, basis, quants, lanes, take):
    for start in range(0, quants, GROUP):
        totals = [None] * GROUP
        for q in range(quants):
            for d in range(3):
                block = stiffened[d * basis:(d + 1) * basis, q * lanes:(q + 1) * lanes]
                for i in range(GROUP):
                    term = block * jac[q, start + i, d:d + 1, :]
                    totals[i] = term if totals[i] is None else totals[i] + term
        take(start, totals)


def mix_faces(table, flux, side, start, quants, lanes):
    totals = [[] for _ in range(GROUP)]
    for f in range(4):
        blocks = [
            table[q * ROWS:(q + 1) * ROWS, f * lanes:(f + 1) * lanes] for q in range(quants)
        ]
        for i in range(GROUP):
            total = blocks[0] * flux[side, 0, start + i, f:f + 1, :]
            for q in range(1, quants):
                total = total + blocks[q] * flux[side, q, start + i, f:f + 1, :]
            totals[i].append(total)
    return [jnp.concatenate(total, axis=0) for total in totals]


def fill_projector(projector, padded):
    modes, faces, basis = projector.shape
    padded[...] = jnp.zeros(padded.shape, F32)
    for f in range(faces):
        for m in range(modes):
            padded[f * ROWS + m:f * ROWS + m + 1, 0:basis] = projector[m, f:f + 1, :]


def predict(stiff_fold, jac, state, stiffened, first, second, basis, quants, lanes):
    for start in range(0, quants, GROUP):
        values = [state(q) for q in range(start, start + GROUP)]
        stiffen(stiff_fold, values, stiffened.at[0], start, lanes)
    for order in range(1, ORDER):
        factor = 1.0 / math.factorial(order + 1)

        def take(start, totals):
            if order + 1 < ORDER:
                stiffen(stiff_fold, totals, stiffened.at[order % 2], start, lanes)
            for p, total in enumerate(totals, start):
                first[p] = first[p] + factor * total
                if second is not None:
                    second[p] = second[p] + (2.0 ** (order + 1) - 1.0) * factor * total

        mix_jacobians(stiffened.at[(order - 1) % 2], jac, basis, quants, lanes, take)


def dense_rows(quants, modes):
    return -(-quants * modes // 32) * 32


def project_table(padded, field, table, dense, basis, quants, lanes, modes):
    fold = fold_columns(padded[:, 0:basis])
    last = dense.shape[0]
    dense[last - 8:last] = jnp.zeros((8, dense.shape[1]), F32)
    for start in range(0, quants, GROUP):
        values = [fold_rows(field(q)) for q in range(start, start + GROUP)]
        flat = dot(fold, jnp.concatenate(values, axis=1))
        for q in range(start, start + GROUP):
            for f in range(4):
                block = flat[f * ROWS:(f + 1) * ROWS, (q - start) * lanes:(q - start + 1) * lanes]
                columns = slice(f * lanes, (f + 1) * lanes)
                table[q * ROWS:(q + 1) * ROWS, columns] = block
                dense[q * modes:(q + 1) * modes, columns] = block[0:modes]


def even_spot():
    return [lax.rem(lax.axis_index(axis), 2) == 0 for axis in ("dom", "sub")]


def send_choice(send_row, faces, lanes):
    low = jnp.broadcast_to(send_row[:, 0:lanes], (8, lanes))
    lane = iota((8, lanes), 1)
    turned = pltpu.roll(low, SLOTS_DOM, 1)
    high = send_row[:, 2 * SLOTS_DOM:2 * SLOTS_DOM + 2 * SLOTS_SUB]
    spread = jnp.broadcast_to(jnp.concatenate([high, high], axis=1), (8, lanes))
    moved = pltpu.roll(spread, SLOTS_SUB, 1)
    left = lax.rem(lane, 2 * SLOTS_SUB) < SLOTS_SUB
    pieces = [
        jnp.where(lane < SLOTS_DOM, low, turned),
        jnp.where(lane < SLOTS_DOM, turned, low),
        jnp.where(left, spread, moved),
        jnp.where(left, moved, spread),
    ]
    even_dom, even_sub = even_spot()
    pieces = [
        jnp.where(even_dom, pieces[1], pieces[0]),
        jnp.where(even_dom, pieces[0], pieces[1]),
        jnp.where(even_sub, pieces[3], pieces[2]),
        jnp.where(even_sub, pieces[2], pieces[3]),
    ]
    return one_hot(jnp.concatenate([piece[0:1] for piece in pieces], axis=1), 0, faces)


def pick_sends(dense, chosen, outs, lanes):
    sent = gather(dense[...], chosen)
    for k, count in enumerate(PACKING):
        out = outs[min(k, 2)]
        rows = sent.shape[0] // count
        values = sent[:, k * lanes:(k + 1) * lanes]
        spot = iota((rows, lanes), 1)
        packed = values[0:rows]
        for g in range(1, count):
            packed = jnp.where(
                spot >= g * (lanes // count), values[g * rows:(g + 1) * rows], packed
            )
        row = rows if k == 3 else 0
        out[row:row + rows] = packed


def spread_received(arrived, count, lanes):
    width = lanes // count
    place = iota(arrived.shape, 1)
    return jnp.concatenate(
        [
            jnp.where((place >= g * width) & (place < (g + 1) * width), arrived, 0.0)
            for g in range(count)
        ],
        axis=0,
    )


def pick_local(table, slot, faces):
    chosen = jnp.concatenate([one_hot(slot[f:f + 1], 0, faces) for f in range(4)], axis=1)
    return gather(table, chosen)


def received_choice(slot, faces, lanes):
    even_dom, even_sub = even_spot()
    starts = (
        jnp.where(even_dom, faces + SLOTS_DOM, faces),
        faces + 2 * SLOTS_DOM + jnp.where(even_sub, SLOTS_SUB, 0),
        jnp.where(even_dom, faces, faces + SLOTS_DOM),
        faces + 2 * SLOTS_DOM + jnp.where(even_sub, 0, SLOTS_SUB),
    )
    widths = (SLOTS_DOM, SLOTS_SUB, SLOTS_DOM, SLOTS_SUB)
    return jnp.concatenate(
        [
            jnp.concatenate(
                [one_hot(slot[f:f + 1], first, lanes, width) for f in range(4)], axis=1
            )
            for first, width in zip(starts, widths)
        ],
        axis=0,
    )


def add_received(picked, dom, sub, chosen, dense, quants, modes, lanes):
    pieces = zip((dom, sub), (PACKING[0], PACKING[2]))
    spread = jnp.concatenate(
        [spread_received(item, count, lanes) for item, count in pieces], axis=1
    )
    dense[...] = gather(spread, chosen)
    for q in range(quants):
        rows = slice(q * ROWS, q * ROWS + modes)
        picked[rows] = picked[rows] + dense[q * modes:(q + 1) * modes]


def add_early(picked, dom, near, chosen, dense, quants, modes, lanes):
    half = near.shape[0] // 2
    add_received(
        picked, dom[...], near[0:half], chosen[0:2 * lanes], dense, quants, modes, lanes
    )


def add_late(picked, dom, far, chosen, dense, quants, modes, lanes):
    spot, count = lax.axis_index("sub"), lax.axis_size("sub")
    met = jnp.where(lax.rem(spot, 2) == 0, spot > 0, spot < count - 1)
    piece = jnp.where(met, far[...], 0.0)
    add_received(
        picked, dom[...], piece, chosen[2 * lanes:4 * lanes], dense, quants, modes, lanes
    )


def lift_weights(lifting):
    basis, depth = lifting.shape
    rest = jnp.zeros((fold_step(basis) - basis, depth), F32)
    high, low = halves(jnp.concatenate([lifting, rest], axis=0))
    return jnp.concatenate([high, low], axis=0)


def lift(weights, high, low, basis):
    step = fold_step(basis)
    both = dot(weights, high)
    return both[0:basis] + both[step:step + basis] + dot(weights[0:step], low)[0:basis]


def local_update(
    base, integral, table, jac, turned_fold, flux, lifting, stiffened, part,
    basis, quants, lanes,
):
    for start in range(0, quants, GROUP):
        values = [integral(q) for q in range(start, start + GROUP)]
        stiffen(turned_fold, values, stiffened, start, lanes)
    weights = lift_weights(lifting)
    for start in range(0, quants, GROUP):
        solved = mix_faces(table, flux, 0, start, quants, lanes)
        high, low = halves(jnp.concatenate(solved, axis=1))
        own = lift(weights, high, low, basis)
        for i in range(GROUP):
            part[start + i] = base(start + i) - own[:, i * lanes:(i + 1) * lanes]

    def take(start, totals):
        for p, total in enumerate(totals, start):
            part[p] = part[p] + total

    mix_jacobians(stiffened, jac, basis, quants, lanes, take)


def near_lift(picked, flux, orient, lifting, quants, lanes, take):
    weights = lift_weights(lifting)
    masks = [
        jnp.concatenate(
            [
                jnp.broadcast_to(jnp.where(orient[f:f + 1] == o, 1.0, 0.0), (ROWS, lanes))
                for f in range(4)
            ],
            axis=0,
        ).astype(BF16)
        for o in range(3)
    ]
    for start in range(0, quants, GROUP):
        highs, lows = [], []
        for solved in mix_faces(picked, flux, 1, start, quants, lanes):
            high, low = halves(solved)
            highs.append(jnp.concatenate([high * mask for mask in masks], axis=0))
            lows.append(jnp.concatenate([low * mask for mask in masks], axis=0))
        near = lift(
            weights, jnp.concatenate(highs, axis=1), jnp.concatenate(lows, axis=1),
            lifting.shape[0],
        )
        for i in range(GROUP):
            take(start + i, near[:, i * lanes:(i + 1) * lanes])


def near_lifting(own_lifting, rotations):
    count, modes, _ = rotations.shape
    block = 4 * ROWS
    row, column = iota((modes, count * block), 0), iota((modes, count * block), 1)
    turned = jnp.zeros((modes, count * block), F32)
    for o in range(count):
        spot = (lax.rem(column, ROWS) == row) & (lax.div(column, block) == o)
        turned = turned + exact_dot(rotations[o], jnp.where(spot, 1.0, 0.0))
    row, column = iota((block, modes), 0), iota((block, modes), 1)
    tall = exact_dot(jnp.where(lax.rem(row, ROWS) == column, 1.0, 0.0), turned)
    row, column = iota(tall.shape, 0), iota(tall.shape, 1)
    same = lax.div(row, ROWS) == lax.div(lax.rem(column, block), ROWS)
    return exact_dot(own_lifting, jnp.where(same, tall, 0.0))


def first_kernel(*refs):
    inputs, refs = refs[:INPUTS], refs[INPUTS:]
    held, refs = refs[:INPUTS], refs[INPUTS:]
    first, second, table, padded, stiff_fold, choice, *sends, stiffened, dense, arrivals = refs
    copies = [
        pltpu.make_async_copy(source, target, arrivals.at[k])
        for k, (source, target) in enumerate(zip(inputs, held))
    ]
    for copy in copies:
        copy.start()
    send_row, projector, stiffness, state, jac = held[:FIRST_USED]
    quants, basis, lanes = state.shape
    modes = projector.shape[0]
    copies[0].wait()
    choice[...] = send_choice(send_row, 4 * lanes, lanes)
    copies[1].wait()
    fill_projector(projector, padded)
    copies[2].wait()
    fold = fold_columns(jnp.concatenate([stiffness[d] for d in range(3)], axis=0))
    stiff_fold[...] = fold.astype(F32)
    copies[3].wait()
    for q in range(quants):
        value = state[q]
        first[q] = value
        second[q] = value
    copies[4].wait()
    predict(
        fold, jac, lambda q: state[q], stiffened, first, second, basis, quants, lanes
    )
    project_table(
        padded, lambda q: first[q], table, dense, basis, quants, lanes, modes
    )
    pick_sends(dense, choice[...], sends, lanes)
    for copy in copies[FIRST_USED:]:
        copy.wait()


def second_kernel(
    state, first, table, near, dom, jac, stiffness, padded, rotations, flux, slot,
    part, picked, lifting, turned_fold, choice,
    stiffened, dense,
):
    quants, basis, lanes = state.shape
    modes = rotations.shape[1]
    turned = jnp.concatenate([stiffness[d].T for d in range(3)], axis=0)
    fold = fold_columns(turned)
    turned_fold[...] = fold.astype(F32)
    own_lifting = padded[...].T[0:basis]
    lifting[...] = near_lifting(own_lifting, rotations)
    picked[...] = pick_local(table[...], slot, 4 * lanes)
    choice[...] = received_choice(slot, 4 * lanes, lanes)
    add_early(picked, dom, near, choice, dense, quants, modes, lanes)
    local_update(
        lambda p: state[p], lambda q: first[q], table, jac, fold, flux, own_lifting,
        stiffened, part, basis, quants, lanes,
    )


def third_kernel(
    state, first, second, part, picked_early, far, dom, rotations, jac, stiff_fold, padded, flux, orient, cluster, lifting, received, choice,
    middle, integral, picked, table, *refs,
):
    *sends, stiffened, dense = refs
    quants, basis, lanes = state.shape
    modes = rotations.shape[1]
    picked[...] = picked_early[...]
    add_late(picked, dom, far, received, dense, quants, modes, lanes)
    fine = cluster[...] == 0

    def take(p, near):
        value = jnp.where(fine, part[p] - near, state[p])
        middle[p] = value
        integral[p] = value

    near_lift(picked, flux, orient, lifting[...], quants, lanes, take)
    predict(
        stiff_fold[...].astype(BF16), jac, lambda q: middle[q], stiffened, integral, None,
        basis, quants, lanes,
    )
    project_table(
        padded, lambda q: jnp.where(fine, integral[q], second[q]), table, dense,
        basis, quants, lanes, modes,
    )
    for q in range(quants):
        integral[q] = jnp.where(fine, integral[q], first[q] + second[q])
    pick_sends(dense, choice[...], sends, lanes)


def fourth_kernel(
    middle, integral, table_one, table_two, picked_one, near, dom, jac, turned_fold, padded,
    rotations, flux, slot, cluster, received,
    part, picked,
    stiffened, dense, total_table,
):
    quants, basis, lanes = middle.shape
    modes = rotations.shape[1]
    own_lifting = padded[...].T[0:basis]
    coarse = jnp.concatenate([cluster[...] != 0] * 4, axis=1)
    total_table[...] = table_two[...] + jnp.where(coarse, table_one[...], 0.0)
    picked[...] = pick_local(table_two[...], slot, 4 * lanes) + jnp.where(
        coarse, picked_one[...], 0.0
    )
    add_early(picked, dom, near, received, dense, quants, modes, lanes)
    local_update(
        lambda p: middle[p], lambda q: integral[q], total_table, jac,
        turned_fold[...].astype(BF16), flux, own_lifting,
        stiffened, part, basis, quants, lanes,
    )


def fifth_kernel(
    part, picked_early, far, dom, rotations, flux, orient, lifting, received, yield_stress,
    updated,
    picked, dense,
):
    quants, basis, lanes = part.shape
    modes = rotations.shape[1]
    picked[...] = picked_early[...]
    add_late(picked, dom, far, received, dense, quants, modes, lanes)
    stepped = [None] * quants

    def take(p, near):
        stepped[p] = part[p] - near

    near_lift(picked, flux, orient, lifting[...], quants, lanes, take)
    mean_part = (stepped[0] + stepped[1] + stepped[2]) / 3.0
    spread = [stepped[q] - mean_part for q in range(3)]
    normal = [item[0:1] for item in spread]
    shear = [stepped[q][0:1] for q in range(3, 6)]
    second_inv = 0.5 * (normal[0] ** 2 + normal[1] ** 2 + normal[2] ** 2) + (
        shear[0] ** 2 + shear[1] ** 2 + shear[2] ** 2
    )
    limit = yield_stress[...]
    scaling = limit / jnp.maximum(jnp.sqrt(second_inv), limit)
    for q in range(3):
        updated[q] = mean_part + scaling * spread[q]
    for q in range(3, 6):
        updated[q] = scaling * stepped[q]
    for q in range(6, quants):
        updated[q] = stepped[q]


def run(body, outs, scratch, *operands, space=pltpu.VMEM):
    vmem = pl.BlockSpec(memory_space=pltpu.VMEM)
    return pl.pallas_call(
        body,
        out_shape=[
            out if isinstance(out, jax.ShapeDtypeStruct) else jax.ShapeDtypeStruct(out, F32)
            for out in outs
        ],
        in_specs=[pl.BlockSpec(memory_space=space)] * len(operands),
        out_specs=[vmem] * len(outs),
        scratch_shapes=scratch,
        compiler_params=pltpu.CompilerParams(vmem_limit_bytes=32 * 1024 * 1024),
        name=body.__name__,
    )(*operands)


def hand_on(near, dom, onward):
    rows = onward.shape[0]
    onward[...] = near[rows:2 * rows]


def exchange(sends):
    def swap(value, axis, first):
        lower = range(first, lax.axis_size(axis) - 1, 2)
        return lax.ppermute(
            value, axis, [(i, i + 1) for i in lower] + [(i + 1, i) for i in lower]
        )

    count = lax.axis_size("sub")
    near = swap(sends[2], "sub", 0)
    dom_even = swap(sends[0], "dom", 0)
    kept, = run(hand_on, [(near.shape[0] // 2, near.shape[1])], [], near, dom_even)
    onward = [(i, (i + (2 if i % 2 == 0 else -2)) % count) for i in range(count)]
    far = lax.ppermute(kept, "sub", onward)
    dom_odd = swap(sends[1], "dom", 1)
    return (near, dom_even), (far, dom_odd)


def on_device(
    modal_state,
    stiffness,
    jacobians,
    flux_solvers,
    projector,
    rotations,
    yield_stress,
    cluster,
    orient,
    neighbour_slot,
    send_map,
):
    basis, quants, lanes = modal_state.shape
    inputs = [
        send_map.reshape(1, -1),
        jnp.transpose(projector, (1, 0, 2)),
        stiffness,
        jnp.transpose(modal_state, (1, 0, 2)),
        jnp.transpose(jacobians, (1, 2, 0, 3)),
        jnp.transpose(flux_solvers, (0, 2, 3, 1, 4)),
        rotations,
        neighbour_slot,
        orient,
        cluster.reshape(1, lanes),
        yield_stress.reshape(1, lanes),
    ]
    inputs = [pltpu.with_memory_space_constraint(item, pltpu.HBM) for item in inputs]
    held = [jax.ShapeDtypeStruct(item.shape, item.dtype) for item in inputs]

    field = (quants, basis, lanes)
    table = (quants * ROWS, 4 * lanes)
    rows = dense_rows(quants, projector.shape[1])
    dense = pltpu.VMEM((rows, 4 * lanes), F32)
    messages = [(rows // 2, lanes)] * 3
    choice = jax.ShapeDtypeStruct((4 * lanes, 4 * lanes), BF16)
    flat = quants * lanes
    fold = (3 * basis, 3 * fold_step(basis))
    stiffened = pltpu.VMEM((3 * basis, flat), F32)
    two_stiffened = pltpu.VMEM((2, 3 * basis, flat), F32)

    outs = run(
        first_kernel,
        held + [field, field, table, (4 * ROWS, 128), fold, choice] + messages,
        [two_stiffened, dense, pltpu.SemaphoreType.DMA((INPUTS,))],
        *inputs, space=pl.ANY,
    )
    _, _, stiff, state, jac, flux, turns, slot, orient, cluster, limit = outs[:INPUTS]
    first, second, table_one, padded, stiff_fold, sending, *sends = outs[INPUTS:]
    early, late = exchange(sends)
    part_one, local_one, lifting, turned_fold, received = run(
        second_kernel, [field, table, (basis, 3 * 4 * ROWS), fold, choice], [stiffened, dense],
        state, first, table_one, *early, jac, stiff, padded, turns, flux, slot,
    )
    middle, integral, picked_one, table_two, *sends = run(
        third_kernel, [field, field, table, table] + messages, [two_stiffened, dense],
        state, first, second, part_one, local_one, *late, turns,
        jac, stiff_fold, padded, flux, orient, cluster, lifting, received, sending,
    )
    early, late = exchange(sends)
    part_two, local_two = run(
        fourth_kernel, [field, table], [stiffened, dense, pltpu.VMEM(table, F32)],
        middle, integral, table_one, table_two, picked_one, *early, jac, turned_fold, padded,
        turns, flux, slot, cluster, received,
    )
    updated, = run(
        fifth_kernel, [field], [pltpu.VMEM(table, F32), dense],
        part_two, local_two, *late, turns, flux, orient, lifting, received, limit,
    )
    return jnp.transpose(updated, (1, 0, 2))


def solution(mesh):
    placed = (
        P(None, None, ("dom", "sub")),
        P(),
        P(None, None, None, ("dom", "sub")),
        P(None, None, None, None, ("dom", "sub")),
        P(),
        P(),
        P(("dom", "sub")),
        P(("dom", "sub")),
        P(None, ("dom", "sub")),
        P(None, ("dom", "sub")),
        P(("dom", "sub")),
    )
    return jax.shard_map(
        on_device,
        mesh=mesh,
        in_specs=placed,
        out_specs=P(None, None, ("dom", "sub")),
        check_vma=False,
    )
```

```python
import math

import jax
import jax.numpy as jnp
from jax import lax
from jax.experimental import pallas as pl
from jax.experimental.pallas import tpu as pltpu
from jax.sharding import PartitionSpec as P

ORDER = 6
SLOTS_DOM = 64
SLOTS_SUB = 32
ROWS = 24
GROUP = 3

F32 = jnp.float32
BF16 = jnp.bfloat16
EXACT = lax.Precision.HIGHEST

PACKING = (2, 2, 4, 4)

INPUTS = 11
FIRST_USED = 5


def iota(shape, dim):
    return lax.broadcasted_iota(jnp.int32, shape, dim)


def dot(a, b):
    return jnp.dot(a, b, preferred_element_type=F32)


def exact_dot(a, b):
    return jnp.dot(a, b, precision=EXACT, preferred_element_type=F32)


def halves(value):
    high = value.astype(BF16)
    return high, (value - high.astype(F32)).astype(BF16)


def one_hot(index_row, first, count, modulus=None):
    number = iota((count, index_row.shape[1]), 0)
    if modulus is not None:
        number = lax.rem(number, modulus)
    return jnp.where(number + first == index_row, 1.0, 0.0).astype(BF16)


def stack_rows(value):
    high = value.astype(BF16).astype(F32)
    return jnp.concatenate([high, value - high], axis=0).astype(BF16)


def gather(table, chosen):
    rows = table.shape[0]
    both = dot(stack_rows(table), chosen)
    return both[0:rows] + both[rows:2 * rows]


def fold_step(basis):
    return -(-basis // 16) * 16


def fold_rows(value):
    basis, lanes = value.shape
    rest = jnp.zeros((fold_step(basis) - basis, lanes), F32)
    value = jnp.concatenate([value, rest], axis=0)
    high, low = halves(value)
    return jnp.concatenate([high, high, low], axis=0)


def fold_columns(matrix):
    basis = matrix.shape[1]
    step = fold_step(basis)
    high, low = halves(matrix)
    row, column = iota((basis, 3 * step), 0), iota((basis, 3 * step), 1)
    outer = jnp.where((column == row) | (column == row + 2 * step), 1.0, 0.0).astype(BF16)
    inner = jnp.where(column == row + step, 1.0, 0.0).astype(BF16)
    return (dot(high, outer) + dot(low, inner)).astype(BF16)


def stiffen(stiff_fold, values, target, start, lanes):
    folded = jnp.concatenate([fold_rows(value) for value in values], axis=1)
    target[:, start * lanes:(start + len(values)) * lanes] = dot(stiff_fold, folded)


def mix_jacobians(stiffened, jac, basis, quants, lanes, take):
    for start in range(0, quants, GROUP):
        totals = [None] * GROUP
        for q in range(quants):
            for d in range(3):
                block = stiffened[d * basis:(d + 1) * basis, q * lanes:(q + 1) * lanes]
                block = block.reshape(basis // 8, 8, lanes)
                for i in range(GROUP):
                    term = block * jac[(q * quants + start + i) * 3 + d]
                    totals[i] = term if totals[i] is None else totals[i] + term
        take(start, [total.reshape(basis, lanes) for total in totals])


def mix_faces(table, flux, side, start, quants, lanes):
    totals = [[] for _ in range(GROUP)]
    for f in range(4):
        blocks = [
            table[q * ROWS:(q + 1) * ROWS, f * lanes:(f + 1) * lanes] for q in range(quants)
        ]
        for i in range(GROUP):
            total = blocks[0] * flux[side, 0, start + i, f:f + 1, :]
            for q in range(1, quants):
                total = total + blocks[q] * flux[side, q, start + i, f:f + 1, :]
            totals[i].append(total)
    return [jnp.concatenate(total, axis=0) for total in totals]


def fill_projector(projector, padded):
    modes, faces, basis = projector.shape
    padded[...] = jnp.zeros(padded.shape, F32)
    for f in range(faces):
        for m in range(modes):
            padded[f * ROWS + m:f * ROWS + m + 1, 0:basis] = projector[m, f:f + 1, :]


def predict(stiff_fold, jac, state, stiffened, first, second, basis, quants, lanes):
    for start in range(0, quants, GROUP):
        values = [state(q) for q in range(start, start + GROUP)]
        stiffen(stiff_fold, values, stiffened.at[0], start, lanes)
    for order in range(1, ORDER):
        factor = 1.0 / math.factorial(order + 1)

        def take(start, totals):
            if order + 1 < ORDER:
                stiffen(stiff_fold, totals, stiffened.at[order % 2], start, lanes)
            for p, total in enumerate(totals, start):
                first[p] = first[p] + factor * total
                if second is not None:
                    second[p] = second[p] + (2.0 ** (order + 1) - 1.0) * factor * total

        mix_jacobians(stiffened.at[(order - 1) % 2], jac, basis, quants, lanes, take)


def dense_rows(quants, modes):
    return -(-quants * modes // 32) * 32


def project_table(padded, field, table, dense, basis, quants, lanes, modes):
    fold = fold_columns(padded[:, 0:basis])
    last = dense.shape[0]
    dense[last - 8:last] = jnp.zeros((8, dense.shape[1]), F32)
    for start in range(0, quants, GROUP):
        values = [fold_rows(field(q)) for q in range(start, start + GROUP)]
        flat = dot(fold, jnp.concatenate(values, axis=1))
        for q in range(start, start + GROUP):
            for f in range(4):
                block = flat[f * ROWS:(f + 1) * ROWS, (q - start) * lanes:(q - start + 1) * lanes]
                columns = slice(f * lanes, (f + 1) * lanes)
                table[q * ROWS:(q + 1) * ROWS, columns] = block
                dense[q * modes:(q + 1) * modes, columns] = block[0:modes]


def even_spot():
    return [lax.rem(lax.axis_index(axis), 2) == 0 for axis in ("dom", "sub")]


def send_choice(send_row, faces, lanes):
    low = jnp.broadcast_to(send_row[:, 0:lanes], (8, lanes))
    lane = iota((8, lanes), 1)
    turned = pltpu.roll(low, SLOTS_DOM, 1)
    high = send_row[:, 2 * SLOTS_DOM:2 * SLOTS_DOM + 2 * SLOTS_SUB]
    spread = jnp.broadcast_to(jnp.concatenate([high, high], axis=1), (8, lanes))
    moved = pltpu.roll(spread, SLOTS_SUB, 1)
    left = lax.rem(lane, 2 * SLOTS_SUB) < SLOTS_SUB
    pieces = [
        jnp.where(lane < SLOTS_DOM, low, turned),
        jnp.where(lane < SLOTS_DOM, turned, low),
        jnp.where(left, spread, moved),
        jnp.where(left, moved, spread),
    ]
    even_dom, even_sub = even_spot()
    pieces = [
        jnp.where(even_dom, pieces[1], pieces[0]),
        jnp.where(even_dom, pieces[0], pieces[1]),
        jnp.where(even_sub, pieces[3], pieces[2]),
        jnp.where(even_sub, pieces[2], pieces[3]),
    ]
    return one_hot(jnp.concatenate([piece[0:1] for piece in pieces], axis=1), 0, faces)


def pick_sends(dense, chosen, outs, lanes):
    sent = gather(dense[...], chosen)
    for k, count in enumerate(PACKING):
        out = outs[min(k, 2)]
        rows = sent.shape[0] // count
        values = sent[:, k * lanes:(k + 1) * lanes]
        spot = iota((rows, lanes), 1)
        packed = values[0:rows]
        for g in range(1, count):
            packed = jnp.where(
                spot >= g * (lanes // count), values[g * rows:(g + 1) * rows], packed
            )
        row = rows if k == 3 else 0
        out[row:row + rows] = packed


def spread_received(arrived, count, lanes):
    width = lanes // count
    place = iota(arrived.shape, 1)
    return jnp.concatenate(
        [
            jnp.where((place >= g * width) & (place < (g + 1) * width), arrived, 0.0)
            for g in range(count)
        ],
        axis=0,
    )


def pick_local(table, slot, faces):
    chosen = jnp.concatenate([one_hot(slot[f:f + 1], 0, faces) for f in range(4)], axis=1)
    return gather(table, chosen)


def received_choice(slot, faces, lanes):
    even_dom, even_sub = even_spot()
    starts = (
        jnp.where(even_dom, faces + SLOTS_DOM, faces),
        faces + 2 * SLOTS_DOM + jnp.where(even_sub, SLOTS_SUB, 0),
        jnp.where(even_dom, faces, faces + SLOTS_DOM),
        faces + 2 * SLOTS_DOM + jnp.where(even_sub, 0, SLOTS_SUB),
    )
    widths = (SLOTS_DOM, SLOTS_SUB, SLOTS_DOM, SLOTS_SUB)
    return jnp.concatenate(
        [
            jnp.concatenate(
                [one_hot(slot[f:f + 1], first, lanes, width) for f in range(4)], axis=1
            )
            for first, width in zip(starts, widths)
        ],
        axis=0,
    )


def add_received(picked, dom, sub, chosen, dense, quants, modes, lanes):
    pieces = zip((dom, sub), (PACKING[0], PACKING[2]))
    spread = jnp.concatenate(
        [spread_received(item, count, lanes) for item, count in pieces], axis=1
    )
    dense[...] = gather(spread, chosen)
    for q in range(quants):
        rows = slice(q * ROWS, q * ROWS + modes)
        picked[rows] = picked[rows] + dense[q * modes:(q + 1) * modes]


def add_early(picked, dom, near, chosen, dense, quants, modes, lanes):
    half = near.shape[0] // 2
    add_received(
        picked, dom[...], near[0:half], chosen[0:2 * lanes], dense, quants, modes, lanes
    )


def add_late(picked, dom, far, chosen, dense, quants, modes, lanes):
    spot, count = lax.axis_index("sub"), lax.axis_size("sub")
    met = jnp.where(lax.rem(spot, 2) == 0, spot > 0, spot < count - 1)
    piece = jnp.where(met, far[...], 0.0)
    add_received(
        picked, dom[...], piece, chosen[2 * lanes:4 * lanes], dense, quants, modes, lanes
    )


def lift_weights(lifting):
    basis, depth = lifting.shape
    rest = jnp.zeros((fold_step(basis) - basis, depth), F32)
    high, low = halves(jnp.concatenate([lifting, rest], axis=0))
    return jnp.concatenate([high, low], axis=0)


def lift(weights, high, low, basis):
    step = fold_step(basis)
    both = dot(weights, high)
    return both[0:basis] + both[step:step + basis] + dot(weights[0:step], low)[0:basis]


def local_update(
    base, integral, table, jac, turned_fold, flux, lifting, stiffened, part,
    basis, quants, lanes,
):
    for start in range(0, quants, GROUP):
        values = [integral(q) for q in range(start, start + GROUP)]
        stiffen(turned_fold, values, stiffened, start, lanes)
    weights = lift_weights(lifting)
    for start in range(0, quants, GROUP):
        solved = mix_faces(table, flux, 0, start, quants, lanes)
        high, low = halves(jnp.concatenate(solved, axis=1))
        own = lift(weights, high, low, basis)
        for i in range(GROUP):
            part[start + i] = base(start + i) - own[:, i * lanes:(i + 1) * lanes]

    def take(start, totals):
        for p, total in enumerate(totals, start):
            part[p] = part[p] + total

    mix_jacobians(stiffened, jac, basis, quants, lanes, take)


def near_lift(picked, flux, orient, lifting, quants, lanes, take):
    weights = lift_weights(lifting)
    masks = [
        jnp.concatenate(
            [
                jnp.broadcast_to(jnp.where(orient[f:f + 1] == o, 1.0, 0.0), (ROWS, lanes))
                for f in range(4)
            ],
            axis=0,
        ).astype(BF16)
        for o in range(3)
    ]
    for start in range(0, quants, GROUP):
        highs, lows = [], []
        for solved in mix_faces(picked, flux, 1, start, quants, lanes):
            high, low = halves(solved)
            highs.append(jnp.concatenate([high * mask for mask in masks], axis=0))
            lows.append(jnp.concatenate([low * mask for mask in masks], axis=0))
        near = lift(
            weights, jnp.concatenate(highs, axis=1), jnp.concatenate(lows, axis=1),
            lifting.shape[0],
        )
        for i in range(GROUP):
            take(start + i, near[:, i * lanes:(i + 1) * lanes])


def near_lifting(own_lifting, rotations):
    count, modes, _ = rotations.shape
    block = 4 * ROWS
    row, column = iota((modes, count * block), 0), iota((modes, count * block), 1)
    turned = jnp.zeros((modes, count * block), F32)
    for o in range(count):
        spot = (lax.rem(column, ROWS) == row) & (lax.div(column, block) == o)
        turned = turned + exact_dot(rotations[o], jnp.where(spot, 1.0, 0.0))
    row, column = iota((block, modes), 0), iota((block, modes), 1)
    tall = exact_dot(jnp.where(lax.rem(row, ROWS) == column, 1.0, 0.0), turned)
    row, column = iota(tall.shape, 0), iota(tall.shape, 1)
    same = lax.div(row, ROWS) == lax.div(lax.rem(column, block), ROWS)
    return exact_dot(own_lifting, jnp.where(same, tall, 0.0))


def first_kernel(*refs):
    inputs, refs = refs[:INPUTS], refs[INPUTS:]
    held, refs = refs[:INPUTS], refs[INPUTS:]
    first, second, table, padded, stiff_fold, choice, jac, *sends, stiffened, dense, arrivals = refs
    copies = [
        pltpu.make_async_copy(source, target, arrivals.at[k])
        for k, (source, target) in enumerate(zip(inputs, held))
    ]
    for copy in copies:
        copy.start()
    send_row, projector, stiffness, state, rows = held[:FIRST_USED]
    quants, basis, lanes = state.shape
    modes = projector.shape[0]
    copies[0].wait()
    choice[...] = send_choice(send_row, 4 * lanes, lanes)
    copies[1].wait()
    fill_projector(projector, padded)
    copies[2].wait()
    fold = fold_columns(jnp.concatenate([stiffness[d] for d in range(3)], axis=0))
    stiff_fold[...] = fold.astype(F32)
    copies[3].wait()
    for q in range(quants):
        value = state[q]
        first[q] = value
        second[q] = value
    copies[4].wait()
    for q in range(quants):
        for p in range(quants):
            for d in range(3):
                jac[(q * quants + p) * 3 + d] = jnp.broadcast_to(
                    rows[q, p, d:d + 1, :], (8, lanes)
                )
    predict(
        fold, jac, lambda q: state[q], stiffened, first, second, basis, quants, lanes
    )
    project_table(
        padded, lambda q: first[q], table, dense, basis, quants, lanes, modes
    )
    pick_sends(dense, choice[...], sends, lanes)
    for copy in copies[FIRST_USED:]:
        copy.wait()


def second_kernel(
    state, first, table, near, dom, jac, stiffness, padded, rotations, flux, slot,
    part, picked, lifting, turned_fold, choice,
    stiffened, dense,
):
    quants, basis, lanes = state.shape
    modes = rotations.shape[1]
    turned = jnp.concatenate([stiffness[d].T for d in range(3)], axis=0)
    fold = fold_columns(turned)
    turned_fold[...] = fold.astype(F32)
    own_lifting = padded[...].T[0:basis]
    lifting[...] = near_lifting(own_lifting, rotations)
    picked[...] = pick_local(table[...], slot, 4 * lanes)
    choice[...] = received_choice(slot, 4 * lanes, lanes)
    add_early(picked, dom, near, choice, dense, quants, modes, lanes)
    local_update(
        lambda p: state[p], lambda q: first[q], table, jac, fold, flux, own_lifting,
        stiffened, part, basis, quants, lanes,
    )


def third_kernel(
    state, first, second, part, picked_early, far, dom, rotations, jac, stiff_fold, padded, flux, orient, cluster, lifting, received, choice,
    middle, integral, picked, table, *refs,
):
    *sends, stiffened, dense = refs
    quants, basis, lanes = state.shape
    modes = rotations.shape[1]
    picked[...] = picked_early[...]
    add_late(picked, dom, far, received, dense, quants, modes, lanes)
    fine = cluster[...] == 0

    def take(p, near):
        value = jnp.where(fine, part[p] - near, state[p])
        middle[p] = value
        integral[p] = value

    near_lift(picked, flux, orient, lifting[...], quants, lanes, take)
    predict(
        stiff_fold[...].astype(BF16), jac, lambda q: middle[q], stiffened, integral, None,
        basis, quants, lanes,
    )
    project_table(
        padded, lambda q: jnp.where(fine, integral[q], second[q]), table, dense,
        basis, quants, lanes, modes,
    )
    for q in range(quants):
        integral[q] = jnp.where(fine, integral[q], first[q] + second[q])
    pick_sends(dense, choice[...], sends, lanes)


def fourth_kernel(
    middle, integral, table_one, table_two, picked_one, near, dom, jac, turned_fold, padded,
    rotations, flux, slot, cluster, received,
    part, picked,
    stiffened, dense, total_table,
):
    quants, basis, lanes = middle.shape
    modes = rotations.shape[1]
    own_lifting = padded[...].T[0:basis]
    coarse = jnp.concatenate([cluster[...] != 0] * 4, axis=1)
    total_table[...] = table_two[...] + jnp.where(coarse, table_one[...], 0.0)
    picked[...] = pick_local(table_two[...], slot, 4 * lanes) + jnp.where(
        coarse, picked_one[...], 0.0
    )
    add_early(picked, dom, near, received, dense, quants, modes, lanes)
    local_update(
        lambda p: middle[p], lambda q: integral[q], total_table, jac,
        turned_fold[...].astype(BF16), flux, own_lifting,
        stiffened, part, basis, quants, lanes,
    )


def fifth_kernel(
    part, picked_early, far, dom, rotations, flux, orient, lifting, received, yield_stress,
    updated,
    picked, dense,
):
    quants, basis, lanes = part.shape
    modes = rotations.shape[1]
    picked[...] = picked_early[...]
    add_late(picked, dom, far, received, dense, quants, modes, lanes)
    stepped = [None] * quants

    def take(p, near):
        stepped[p] = part[p] - near

    near_lift(picked, flux, orient, lifting[...], quants, lanes, take)
    mean_part = (stepped[0] + stepped[1] + stepped[2]) / 3.0
    spread = [stepped[q] - mean_part for q in range(3)]
    normal = [item[0:1] for item in spread]
    shear = [stepped[q][0:1] for q in range(3, 6)]
    second_inv = 0.5 * (normal[0] ** 2 + normal[1] ** 2 + normal[2] ** 2) + (
        shear[0] ** 2 + shear[1] ** 2 + shear[2] ** 2
    )
    limit = yield_stress[...]
    scaling = limit / jnp.maximum(jnp.sqrt(second_inv), limit)
    for q in range(3):
        updated[q] = mean_part + scaling * spread[q]
    for q in range(3, 6):
        updated[q] = scaling * stepped[q]
    for q in range(6, quants):
        updated[q] = stepped[q]


def run(body, outs, scratch, *operands, space=pltpu.VMEM):
    vmem = pl.BlockSpec(memory_space=pltpu.VMEM)
    return pl.pallas_call(
        body,
        out_shape=[
            out if isinstance(out, jax.ShapeDtypeStruct) else jax.ShapeDtypeStruct(out, F32)
            for out in outs
        ],
        in_specs=[pl.BlockSpec(memory_space=space)] * len(operands),
        out_specs=[vmem] * len(outs),
        scratch_shapes=scratch,
        compiler_params=pltpu.CompilerParams(vmem_limit_bytes=32 * 1024 * 1024),
        name=body.__name__,
    )(*operands)


def hand_on(near, dom, onward):
    rows = onward.shape[0]
    onward[...] = near[rows:2 * rows]


def exchange(sends):
    def swap(value, axis, first):
        lower = range(first, lax.axis_size(axis) - 1, 2)
        return lax.ppermute(
            value, axis, [(i, i + 1) for i in lower] + [(i + 1, i) for i in lower]
        )

    count = lax.axis_size("sub")
    near = swap(sends[2], "sub", 0)
    dom_even = swap(sends[0], "dom", 0)
    kept, = run(hand_on, [(near.shape[0] // 2, near.shape[1])], [], near, dom_even)
    onward = [(i, (i + (2 if i % 2 == 0 else -2)) % count) for i in range(count)]
    far = lax.ppermute(kept, "sub", onward)
    dom_odd = swap(sends[1], "dom", 1)
    return (near, dom_even), (far, dom_odd)


def on_device(
    modal_state,
    stiffness,
    jacobians,
    flux_solvers,
    projector,
    rotations,
    yield_stress,
    cluster,
    orient,
    neighbour_slot,
    send_map,
):
    basis, quants, lanes = modal_state.shape
    inputs = [
        send_map.reshape(1, -1),
        jnp.transpose(projector, (1, 0, 2)),
        stiffness,
        jnp.transpose(modal_state, (1, 0, 2)),
        jnp.transpose(jacobians, (1, 2, 0, 3)),
        jnp.transpose(flux_solvers, (0, 2, 3, 1, 4)),
        rotations,
        neighbour_slot,
        orient,
        cluster.reshape(1, lanes),
        yield_stress.reshape(1, lanes),
    ]
    inputs = [pltpu.with_memory_space_constraint(item, pltpu.HBM) for item in inputs]
    held = [jax.ShapeDtypeStruct(item.shape, item.dtype) for item in inputs]

    field = (quants, basis, lanes)
    table = (quants * ROWS, 4 * lanes)
    rows = dense_rows(quants, projector.shape[1])
    dense = pltpu.VMEM((rows, 4 * lanes), F32)
    messages = [(rows // 2, lanes)] * 3
    choice = jax.ShapeDtypeStruct((4 * lanes, 4 * lanes), BF16)
    flat = quants * lanes
    fold = (3 * basis, 3 * fold_step(basis))
    stiffened = pltpu.VMEM((3 * basis, flat), F32)
    two_stiffened = pltpu.VMEM((2, 3 * basis, flat), F32)

    outs = run(
        first_kernel,
        held + [field, field, table, (4 * ROWS, 128), fold, choice, (3 * quants * quants, 8, lanes)] + messages,
        [two_stiffened, dense, pltpu.SemaphoreType.DMA((INPUTS,))],
        *inputs, space=pl.ANY,
    )
    _, _, stiff, state, _, flux, turns, slot, orient, cluster, limit = outs[:INPUTS]
    first, second, table_one, padded, stiff_fold, sending, jac, *sends = outs[INPUTS:]
    early, late = exchange(sends)
    part_one, local_one, lifting, turned_fold, received = run(
        second_kernel, [field, table, (basis, 3 * 4 * ROWS), fold, choice], [stiffened, dense],
        state, first, table_one, *early, jac, stiff, padded, turns, flux, slot,
    )
    middle, integral, picked_one, table_two, *sends = run(
        third_kernel, [field, field, table, table] + messages, [two_stiffened, dense],
        state, first, second, part_one, local_one, *late, turns,
        jac, stiff_fold, padded, flux, orient, cluster, lifting, received, sending,
    )
    early, late = exchange(sends)
    part_two, local_two = run(
        fourth_kernel, [field, table], [stiffened, dense, pltpu.VMEM(table, F32)],
        middle, integral, table_one, table_two, picked_one, *early, jac, turned_fold, padded,
        turns, flux, slot, cluster, received,
    )
    updated, = run(
        fifth_kernel, [field], [pltpu.VMEM(table, F32), dense],
        part_two, local_two, *late, turns, flux, orient, lifting, received, limit,
    )
    return jnp.transpose(updated, (1, 0, 2))


def solution(mesh):
    placed = (
        P(None, None, ("dom", "sub")),
        P(),
        P(None, None, None, ("dom", "sub")),
        P(None, None, None, None, ("dom", "sub")),
        P(),
        P(),
        P(("dom", "sub")),
        P(("dom", "sub")),
        P(None, ("dom", "sub")),
        P(None, ("dom", "sub")),
        P(("dom", "sub")),
    )
    return jax.shard_map(
        on_device,
        mesh=mesh,
        in_specs=placed,
        out_specs=P(None, None, ("dom", "sub")),
        check_vma=False,
    )
```

```python
import math

import jax
import jax.numpy as jnp
from jax import lax
from jax.experimental import pallas as pl
from jax.experimental.pallas import tpu as pltpu
from jax.sharding import PartitionSpec as P

ORDER = 6
SLOTS_DOM = 64
SLOTS_SUB = 32
ROWS = 24
GROUP = 3

F32 = jnp.float32
BF16 = jnp.bfloat16
EXACT = lax.Precision.HIGHEST

PACKING = (2, 2, 4, 4)

INPUTS = 11
FIRST_USED = 5


def iota(shape, dim):
    return lax.broadcasted_iota(jnp.int32, shape, dim)


def dot(a, b):
    return jnp.dot(a, b, preferred_element_type=F32)


def exact_dot(a, b):
    return jnp.dot(a, b, precision=EXACT, preferred_element_type=F32)


def halves(value):
    high = value.astype(BF16)
    return high, (value - high.astype(F32)).astype(BF16)


def one_hot(index_row, first, count, modulus=None):
    number = iota((count, index_row.shape[1]), 0)
    if modulus is not None:
        number = lax.rem(number, modulus)
    return jnp.where(number + first == index_row, 1.0, 0.0).astype(BF16)


def stack_rows(value):
    high = value.astype(BF16).astype(F32)
    return jnp.concatenate([high, value - high], axis=0).astype(BF16)


def gather(table, chosen):
    rows = table.shape[0]
    both = dot(stack_rows(table), chosen)
    return both[0:rows] + both[rows:2 * rows]


def fold_step(basis):
    return -(-basis // 16) * 16


def fold_rows(value):
    basis, lanes = value.shape
    rest = jnp.zeros((fold_step(basis) - basis, lanes), F32)
    value = jnp.concatenate([value, rest], axis=0)
    high, low = halves(value)
    return jnp.concatenate([high, high, low], axis=0)


def fold_columns(matrix):
    basis = matrix.shape[1]
    step = fold_step(basis)
    high, low = halves(matrix)
    row, column = iota((basis, 3 * step), 0), iota((basis, 3 * step), 1)
    outer = jnp.where((column == row) | (column == row + 2 * step), 1.0, 0.0).astype(BF16)
    inner = jnp.where(column == row + step, 1.0, 0.0).astype(BF16)
    return (dot(high, outer) + dot(low, inner)).astype(BF16)


def stiffen(stiff_fold, values, target, start, lanes):
    folded = jnp.concatenate([fold_rows(value) for value in values], axis=1)
    target[:, start * lanes:(start + len(values)) * lanes] = dot(stiff_fold, folded)


def mix_jacobians(stiffened, jac, basis, quants, lanes, take):
    for start in range(0, quants, GROUP):
        totals = [None] * GROUP
        for q in range(quants):
            for d in range(3):
                block = stiffened[d * basis:(d + 1) * basis, q * lanes:(q + 1) * lanes]
                for i in range(GROUP):
                    term = block * jac[q, start + i, d:d + 1, :]
                    totals[i] = term if totals[i] is None else totals[i] + term
        take(start, totals)


def mix_faces(table, flux, side, start, quants, lanes):
    totals = [[] for _ in range(GROUP)]
    for f in range(4):
        blocks = [
            table[q * ROWS:(q + 1) * ROWS, f * lanes:(f + 1) * lanes] for q in range(quants)
        ]
        for i in range(GROUP):
            total = blocks[0] * flux[side, 0, start + i, f:f + 1, :]
            for q in range(1, quants):
                total = total + blocks[q] * flux[side, q, start + i, f:f + 1, :]
            totals[i].append(total)
    return [jnp.concatenate(total, axis=0) for total in totals]


def fill_projector(projector, padded):
    modes, faces, basis = projector.shape
    padded[...] = jnp.zeros(padded.shape, F32)
    for f in range(faces):
        for m in range(modes):
            padded[f * ROWS + m:f * ROWS + m + 1, 0:basis] = projector[m, f:f + 1, :]


def predict(stiff_fold, jac, state, stiffened, first, second, basis, quants, lanes):
    for start in range(0, quants, GROUP):
        values = [state(q) for q in range(start, start + GROUP)]
        stiffen(stiff_fold, values, stiffened.at[0], start, lanes)
    for order in range(1, ORDER):
        factor = 1.0 / math.factorial(order + 1)

        def take(start, totals):
            if order + 1 < ORDER:
                stiffen(stiff_fold, totals, stiffened.at[order % 2], start, lanes)
            for p, total in enumerate(totals, start):
                first[p] = first[p] + factor * total
                if second is not None:
                    second[p] = second[p] + (2.0 ** (order + 1) - 1.0) * factor * total

        mix_jacobians(stiffened.at[(order - 1) % 2], jac, basis, quants, lanes, take)


def dense_rows(quants, modes):
    return -(-quants * modes // 32) * 32


def project_table(padded, field, table, dense, basis, quants, lanes, modes):
    fold = fold_columns(padded[:, 0:basis])
    last = dense.shape[0]
    dense[last - 8:last] = jnp.zeros((8, dense.shape[1]), F32)
    for start in range(0, quants, GROUP):
        values = [fold_rows(field(q)) for q in range(start, start + GROUP)]
        flat = dot(fold, jnp.concatenate(values, axis=1))
        for q in range(start, start + GROUP):
            for f in range(4):
                block = flat[f * ROWS:(f + 1) * ROWS, (q - start) * lanes:(q - start + 1) * lanes]
                columns = slice(f * lanes, (f + 1) * lanes)
                table[q * ROWS:(q + 1) * ROWS, columns] = block
                dense[q * modes:(q + 1) * modes, columns] = block[0:modes]


def even_spot():
    return [lax.rem(lax.axis_index(axis), 2) == 0 for axis in ("dom", "sub")]


def send_choice(send_row, faces, lanes):
    low = jnp.broadcast_to(send_row[:, 0:lanes], (8, lanes))
    lane = iota((8, lanes), 1)
    turned = pltpu.roll(low, SLOTS_DOM, 1)
    high = send_row[:, 2 * SLOTS_DOM:2 * SLOTS_DOM + 2 * SLOTS_SUB]
    spread = jnp.broadcast_to(jnp.concatenate([high, high], axis=1), (8, lanes))
    moved = pltpu.roll(spread, SLOTS_SUB, 1)
    left = lax.rem(lane, 2 * SLOTS_SUB) < SLOTS_SUB
    pieces = [
        jnp.where(lane < SLOTS_DOM, low, turned),
        jnp.where(lane < SLOTS_DOM, turned, low),
        jnp.where(left, spread, moved),
        jnp.where(left, moved, spread),
    ]
    even_dom, even_sub = even_spot()
    pieces = [
        jnp.where(even_dom, pieces[1], pieces[0]),
        jnp.where(even_dom, pieces[0], pieces[1]),
        jnp.where(even_sub, pieces[3], pieces[2]),
        jnp.where(even_sub, pieces[2], pieces[3]),
    ]
    return one_hot(jnp.concatenate([piece[0:1] for piece in pieces], axis=1), 0, faces)


def pick_sends(dense, chosen, outs, lanes):
    sent = gather(dense[...], chosen)
    for k, count in enumerate(PACKING):
        out = outs[min(k, 2)]
        rows = sent.shape[0] // count
        values = sent[:, k * lanes:(k + 1) * lanes]
        spot = iota((rows, lanes), 1)
        packed = values[0:rows]
        for g in range(1, count):
            packed = jnp.where(
                spot >= g * (lanes // count), values[g * rows:(g + 1) * rows], packed
            )
        row = rows if k == 3 else 0
        out[row:row + rows] = packed


def spread_received(arrived, count, lanes):
    width = lanes // count
    place = iota(arrived.shape, 1)
    return jnp.concatenate(
        [
            jnp.where((place >= g * width) & (place < (g + 1) * width), arrived, 0.0)
            for g in range(count)
        ],
        axis=0,
    )


def pick_local(table, slot, faces):
    chosen = jnp.concatenate([one_hot(slot[f:f + 1], 0, faces) for f in range(4)], axis=1)
    return gather(table, chosen)


def received_choice(slot, faces, lanes):
    even_dom, even_sub = even_spot()
    starts = (
        jnp.where(even_dom, faces + SLOTS_DOM, faces),
        faces + 2 * SLOTS_DOM + jnp.where(even_sub, SLOTS_SUB, 0),
        jnp.where(even_dom, faces, faces + SLOTS_DOM),
        faces + 2 * SLOTS_DOM + jnp.where(even_sub, 0, SLOTS_SUB),
    )
    widths = (SLOTS_DOM, SLOTS_SUB, SLOTS_DOM, SLOTS_SUB)
    return jnp.concatenate(
        [
            jnp.concatenate(
                [one_hot(slot[f:f + 1], first, lanes, width) for f in range(4)], axis=1
            )
            for first, width in zip(starts, widths)
        ],
        axis=0,
    )


def add_received(picked, dom, sub, chosen, dense, quants, modes, lanes):
    pieces = zip((dom, sub), (PACKING[0], PACKING[2]))
    spread = jnp.concatenate(
        [spread_received(item, count, lanes) for item, count in pieces], axis=1
    )
    dense[...] = gather(spread, chosen)
    for q in range(quants):
        rows = slice(q * ROWS, q * ROWS + modes)
        picked[rows] = picked[rows] + dense[q * modes:(q + 1) * modes]


def add_early(picked, dom, near, chosen, dense, quants, modes, lanes):
    half = near.shape[0] // 2
    add_received(
        picked, dom[...], near[0:half], chosen[0:2 * lanes], dense, quants, modes, lanes
    )


def add_late(picked, dom, far, chosen, dense, quants, modes, lanes):
    spot, count = lax.axis_index("sub"), lax.axis_size("sub")
    met = jnp.where(lax.rem(spot, 2) == 0, spot > 0, spot < count - 1)
    piece = jnp.where(met, far[...], 0.0)
    add_received(
        picked, dom[...], piece, chosen[2 * lanes:4 * lanes], dense, quants, modes, lanes
    )


def lift_weights(lifting):
    basis, depth = lifting.shape
    rest = jnp.zeros((fold_step(basis) - basis, depth), F32)
    high, low = halves(jnp.concatenate([lifting, rest], axis=0))
    return jnp.concatenate([high, low], axis=0)


def lift(weights, high, low, basis):
    step = fold_step(basis)
    both = dot(weights, high)
    return both[0:basis] + both[step:step + basis] + dot(weights[0:step], low)[0:basis]


def local_update(
    base, integral, table, jac, turned_fold, flux, lifting, stiffened, part,
    basis, quants, lanes,
):
    for start in range(0, quants, GROUP):
        values = [integral(q) for q in range(start, start + GROUP)]
        stiffen(turned_fold, values, stiffened, start, lanes)
    weights = lift_weights(lifting)
    for start in range(0, quants, GROUP):
        solved = mix_faces(table, flux, 0, start, quants, lanes)
        high, low = halves(jnp.concatenate(solved, axis=1))
        own = lift(weights, high, low, basis)
        for i in range(GROUP):
            part[start + i] = base(start + i) - own[:, i * lanes:(i + 1) * lanes]

    def take(start, totals):
        for p, total in enumerate(totals, start):
            part[p] = part[p] + total

    mix_jacobians(stiffened, jac, basis, quants, lanes, take)


def near_lift(picked, flux, orient, lifting, quants, lanes, take):
    weights = lift_weights(lifting)
    masks = [
        jnp.concatenate(
            [
                jnp.broadcast_to(jnp.where(orient[f:f + 1] == o, 1.0, 0.0), (ROWS, lanes))
                for f in range(4)
            ],
            axis=0,
        ).astype(BF16)
        for o in range(3)
    ]
    for start in range(0, quants, GROUP):
        highs, lows = [], []
        for solved in mix_faces(picked, flux, 1, start, quants, lanes):
            high, low = halves(solved)
            highs.append(jnp.concatenate([high * mask for mask in masks], axis=0))
            lows.append(jnp.concatenate([low * mask for mask in masks], axis=0))
        near = lift(
            weights, jnp.concatenate(highs, axis=1), jnp.concatenate(lows, axis=1),
            lifting.shape[0],
        )
        for i in range(GROUP):
            take(start + i, near[:, i * lanes:(i + 1) * lanes])


def near_lifting(own_lifting, rotations):
    count, modes, _ = rotations.shape
    block = 4 * ROWS
    row, column = iota((modes, count * block), 0), iota((modes, count * block), 1)
    turned = jnp.zeros((modes, count * block), F32)
    for o in range(count):
        spot = (lax.rem(column, ROWS) == row) & (lax.div(column, block) == o)
        turned = turned + exact_dot(rotations[o], jnp.where(spot, 1.0, 0.0))
    row, column = iota((block, modes), 0), iota((block, modes), 1)
    tall = exact_dot(jnp.where(lax.rem(row, ROWS) == column, 1.0, 0.0), turned)
    row, column = iota(tall.shape, 0), iota(tall.shape, 1)
    same = lax.div(row, ROWS) == lax.div(lax.rem(column, block), ROWS)
    return exact_dot(own_lifting, jnp.where(same, tall, 0.0))


def first_kernel(*refs):
    inputs, refs = refs[:INPUTS], refs[INPUTS:]
    held, refs = refs[:INPUTS], refs[INPUTS:]
    first, second, table, padded, stiff_fold, choice, *sends, stiffened, dense, arrivals = refs
    copies = [
        pltpu.make_async_copy(source, target, arrivals.at[k])
        for k, (source, target) in enumerate(zip(inputs, held))
    ]
    for copy in copies:
        copy.start()
    send_row, projector, stiffness, state, jac = held[:FIRST_USED]
    quants, basis, lanes = state.shape
    modes = projector.shape[0]
    copies[0].wait()
    choice[...] = send_choice(send_row, 4 * lanes, lanes)
    copies[1].wait()
    fill_projector(projector, padded)
    copies[2].wait()
    fold = fold_columns(jnp.concatenate([stiffness[d] for d in range(3)], axis=0))
    stiff_fold[...] = fold.astype(F32)
    copies[3].wait()
    for q in range(quants):
        value = state[q]
        first[q] = value
        second[q] = value
    copies[4].wait()
    predict(
        fold, jac, lambda q: state[q], stiffened, first, second, basis, quants, lanes
    )
    project_table(
        padded, lambda q: first[q], table, dense, basis, quants, lanes, modes
    )
    pick_sends(dense, choice[...], sends, lanes)
    for copy in copies[FIRST_USED:]:
        copy.wait()


def second_kernel(
    state, first, table, dom, near, jac, stiffness, padded, rotations, flux, slot,
    part, picked, lifting, turned_fold, choice,
    stiffened, dense,
):
    quants, basis, lanes = state.shape
    modes = rotations.shape[1]
    turned = jnp.concatenate([stiffness[d].T for d in range(3)], axis=0)
    fold = fold_columns(turned)
    turned_fold[...] = fold.astype(F32)
    own_lifting = padded[...].T[0:basis]
    lifting[...] = near_lifting(own_lifting, rotations)
    picked[...] = pick_local(table[...], slot, 4 * lanes)
    choice[...] = received_choice(slot, 4 * lanes, lanes)
    add_early(picked, dom, near, choice, dense, quants, modes, lanes)
    local_update(
        lambda p: state[p], lambda q: first[q], table, jac, fold, flux, own_lifting,
        stiffened, part, basis, quants, lanes,
    )


def third_kernel(
    state, first, second, part, picked_early, far, dom, rotations, jac, stiff_fold, padded, flux, orient, cluster, lifting, received, choice,
    middle, integral, picked, table, *refs,
):
    *sends, stiffened, dense = refs
    quants, basis, lanes = state.shape
    modes = rotations.shape[1]
    picked[...] = picked_early[...]
    add_late(picked, dom, far, received, dense, quants, modes, lanes)
    fine = cluster[...] == 0

    def take(p, near):
        value = jnp.where(fine, part[p] - near, state[p])
        middle[p] = value
        integral[p] = value

    near_lift(picked, flux, orient, lifting[...], quants, lanes, take)
    predict(
        stiff_fold[...].astype(BF16), jac, lambda q: middle[q], stiffened, integral, None,
        basis, quants, lanes,
    )
    project_table(
        padded, lambda q: jnp.where(fine, integral[q], second[q]), table, dense,
        basis, quants, lanes, modes,
    )
    for q in range(quants):
        integral[q] = jnp.where(fine, integral[q], first[q] + second[q])
    pick_sends(dense, choice[...], sends, lanes)


def fourth_kernel(
    middle, integral, table_one, table_two, picked_one, dom, near, jac, turned_fold, padded,
    rotations, flux, slot, cluster, received,
    part, picked,
    stiffened, dense, total_table,
):
    quants, basis, lanes = middle.shape
    modes = rotations.shape[1]
    own_lifting = padded[...].T[0:basis]
    coarse = jnp.concatenate([cluster[...] != 0] * 4, axis=1)
    total_table[...] = table_two[...] + jnp.where(coarse, table_one[...], 0.0)
    picked[...] = pick_local(table_two[...], slot, 4 * lanes) + jnp.where(
        coarse, picked_one[...], 0.0
    )
    add_early(picked, dom, near, received, dense, quants, modes, lanes)
    local_update(
        lambda p: middle[p], lambda q: integral[q], total_table, jac,
        turned_fold[...].astype(BF16), flux, own_lifting,
        stiffened, part, basis, quants, lanes,
    )


def fifth_kernel(
    part, picked_early, far, dom, rotations, flux, orient, lifting, received, yield_stress,
    updated,
    picked, dense,
):
    quants, basis, lanes = part.shape
    modes = rotations.shape[1]
    picked[...] = picked_early[...]
    add_late(picked, dom, far, received, dense, quants, modes, lanes)
    stepped = [None] * quants

    def take(p, near):
        stepped[p] = part[p] - near

    near_lift(picked, flux, orient, lifting[...], quants, lanes, take)
    mean_part = (stepped[0] + stepped[1] + stepped[2]) / 3.0
    spread = [stepped[q] - mean_part for q in range(3)]
    normal = [item[0:1] for item in spread]
    shear = [stepped[q][0:1] for q in range(3, 6)]
    second_inv = 0.5 * (normal[0] ** 2 + normal[1] ** 2 + normal[2] ** 2) + (
        shear[0] ** 2 + shear[1] ** 2 + shear[2] ** 2
    )
    limit = yield_stress[...]
    scaling = limit / jnp.maximum(jnp.sqrt(second_inv), limit)
    for q in range(3):
        updated[q] = mean_part + scaling * spread[q]
    for q in range(3, 6):
        updated[q] = scaling * stepped[q]
    for q in range(6, quants):
        updated[q] = stepped[q]


def run(body, outs, scratch, *operands, space=pltpu.VMEM):
    vmem = pl.BlockSpec(memory_space=pltpu.VMEM)
    return pl.pallas_call(
        body,
        out_shape=[
            out if isinstance(out, jax.ShapeDtypeStruct) else jax.ShapeDtypeStruct(out, F32)
            for out in outs
        ],
        in_specs=[pl.BlockSpec(memory_space=space)] * len(operands),
        out_specs=[vmem] * len(outs),
        scratch_shapes=scratch,
        compiler_params=pltpu.CompilerParams(vmem_limit_bytes=32 * 1024 * 1024),
        name=body.__name__,
    )(*operands)


def hand_on(near, dom, onward):
    rows = onward.shape[0]
    onward[...] = near[rows:2 * rows]


def exchange(sends):
    def swap(value, axis, first):
        lower = range(first, lax.axis_size(axis) - 1, 2)
        return lax.ppermute(
            value, axis, [(i, i + 1) for i in lower] + [(i + 1, i) for i in lower]
        )

    count = lax.axis_size("sub")
    near = swap(sends[2], "sub", 0)
    dom_even = swap(sends[0], "dom", 0)
    kept, = run(hand_on, [(near.shape[0] // 2, near.shape[1])], [], near, dom_even)
    onward = [(i, (i + (2 if i % 2 == 0 else -2)) % count) for i in range(count)]
    far = lax.ppermute(kept, "sub", onward)
    dom_odd = swap(sends[1], "dom", 1)
    return (dom_even, near), (far, dom_odd)


def on_device(
    modal_state,
    stiffness,
    jacobians,
    flux_solvers,
    projector,
    rotations,
    yield_stress,
    cluster,
    orient,
    neighbour_slot,
    send_map,
):
    basis, quants, lanes = modal_state.shape
    inputs = [
        send_map.reshape(1, -1),
        jnp.transpose(projector, (1, 0, 2)),
        stiffness,
        jnp.transpose(modal_state, (1, 0, 2)),
        jnp.transpose(jacobians, (1, 2, 0, 3)),
        jnp.transpose(flux_solvers, (0, 2, 3, 1, 4)),
        rotations,
        neighbour_slot,
        orient,
        cluster.reshape(1, lanes),
        yield_stress.reshape(1, lanes),
    ]
    inputs = [pltpu.with_memory_space_constraint(item, pltpu.HBM) for item in inputs]
    held = [jax.ShapeDtypeStruct(item.shape, item.dtype) for item in inputs]

    field = (quants, basis, lanes)
    table = (quants * ROWS, 4 * lanes)
    rows = dense_rows(quants, projector.shape[1])
    dense = pltpu.VMEM((rows, 4 * lanes), F32)
    messages = [(rows // 2, lanes)] * 3
    choice = jax.ShapeDtypeStruct((4 * lanes, 4 * lanes), BF16)
    flat = quants * lanes
    fold = (3 * basis, 3 * fold_step(basis))
    stiffened = pltpu.VMEM((3 * basis, flat), F32)
    two_stiffened = pltpu.VMEM((2, 3 * basis, flat), F32)

    outs = run(
        first_kernel,
        held + [field, field, table, (4 * ROWS, 128), fold, choice] + messages,
        [two_stiffened, dense, pltpu.SemaphoreType.DMA((INPUTS,))],
        *inputs, space=pl.ANY,
    )
    _, _, stiff, state, jac, flux, turns, slot, orient, cluster, limit = outs[:INPUTS]
    first, second, table_one, padded, stiff_fold, sending, *sends = outs[INPUTS:]
    early, late = exchange(sends)
    part_one, local_one, lifting, turned_fold, received = run(
        second_kernel, [field, table, (basis, 3 * 4 * ROWS), fold, choice], [stiffened, dense],
        state, first, table_one, *early, jac, stiff, padded, turns, flux, slot,
    )
    middle, integral, picked_one, table_two, *sends = run(
        third_kernel, [field, field, table, table] + messages, [two_stiffened, dense],
        state, first, second, part_one, local_one, *late, turns,
        jac, stiff_fold, padded, flux, orient, cluster, lifting, received, sending,
    )
    early, late = exchange(sends)
    part_two, local_two = run(
        fourth_kernel, [field, table], [stiffened, dense, pltpu.VMEM(table, F32)],
        middle, integral, table_one, table_two, picked_one, *early, jac, turned_fold, padded,
        turns, flux, slot, cluster, received,
    )
    updated, = run(
        fifth_kernel, [field], [pltpu.VMEM(table, F32), dense],
        part_two, local_two, *late, turns, flux, orient, lifting, received, limit,
    )
    return jnp.transpose(updated, (1, 0, 2))


def solution(mesh):
    placed = (
        P(None, None, ("dom", "sub")),
        P(),
        P(None, None, None, ("dom", "sub")),
        P(None, None, None, None, ("dom", "sub")),
        P(),
        P(),
        P(("dom", "sub")),
        P(("dom", "sub")),
        P(None, ("dom", "sub")),
        P(None, ("dom", "sub")),
        P(("dom", "sub")),
    )
    return jax.shard_map(
        on_device,
        mesh=mesh,
        in_specs=placed,
        out_specs=P(None, None, ("dom", "sub")),
        check_vma=False,
    )
```

```python
import math

import jax
import jax.numpy as jnp
from jax import lax
from jax.experimental import pallas as pl
from jax.experimental.pallas import tpu as pltpu
from jax.sharding import PartitionSpec as P

ORDER = 6
SLOTS_DOM = 64
SLOTS_SUB = 32
ROWS = 24
GROUP = 3

F32 = jnp.float32
BF16 = jnp.bfloat16
EXACT = lax.Precision.HIGHEST

PACKING = (2, 2, 4, 4)

INPUTS = 11
FIRST_USED = 5


def iota(shape, dim):
    return lax.broadcasted_iota(jnp.int32, shape, dim)


def dot(a, b):
    return jnp.dot(a, b, preferred_element_type=F32)


def exact_dot(a, b):
    return jnp.dot(a, b, precision=EXACT, preferred_element_type=F32)


def halves(value):
    high = value.astype(BF16)
    return high, (value - high.astype(F32)).astype(BF16)


def one_hot(index_row, first, count, modulus=None):
    number = iota((count, index_row.shape[1]), 0)
    if modulus is not None:
        number = lax.rem(number, modulus)
    return jnp.where(number + first == index_row, 1.0, 0.0).astype(BF16)


def stack_rows(value):
    high = value.astype(BF16).astype(F32)
    return jnp.concatenate([high, value - high], axis=0).astype(BF16)


def gather(table, chosen):
    rows = table.shape[0]
    both = dot(stack_rows(table), chosen)
    return both[0:rows] + both[rows:2 * rows]


def fold_step(basis):
    return -(-basis // 16) * 16


def fold_rows(value):
    basis, lanes = value.shape
    rest = jnp.zeros((fold_step(basis) - basis, lanes), F32)
    value = jnp.concatenate([value, rest], axis=0)
    high, low = halves(value)
    return jnp.concatenate([high, high, low], axis=0)


def fold_columns(matrix):
    basis = matrix.shape[1]
    step = fold_step(basis)
    high, low = halves(matrix)
    row, column = iota((basis, 3 * step), 0), iota((basis, 3 * step), 1)
    outer = jnp.where((column == row) | (column == row + 2 * step), 1.0, 0.0).astype(BF16)
    inner = jnp.where(column == row + step, 1.0, 0.0).astype(BF16)
    return (dot(high, outer) + dot(low, inner)).astype(BF16)


def stiffen(stiff_fold, values, target, start, lanes):
    folded = jnp.concatenate([fold_rows(value) for value in values], axis=1)
    target[:, start * lanes:(start + len(values)) * lanes] = dot(stiff_fold, folded)


def mix_jacobians(stiffened, jac, basis, quants, lanes, take):
    for start in range(0, quants, GROUP):
        totals = [None] * GROUP
        for q in range(quants):
            for d in range(3):
                block = stiffened[d * basis:(d + 1) * basis, q * lanes:(q + 1) * lanes]
                for i in range(GROUP):
                    term = block * jac[q, start + i, d:d + 1, :]
                    totals[i] = term if totals[i] is None else totals[i] + term
        take(start, totals)


def mix_faces(table, flux, side, start, quants, lanes):
    totals = [[] for _ in range(GROUP)]
    for f in range(4):
        blocks = [
            table[q * ROWS:(q + 1) * ROWS, f * lanes:(f + 1) * lanes] for q in range(quants)
        ]
        for i in range(GROUP):
            total = blocks[0] * flux[side, 0, start + i, f:f + 1, :]
            for q in range(1, quants):
                total = total + blocks[q] * flux[side, q, start + i, f:f + 1, :]
            totals[i].append(total)
    return [jnp.concatenate(total, axis=0) for total in totals]


def fill_projector(projector, padded):
    modes, faces, basis = projector.shape
    padded[...] = jnp.zeros(padded.shape, F32)
    for f in range(faces):
        for m in range(modes):
            padded[f * ROWS + m:f * ROWS + m + 1, 0:basis] = projector[m, f:f + 1, :]


def predict(stiff_fold, jac, state, stiffened, first, second, basis, quants, lanes):
    for start in range(0, quants, GROUP):
        values = [state(q) for q in range(start, start + GROUP)]
        stiffen(stiff_fold, values, stiffened.at[0], start, lanes)
    for order in range(1, ORDER):
        factor = 1.0 / math.factorial(order + 1)

        def take(start, totals):
            if order + 1 < ORDER:
                stiffen(stiff_fold, totals, stiffened.at[order % 2], start, lanes)
            for p, total in enumerate(totals, start):
                before = state(p) if order == 1 else first[p]
                first[p] = before + factor * total
                if second is not None:
                    before = state(p) if order == 1 else second[p]
                    second[p] = before + (2.0 ** (order + 1) - 1.0) * factor * total

        mix_jacobians(stiffened.at[(order - 1) % 2], jac, basis, quants, lanes, take)


def dense_rows(quants, modes):
    return -(-quants * modes // 32) * 32


def project_table(padded, field, table, dense, basis, quants, lanes, modes):
    fold = fold_columns(padded[:, 0:basis])
    last = dense.shape[0]
    dense[last - 8:last] = jnp.zeros((8, dense.shape[1]), F32)
    for start in range(0, quants, GROUP):
        values = [fold_rows(field(q)) for q in range(start, start + GROUP)]
        flat = dot(fold, jnp.concatenate(values, axis=1))
        for q in range(start, start + GROUP):
            for f in range(4):
                block = flat[f * ROWS:(f + 1) * ROWS, (q - start) * lanes:(q - start + 1) * lanes]
                columns = slice(f * lanes, (f + 1) * lanes)
                table[q * ROWS:(q + 1) * ROWS, columns] = block
                dense[q * modes:(q + 1) * modes, columns] = block[0:modes]


def even_spot():
    return [lax.rem(lax.axis_index(axis), 2) == 0 for axis in ("dom", "sub")]


def send_choice(send_row, faces, lanes):
    low = jnp.broadcast_to(send_row[:, 0:lanes], (8, lanes))
    lane = iota((8, lanes), 1)
    turned = pltpu.roll(low, SLOTS_DOM, 1)
    high = send_row[:, 2 * SLOTS_DOM:2 * SLOTS_DOM + 2 * SLOTS_SUB]
    spread = jnp.broadcast_to(jnp.concatenate([high, high], axis=1), (8, lanes))
    moved = pltpu.roll(spread, SLOTS_SUB, 1)
    left = lax.rem(lane, 2 * SLOTS_SUB) < SLOTS_SUB
    pieces = [
        jnp.where(lane < SLOTS_DOM, low, turned),
        jnp.where(lane < SLOTS_DOM, turned, low),
        jnp.where(left, spread, moved),
        jnp.where(left, moved, spread),
    ]
    even_dom, even_sub = even_spot()
    pieces = [
        jnp.where(even_dom, pieces[1], pieces[0]),
        jnp.where(even_dom, pieces[0], pieces[1]),
        jnp.where(even_sub, pieces[3], pieces[2]),
        jnp.where(even_sub, pieces[2], pieces[3]),
    ]
    return one_hot(jnp.concatenate([piece[0:1] for piece in pieces], axis=1), 0, faces)


def pick_sends(dense, chosen, outs, lanes):
    sent = gather(dense[...], chosen)
    for k, count in enumerate(PACKING):
        out = outs[min(k, 2)]
        rows = sent.shape[0] // count
        values = sent[:, k * lanes:(k + 1) * lanes]
        spot = iota((rows, lanes), 1)
        packed = values[0:rows]
        for g in range(1, count):
            packed = jnp.where(
                spot >= g * (lanes // count), values[g * rows:(g + 1) * rows], packed
            )
        row = rows if k == 3 else 0
        out[row:row + rows] = packed


def spread_received(arrived, count, lanes):
    width = lanes // count
    place = iota(arrived.shape, 1)
    return jnp.concatenate(
        [
            jnp.where((place >= g * width) & (place < (g + 1) * width), arrived, 0.0)
            for g in range(count)
        ],
        axis=0,
    )


def pick_local(table, slot, faces):
    chosen = jnp.concatenate([one_hot(slot[f:f + 1], 0, faces) for f in range(4)], axis=1)
    return gather(table, chosen)


def received_choice(slot, faces, lanes):
    even_dom, even_sub = even_spot()
    starts = (
        jnp.where(even_dom, faces + SLOTS_DOM, faces),
        faces + 2 * SLOTS_DOM + jnp.where(even_sub, SLOTS_SUB, 0),
        jnp.where(even_dom, faces, faces + SLOTS_DOM),
        faces + 2 * SLOTS_DOM + jnp.where(even_sub, 0, SLOTS_SUB),
    )
    widths = (SLOTS_DOM, SLOTS_SUB, SLOTS_DOM, SLOTS_SUB)
    return jnp.concatenate(
        [
            jnp.concatenate(
                [one_hot(slot[f:f + 1], first, lanes, width) for f in range(4)], axis=1
            )
            for first, width in zip(starts, widths)
        ],
        axis=0,
    )


def add_received(picked, dom, sub, chosen, dense, quants, modes, lanes):
    pieces = zip((dom, sub), (PACKING[0], PACKING[2]))
    spread = jnp.concatenate(
        [spread_received(item, count, lanes) for item, count in pieces], axis=1
    )
    dense[...] = gather(spread, chosen)
    for q in range(quants):
        rows = slice(q * ROWS, q * ROWS + modes)
        picked[rows] = picked[rows] + dense[q * modes:(q + 1) * modes]


def add_early(picked, dom, near, chosen, dense, quants, modes, lanes):
    half = near.shape[0] // 2
    add_received(
        picked, dom[...], near[0:half], chosen[0:2 * lanes], dense, quants, modes, lanes
    )


def add_late(picked, dom, far, chosen, dense, quants, modes, lanes):
    spot, count = lax.axis_index("sub"), lax.axis_size("sub")
    met = jnp.where(lax.rem(spot, 2) == 0, spot > 0, spot < count - 1)
    piece = jnp.where(met, far[...], 0.0)
    add_received(
        picked, dom[...], piece, chosen[2 * lanes:4 * lanes], dense, quants, modes, lanes
    )


def lift_weights(lifting):
    basis, depth = lifting.shape
    rest = jnp.zeros((fold_step(basis) - basis, depth), F32)
    high, low = halves(jnp.concatenate([lifting, rest], axis=0))
    return jnp.concatenate([high, low], axis=0)


def lift(weights, high, low, basis):
    step = fold_step(basis)
    both = dot(weights, high)
    return both[0:basis] + both[step:step + basis] + dot(weights[0:step], low)[0:basis]


def local_update(
    base, integral, table, jac, turned_fold, flux, lifting, stiffened, part,
    basis, quants, lanes,
):
    for start in range(0, quants, GROUP):
        values = [integral(q) for q in range(start, start + GROUP)]
        stiffen(turned_fold, values, stiffened, start, lanes)
    weights = lift_weights(lifting)
    for start in range(0, quants, GROUP):
        solved = mix_faces(table, flux, 0, start, quants, lanes)
        high, low = halves(jnp.concatenate(solved, axis=1))
        own = lift(weights, high, low, basis)
        for i in range(GROUP):
            part[start + i] = base(start + i) - own[:, i * lanes:(i + 1) * lanes]

    def take(start, totals):
        for p, total in enumerate(totals, start):
            part[p] = part[p] + total

    mix_jacobians(stiffened, jac, basis, quants, lanes, take)


def near_lift(picked, flux, orient, lifting, quants, lanes, take):
    weights = lift_weights(lifting)
    masks = [
        jnp.concatenate(
            [
                jnp.broadcast_to(jnp.where(orient[f:f + 1] == o, 1.0, 0.0), (ROWS, lanes))
                for f in range(4)
            ],
            axis=0,
        ).astype(BF16)
        for o in range(3)
    ]
    for start in range(0, quants, GROUP):
        highs, lows = [], []
        for solved in mix_faces(picked, flux, 1, start, quants, lanes):
            high, low = halves(solved)
            highs.append(jnp.concatenate([high * mask for mask in masks], axis=0))
            lows.append(jnp.concatenate([low * mask for mask in masks], axis=0))
        near = lift(
            weights, jnp.concatenate(highs, axis=1), jnp.concatenate(lows, axis=1),
            lifting.shape[0],
        )
        for i in range(GROUP):
            take(start + i, near[:, i * lanes:(i + 1) * lanes])


def near_lifting(own_lifting, rotations):
    count, modes, _ = rotations.shape
    block = 4 * ROWS
    row, column = iota((modes, count * block), 0), iota((modes, count * block), 1)
    turned = jnp.zeros((modes, count * block), F32)
    for o in range(count):
        spot = (lax.rem(column, ROWS) == row) & (lax.div(column, block) == o)
        turned = turned + exact_dot(rotations[o], jnp.where(spot, 1.0, 0.0))
    row, column = iota((block, modes), 0), iota((block, modes), 1)
    tall = exact_dot(jnp.where(lax.rem(row, ROWS) == column, 1.0, 0.0), turned)
    row, column = iota(tall.shape, 0), iota(tall.shape, 1)
    same = lax.div(row, ROWS) == lax.div(lax.rem(column, block), ROWS)
    return exact_dot(own_lifting, jnp.where(same, tall, 0.0))


def first_kernel(*refs):
    inputs, refs = refs[:INPUTS], refs[INPUTS:]
    held, refs = refs[:INPUTS], refs[INPUTS:]
    first, second, table, padded, stiff_fold, choice, *sends, stiffened, dense, arrivals = refs
    copies = [
        pltpu.make_async_copy(source, target, arrivals.at[k])
        for k, (source, target) in enumerate(zip(inputs, held))
    ]
    for copy in copies:
        copy.start()
    send_row, projector, stiffness, state, jac = held[:FIRST_USED]
    quants, basis, lanes = state.shape
    modes = projector.shape[0]
    copies[0].wait()
    choice[...] = send_choice(send_row, 4 * lanes, lanes)
    copies[1].wait()
    fill_projector(projector, padded)
    copies[2].wait()
    fold = fold_columns(jnp.concatenate([stiffness[d] for d in range(3)], axis=0))
    stiff_fold[...] = fold.astype(F32)
    copies[3].wait()
    copies[4].wait()
    predict(
        fold, jac, lambda q: state[q], stiffened, first, second, basis, quants, lanes
    )
    project_table(
        padded, lambda q: first[q], table, dense, basis, quants, lanes, modes
    )
    pick_sends(dense, choice[...], sends, lanes)
    for copy in copies[FIRST_USED:]:
        copy.wait()


def second_kernel(
    state, first, table, near, dom, jac, stiffness, padded, rotations, flux, slot,
    part, picked, lifting, turned_fold, choice,
    stiffened, dense,
):
    quants, basis, lanes = state.shape
    modes = rotations.shape[1]
    turned = jnp.concatenate([stiffness[d].T for d in range(3)], axis=0)
    fold = fold_columns(turned)
    turned_fold[...] = fold.astype(F32)
    own_lifting = padded[...].T[0:basis]
    lifting[...] = near_lifting(own_lifting, rotations)
    picked[...] = pick_local(table[...], slot, 4 * lanes)
    choice[...] = received_choice(slot, 4 * lanes, lanes)
    add_early(picked, dom, near, choice, dense, quants, modes, lanes)
    local_update(
        lambda p: state[p], lambda q: first[q], table, jac, fold, flux, own_lifting,
        stiffened, part, basis, quants, lanes,
    )


def third_kernel(
    state, first, second, part, picked_early, far, dom, rotations, jac, stiff_fold, padded, flux, orient, cluster, lifting, received, choice,
    middle, integral, picked, table, *refs,
):
    *sends, stiffened, dense = refs
    quants, basis, lanes = state.shape
    modes = rotations.shape[1]
    picked[...] = picked_early[...]
    add_late(picked, dom, far, received, dense, quants, modes, lanes)
    fine = cluster[...] == 0

    def take(p, near):
        middle[p] = jnp.where(fine, part[p] - near, state[p])

    near_lift(picked, flux, orient, lifting[...], quants, lanes, take)
    predict(
        stiff_fold[...].astype(BF16), jac, lambda q: middle[q], stiffened, integral, None,
        basis, quants, lanes,
    )
    project_table(
        padded, lambda q: jnp.where(fine, integral[q], second[q]), table, dense,
        basis, quants, lanes, modes,
    )
    for q in range(quants):
        integral[q] = jnp.where(fine, integral[q], first[q] + second[q])
    pick_sends(dense, choice[...], sends, lanes)


def fourth_kernel(
    middle, integral, table_one, table_two, picked_one, near, dom, jac, turned_fold, padded,
    rotations, flux, slot, cluster, received,
    part, picked,
    stiffened, dense, total_table,
):
    quants, basis, lanes = middle.shape
    modes = rotations.shape[1]
    own_lifting = padded[...].T[0:basis]
    coarse = jnp.concatenate([cluster[...] != 0] * 4, axis=1)
    total_table[...] = table_two[...] + jnp.where(coarse, table_one[...], 0.0)
    picked[...] = pick_local(table_two[...], slot, 4 * lanes) + jnp.where(
        coarse, picked_one[...], 0.0
    )
    add_early(picked, dom, near, received, dense, quants, modes, lanes)
    local_update(
        lambda p: middle[p], lambda q: integral[q], total_table, jac,
        turned_fold[...].astype(BF16), flux, own_lifting,
        stiffened, part, basis, quants, lanes,
    )


def fifth_kernel(
    part, picked_early, far, dom, rotations, flux, orient, lifting, received, yield_stress,
    updated,
    picked, dense,
):
    quants, basis, lanes = part.shape
    modes = rotations.shape[1]
    picked[...] = picked_early[...]
    add_late(picked, dom, far, received, dense, quants, modes, lanes)
    stepped = [None] * quants

    def take(p, near):
        stepped[p] = part[p] - near

    near_lift(picked, flux, orient, lifting[...], quants, lanes, take)
    mean_part = (stepped[0] + stepped[1] + stepped[2]) / 3.0
    spread = [stepped[q] - mean_part for q in range(3)]
    normal = [item[0:1] for item in spread]
    shear = [stepped[q][0:1] for q in range(3, 6)]
    second_inv = 0.5 * (normal[0] ** 2 + normal[1] ** 2 + normal[2] ** 2) + (
        shear[0] ** 2 + shear[1] ** 2 + shear[2] ** 2
    )
    limit = yield_stress[...]
    scaling = limit / jnp.maximum(jnp.sqrt(second_inv), limit)
    for q in range(3):
        updated[q] = mean_part + scaling * spread[q]
    for q in range(3, 6):
        updated[q] = scaling * stepped[q]
    for q in range(6, quants):
        updated[q] = stepped[q]


def run(body, outs, scratch, *operands, space=pltpu.VMEM):
    vmem = pl.BlockSpec(memory_space=pltpu.VMEM)
    return pl.pallas_call(
        body,
        out_shape=[
            out if isinstance(out, jax.ShapeDtypeStruct) else jax.ShapeDtypeStruct(out, F32)
            for out in outs
        ],
        in_specs=[pl.BlockSpec(memory_space=space)] * len(operands),
        out_specs=[vmem] * len(outs),
        scratch_shapes=scratch,
        compiler_params=pltpu.CompilerParams(vmem_limit_bytes=32 * 1024 * 1024),
        name=body.__name__,
    )(*operands)


def hand_on(near, dom, onward):
    rows = onward.shape[0]
    onward[...] = near[rows:2 * rows]


def exchange(sends):
    def swap(value, axis, first):
        lower = range(first, lax.axis_size(axis) - 1, 2)
        return lax.ppermute(
            value, axis, [(i, i + 1) for i in lower] + [(i + 1, i) for i in lower]
        )

    count = lax.axis_size("sub")
    near = swap(sends[2], "sub", 0)
    dom_even = swap(sends[0], "dom", 0)
    kept, = run(hand_on, [(near.shape[0] // 2, near.shape[1])], [], near, dom_even)
    onward = [(i, (i + (2 if i % 2 == 0 else -2)) % count) for i in range(count)]
    far = lax.ppermute(kept, "sub", onward)
    dom_odd = swap(sends[1], "dom", 1)
    return (near, dom_even), (far, dom_odd)


def on_device(
    modal_state,
    stiffness,
    jacobians,
    flux_solvers,
    projector,
    rotations,
    yield_stress,
    cluster,
    orient,
    neighbour_slot,
    send_map,
):
    basis, quants, lanes = modal_state.shape
    inputs = [
        send_map.reshape(1, -1),
        jnp.transpose(projector, (1, 0, 2)),
        stiffness,
        jnp.transpose(modal_state, (1, 0, 2)),
        jnp.transpose(jacobians, (1, 2, 0, 3)),
        jnp.transpose(flux_solvers, (0, 2, 3, 1, 4)),
        rotations,
        neighbour_slot,
        orient,
        cluster.reshape(1, lanes),
        yield_stress.reshape(1, lanes),
    ]
    inputs = [pltpu.with_memory_space_constraint(item, pltpu.HBM) for item in inputs]
    held = [jax.ShapeDtypeStruct(item.shape, item.dtype) for item in inputs]

    field = (quants, basis, lanes)
    table = (quants * ROWS, 4 * lanes)
    rows = dense_rows(quants, projector.shape[1])
    dense = pltpu.VMEM((rows, 4 * lanes), F32)
    messages = [(rows // 2, lanes)] * 3
    choice = jax.ShapeDtypeStruct((4 * lanes, 4 * lanes), BF16)
    flat = quants * lanes
    fold = (3 * basis, 3 * fold_step(basis))
    stiffened = pltpu.VMEM((3 * basis, flat), F32)
    two_stiffened = pltpu.VMEM((2, 3 * basis, flat), F32)

    outs = run(
        first_kernel,
        held + [field, field, table, (4 * ROWS, 128), fold, choice] + messages,
        [two_stiffened, dense, pltpu.SemaphoreType.DMA((INPUTS,))],
        *inputs, space=pl.ANY,
    )
    _, _, stiff, state, jac, flux, turns, slot, orient, cluster, limit = outs[:INPUTS]
    first, second, table_one, padded, stiff_fold, sending, *sends = outs[INPUTS:]
    early, late = exchange(sends)
    part_one, local_one, lifting, turned_fold, received = run(
        second_kernel, [field, table, (basis, 3 * 4 * ROWS), fold, choice], [stiffened, dense],
        state, first, table_one, *early, jac, stiff, padded, turns, flux, slot,
    )
    middle, integral, picked_one, table_two, *sends = run(
        third_kernel, [field, field, table, table] + messages, [two_stiffened, dense],
        state, first, second, part_one, local_one, *late, turns,
        jac, stiff_fold, padded, flux, orient, cluster, lifting, received, sending,
    )
    early, late = exchange(sends)
    part_two, local_two = run(
        fourth_kernel, [field, table], [stiffened, dense, pltpu.VMEM(table, F32)],
        middle, integral, table_one, table_two, picked_one, *early, jac, turned_fold, padded,
        turns, flux, slot, cluster, received,
    )
    updated, = run(
        fifth_kernel, [field], [pltpu.VMEM(table, F32), dense],
        part_two, local_two, *late, turns, flux, orient, lifting, received, limit,
    )
    return jnp.transpose(updated, (1, 0, 2))


def solution(mesh):
    placed = (
        P(None, None, ("dom", "sub")),
        P(),
        P(None, None, None, ("dom", "sub")),
        P(None, None, None, None, ("dom", "sub")),
        P(),
        P(),
        P(("dom", "sub")),
        P(("dom", "sub")),
        P(None, ("dom", "sub")),
        P(None, ("dom", "sub")),
        P(("dom", "sub")),
    )
    return jax.shard_map(
        on_device,
        mesh=mesh,
        in_specs=placed,
        out_specs=P(None, None, ("dom", "sub")),
        check_vma=False,
    )
```
